32 devices in a mesh: ctx: 4 (over y, x), seq: 8 (over z, core).
Axes of the slice: x: 2, y: 2, z: 4, core: 2. Of those that a mesh axis runs over, the one named last changes fastest.
Arguments:
- block_input: bfloat16 [16, 1024, 1024], P('ctx', 'seq'), may hold values from -6 to 6
- valid_len: int32 [16], P('ctx'), may hold values from 128 to 1024, as said below
- out_grad: bfloat16 [16, 1024, 1024], P('ctx', 'seq'), may hold values from -6 to 6
- first_gain: float32 [1024], replicated, may hold values from 0.5 to 1.5
- first_shift: float32 [1024], replicated, may hold values from -1.5 to 1.5
- log_step: float32 [1024], replicated, may hold values from -6.9 to -2.3
- decay_log: float32 [1024, 64], replicated, may hold values from -3 to 0
- turn_rate: float32 [1024, 64], replicated, may hold values from 0 to 3
- read_real: float32 [1024, 64], replicated, may hold values from -1.8 to 1.8
- read_imag: float32 [1024, 64], replicated, may hold values from -1.8 to 1.8
- skip_gain: float32 [1024], replicated, may hold values from -4 to 4
- glu_weight: bfloat16 [1024, 2048], replicated, may hold values from -0.1875 to 0.1875
- glu_bias: float32 [2048], replicated, may hold values from -1.5 to 1.5
- second_gain: float32 [1024], replicated, may hold values from 0.5 to 1.5
- second_shift: float32 [1024], replicated, may hold values from -1.5 to 1.5
- up_weight: bfloat16 [1024, 4096], replicated, may hold values from -0.1875 to 0.1875
- up_bias: float32 [4096], replicated, may hold values from -1.5 to 1.5
- down_weight: bfloat16 [4096, 1024], replicated, may hold values from -0.09375 to 0.09375
- down_bias: float32 [1024], replicated, may hold values from -1.5 to 1.5
Outputs:
- block_output: bfloat16 [16, 1024, 1024], P('ctx', 'seq')
- input_grad: bfloat16 [16, 1024, 1024], P('ctx', 'seq')
- first_gain_grad: float32 [1024], replicated
- first_shift_grad: float32 [1024], replicated
- log_step_grad: float32 [1024], replicated
- decay_log_grad: float32 [1024, 64], replicated
- turn_rate_grad: float32 [1024, 64], replicated
- read_real_grad: float32 [1024, 64], replicated
- read_imag_grad: float32 [1024, 64], replicated
- skip_gain_grad: float32 [1024], replicated
- glu_weight_grad: float32 [1024, 2048], P('seq')
- glu_bias_grad: float32 [2048], replicated
- second_gain_grad: float32 [1024], replicated
- second_shift_grad: float32 [1024], replicated
- up_weight_grad: float32 [1024, 4096], P('seq')
- up_bias_grad: float32 [4096], replicated
- down_weight_grad: float32 [4096, 1024], P('seq')
- down_bias_grad: float32 [1024], replicated
The draws below stay inside these ranges and needn't reach their ends.
Inputs may be any that keep to these rules, and one draw needn't show every extreme that they name: `valid_len`: among the 4 contexts of each index of ctx one has more than 896 valid positions; in some index of ctx that context is valid in all 1024 positions. The others have at least 128.
All inputs are finite; a program needn't handle non-finite values.
Results may differ from the reference program's by a relative error of at most 0.0067.
Values sent between devices are 32-bit elements; how exact they have to be, the bound alone decides.
No kernel may reach another device: no remote copies, remote signals or barrier semaphores. Data moves between devices by JAX's collectives and lax.ppermute only.
A program may use at most 256 MiB of HBM per device.

```python
import math
import jax
import jax.numpy as jnp
from jax import lax

D = 1024
NSTATE = 64
FF = 4096
TOK_SEQ = 128
CPG = 4
LEN = 1024
CTXS = 16


def draw_valid_len(key, part):
    key = jax.random.fold_in(key, 11)
    key_lengths, key_choice, key_tail, key_group = jax.random.split(key, 4)
    groups = CTXS // CPG
    lengths = jax.random.randint(key_lengths, (CTXS,), LEN // 8, LEN + 1)
    chosen = jax.random.randint(key_choice, (groups,), 0, CPG)
    tails = LEN - jax.random.randint(key_tail, (groups,), 0, TOK_SEQ)
    full_group = jax.random.randint(key_group, (), 0, groups)
    tails = jnp.where(jnp.arange(groups) == full_group, LEN, tails)
    context_ids = jnp.arange(CTXS)
    group_ids = context_ids // CPG
    is_long = context_ids % CPG == chosen[group_ids]
    return jnp.where(is_long, tails[group_ids], lengths).astype(jnp.int32)


def level_of(own_key, shape, cuts, low, top_value):
    factor_of = 1.0
    for dim, parts in cuts:
        draws = jax.random.uniform(jax.random.fold_in(jax.random.fold_in(own_key, 6), dim), (parts,), jnp.float32, low / len(cuts), top_value / len(cuts))
        factor_of = factor_of * jnp.repeat(jnp.exp(draws), shape[dim] // parts).reshape((-1,) + (1,) * (len(shape) - 1 - dim))
    return factor_of


def noise(rng, dims, spread, reach, cuts=(), held_as=jnp.bfloat16):
    array = jax.random.normal(rng, dims, jnp.float32) * spread
    if len(cuts) > 0:
        array = level_of(rng, dims, cuts, -0.22, 0.18) * array
    return jnp.clip(array, min=-reach, max=reach).astype(held_as)


def setup_inputs(seed: int = 0) -> dict:
    splits = jax.random.split(jax.random.key(seed), 20)
    return {
        "block_input": noise(splits[0], (CTXS, LEN, D), 1.0, 6.0, ((0, 4), (1, 8))),
        "valid_len": draw_valid_len(jax.random.fold_in(splits[19], 71), 0),
        "out_grad": noise(splits[2], (CTXS, LEN, D), 1.0, 6.0, ((0, 4), (1, 8))),
        "first_gain": jnp.clip(1.0 + 0.1 * jax.random.normal(splits[3], (D,), jnp.float32), 0.5, 1.5),
        "first_shift": noise(splits[4], (D,), 0.3, 1.5, (), jnp.float32),
        "log_step": jnp.clip(jax.random.uniform(splits[5], (D,), jnp.float32, -6.9, -2.3), -6.9, -2.3),
        "decay_log": jnp.clip(jax.random.uniform(splits[6], (D, NSTATE), jnp.float32, -3.0, 0.0), -3.0, 0.0),
        "turn_rate": jnp.clip(jax.random.uniform(splits[7], (D, NSTATE), jnp.float32, 0.0, 3.0), 0.0, 3.0),
        "read_real": noise(splits[8], (D, NSTATE), 0.3, 1.8, (), jnp.float32),
        "read_imag": noise(splits[9], (D, NSTATE), 0.3, 1.8, (), jnp.float32),
        "skip_gain": noise(splits[10], (D,), 1.0, 4.0, (), jnp.float32),
        "glu_weight": noise(splits[11], (D, 2 * D), D ** -0.5, 0.1875),
        "glu_bias": noise(splits[12], (2 * D,), 0.3, 1.5, (), jnp.float32),
        "second_gain": jnp.clip(1.0 + 0.1 * jax.random.normal(splits[13], (D,), jnp.float32), 0.5, 1.5),
        "second_shift": noise(splits[14], (D,), 0.3, 1.5, (), jnp.float32),
        "up_weight": noise(splits[15], (D, FF), D ** -0.5, 0.1875),
        "up_bias": noise(splits[16], (FF,), 0.3, 1.5, (), jnp.float32),
        "down_weight": noise(splits[17], (FF, D), FF ** -0.5, 0.09375),
        "down_bias": noise(splits[18], (D,), 0.3, 1.5, (), jnp.float32),
    }


@jax.custom_vjp
def low(v):
    return lax.optimization_barrier(v.astype(jnp.bfloat16)).astype(jnp.float32)

@jax.custom_vjp
def low_back(v):
    return v

def low_keep(v):
    return (low(v), None)

def low_pass(kept, grad):
    return (grad,)

def back_keep(v):
    return (v, None)

def back_low(kept, grad):
    return (low(grad),)
low.defvjp(low_keep, low_pass)
low_back.defvjp(back_keep, back_low)
EPSILON = 1e-05
PRECISE = lax.Precision.HIGHEST

def layer_norm(values_in, gain_vec, shift_vec):
    centre = values_in - lax.optimization_barrier(jnp.mean(values_in, axis=-1, keepdims=True))
    variance = lax.optimization_barrier(jnp.mean(centre * centre, axis=-1, keepdims=True))
    return centre * lax.rsqrt(variance + EPSILON) * gain_vec + shift_vec

def kernel_piece(ssm_params, place_block):
    log_step, decay_log, turn_rate, read_real, read_imag = ssm_params
    step_size = jnp.exp(log_step)[:, None]
    decay_rate = jnp.exp(decay_log)
    rate_step = -decay_rate * step_size
    turn_step = turn_rate * step_size
    growth = jnp.exp(rate_step)
    edge_real = growth * jnp.cos(turn_step) - 1.0
    edge_imag = growth * jnp.sin(turn_step)
    modulus = decay_rate * decay_rate + turn_rate * turn_rate
    ratio_real = (-edge_real * decay_rate + edge_imag * turn_rate) / modulus
    ratio_imag = (-edge_imag * decay_rate - edge_real * turn_rate) / modulus
    coef_real = read_real * ratio_real - read_imag * ratio_imag
    coef_imag = read_real * ratio_imag + read_imag * ratio_real
    magnitude = jnp.exp(rate_step[:, :, None] * place_block[None, None, :])
    angles = turn_step[:, :, None] * place_block[None, None, :]
    terms = magnitude * (coef_real[:, :, None] * jnp.cos(angles) - coef_imag[:, :, None] * jnp.sin(angles))
    return 2.0 * lax.optimization_barrier(jnp.sum(terms, axis=1)).T

def full_kernel(ssm_params):
    channels = ssm_params[0].shape[0]
    seq_len = LEN
    group_size = min(channels, 32)
    group_count = channels // group_size
    positions = jnp.arange(seq_len).astype(jnp.float32)
    grouped = jax.tree.map(lambda tensor: tensor.reshape((group_count, group_size) + tensor.shape[1:]), ssm_params)
    blocks = lax.map(jax.checkpoint(lambda piece_params: kernel_piece(piece_params, positions)), grouped)
    return blocks.transpose(1, 0, 2).reshape(seq_len, channels)

def causal_conv(signal, kernel_full):
    seq_len = signal.shape[1]
    spec_signal = jnp.fft.rfft(signal, n=2 * seq_len, axis=1)
    spec_kernel = jnp.fft.rfft(kernel_full, n=2 * seq_len, axis=0)
    return jnp.fft.irfft(spec_signal * spec_kernel[None], n=2 * seq_len, axis=1)[:, :seq_len]

def forward(inputs, valid_mask, params):
    first_gain, first_shift, log_step, decay_log, turn_rate, read_real, read_imag, skip_gain, glu_weight, glu_bias, second_gain, second_shift, up_weight, up_bias, down_weight, down_bias = params
    signal = layer_norm(inputs, first_gain, first_shift) * valid_mask
    kernel_full = full_kernel((log_step, decay_log, turn_rate, read_real, read_imag))
    mixed_seq = causal_conv(signal, kernel_full) + skip_gain * signal
    activated = low(jax.nn.gelu(mixed_seq, approximate=True))
    gate_rows = low_back(jnp.einsum('cld,de->cle', activated, glu_weight, precision=PRECISE) + glu_bias)
    channels = inputs.shape[-1]
    hidden = inputs + gate_rows[..., :channels] * jax.nn.sigmoid(gate_rows[..., channels:])
    second = low(layer_norm(hidden, second_gain, second_shift))
    inner_rows = low_back(jnp.einsum('cld,df->clf', second, up_weight, precision=PRECISE) + up_bias)
    widened = low(jax.nn.gelu(inner_rows, approximate=True))
    result = hidden + jnp.einsum('clf,fd->cld', widened, down_weight, precision=PRECISE) + down_bias
    return result * valid_mask

def reference(block_input, valid_len, out_grad, first_gain, first_shift, log_step, decay_log, turn_rate, read_real, read_imag, skip_gain, glu_weight, glu_bias, second_gain, second_shift, up_weight, up_bias, down_weight, down_bias):
    params = jax.tree.map(lambda tensor: tensor.astype(jnp.float32), (first_gain, first_shift, log_step, decay_log, turn_rate, read_real, read_imag, skip_gain, glu_weight, glu_bias, second_gain, second_shift, up_weight, up_bias, down_weight, down_bias))
    contexts = block_input.shape[0]
    seq_len = block_input.shape[1]
    channels = block_input.shape[2]
    per_step = math.gcd(contexts, max(1, 4096 // seq_len))
    step_count = contexts // per_step
    positions = jnp.arange(seq_len)
    valid_mask = (positions[None, :] < valid_len[:, None]).astype(jnp.float32)[..., None]
    inputs = block_input.astype(jnp.float32).reshape(step_count, per_step, seq_len, channels)
    mask_groups = valid_mask.reshape(step_count, per_step, seq_len, 1)
    grads_in = out_grad.astype(jnp.float32).reshape(step_count, per_step, seq_len, channels)

    def accumulate(running, pieces):
        group_in, group_mask, group_grad = pieces
        result, pullback = jax.vjp(lambda values_in, weights: forward(values_in, group_mask, weights), group_in, params)
        grad_values, grad_params = pullback(group_grad)
        return (jax.tree.map(jnp.add, running, grad_params), (result.astype(jnp.bfloat16), grad_values.astype(jnp.bfloat16)))
    initial = jax.tree.map(jnp.zeros_like, params)
    totals, (outputs, input_grads) = lax.scan(accumulate, initial, (inputs, mask_groups, grads_in))
    return (outputs.reshape(contexts, seq_len, channels), input_grads.reshape(contexts, seq_len, channels), totals[0], totals[1], totals[2], totals[3], totals[4], totals[5], totals[6], totals[7], totals[8], totals[9], totals[10], totals[11], totals[12], totals[13], totals[14], totals[15])
```

```python
import functools
import math

import jax
import jax.numpy as jnp
import numpy as np
from jax import lax
from jax.experimental import pallas as pl
from jax.experimental.pallas import tpu as pltpu
from jax.sharding import PartitionSpec as P

EPSILON = 1e-05
PRECISE = lax.Precision.HIGHEST


def gelu_tanh(values_in):
    return jax.nn.gelu(values_in, approximate=True)


def layer_norm(values_in, gain_vec, shift_vec):
    centre = values_in - jnp.mean(values_in, axis=-1, keepdims=True)
    scale_rows = lax.rsqrt(jnp.mean(centre * centre, axis=-1, keepdims=True) + EPSILON)
    unit_rows = centre * scale_rows
    return (unit_rows * gain_vec + shift_vec, unit_rows, scale_rows)


def norm_back(grad_rows, unit_rows, scale_rows, gain_vec):
    scaled = grad_rows * gain_vec
    return scale_rows * (
        scaled
        - jnp.mean(scaled, axis=-1, keepdims=True)
        - unit_rows * jnp.mean(scaled * unit_rows, axis=-1, keepdims=True)
    )


def kernel_piece(ssm_params, place_block):
    log_step, decay_log, turn_rate, read_real, read_imag = ssm_params
    step_size = jnp.exp(log_step)[:, None]
    decay_rate = jnp.exp(decay_log)
    rate_step = -decay_rate * step_size
    turn_step = turn_rate * step_size
    growth = jnp.exp(rate_step)
    edge_real = growth * jnp.cos(turn_step) - 1.0
    edge_imag = growth * jnp.sin(turn_step)
    modulus = decay_rate * decay_rate + turn_rate * turn_rate
    ratio_real = (-edge_real * decay_rate + edge_imag * turn_rate) / modulus
    ratio_imag = (-edge_imag * decay_rate - edge_real * turn_rate) / modulus
    coef_real = read_real * ratio_real - read_imag * ratio_imag
    coef_imag = read_real * ratio_imag + read_imag * ratio_real
    magnitude = jnp.exp(rate_step[:, :, None] * place_block[None, None, :])
    angles = turn_step[:, :, None] * place_block[None, None, :]
    terms = magnitude * (
        coef_real[:, :, None] * jnp.cos(angles) - coef_imag[:, :, None] * jnp.sin(angles)
    )
    return 2.0 * jnp.sum(terms, axis=1).T


def kernel_layout(ssm_params, positions):
    channels = ssm_params[0].shape[0]
    group_size = min(channels, 128)
    span_size = min(positions.shape[0], 128)
    group_count = channels // group_size
    grouped = jax.tree.map(
        lambda tensor: tensor.reshape((group_count, group_size) + tensor.shape[1:]), ssm_params
    )
    span_rows = positions.reshape(-1, span_size)
    return (channels, group_size, span_size, group_count, grouped, span_rows)


def kernel_block(ssm_params, positions):
    channels, group_size, span_size, group_count, grouped, span_rows = kernel_layout(
        ssm_params, positions
    )

    def per_group(piece_params):
        return lax.map(lambda place_block: kernel_piece(piece_params, place_block), span_rows)

    blocks = lax.map(per_group, grouped)
    return blocks.transpose(1, 2, 0, 3).reshape(positions.shape[0], channels)


def kernel_grads(ssm_params, positions, upstream):
    channels, group_size, span_size, group_count, grouped, span_rows = kernel_layout(
        ssm_params, positions
    )
    upstream_groups = upstream.reshape(
        span_rows.shape[0], span_size, group_count, group_size
    ).transpose(2, 0, 1, 3)

    def per_group(pairing):
        piece_params, piece_grad = pairing

        def accumulate(running, inputs_block):
            place_block, grad_block = inputs_block
            _, pullback = jax.vjp(
                lambda inner_params: kernel_piece(inner_params, place_block), piece_params
            )
            return (jax.tree.map(jnp.add, running, pullback(grad_block)[0]), None)

        initial = jax.tree.map(jnp.zeros_like, piece_params)
        totals, _ = lax.scan(accumulate, initial, (span_rows, piece_grad))
        return totals

    summed = lax.map(per_group, (grouped, upstream_groups))
    return jax.tree.map(lambda tensor: tensor.reshape((channels,) + tensor.shape[2:]), summed)


def phase_table(first_index, second_index, modulus):
    products_mod = first_index[:, None] * second_index[None, :] % modulus
    angles = products_mod.astype(jnp.float32) * (2.0 * math.pi / modulus)
    return (jnp.cos(angles), jnp.sin(angles))


def first_section(series, row_index, freq_index, modulus):
    cosine, sine_part = phase_table(row_index, freq_index, modulus)
    real_part = jnp.einsum("bnjh,nk->bkjh", series, cosine, precision=PRECISE)
    imag_part = -jnp.einsum("bnjh,nk->bkjh", series, sine_part, precision=PRECISE)
    return (real_part, imag_part)


def rotate(real_part, imag_part, row_index, col_index, modulus, direction):
    cosine, sine_part = phase_table(row_index, col_index, modulus)
    cosine = cosine[None, :, :, None]
    sine_part = direction * sine_part[None, :, :, None]
    return (real_part * cosine - imag_part * sine_part, real_part * sine_part + imag_part * cosine)


def mix_columns(real_part, imag_part, col_index, out_index, modulus, direction):
    cosine, sine_part = phase_table(col_index, out_index, modulus)
    sine_part = direction * sine_part

    def contract(operand, matrix):
        return jnp.einsum("bkjh,jm->bkmh", operand, matrix, precision=PRECISE)

    return (
        contract(real_part, cosine) - contract(imag_part, sine_part),
        contract(real_part, sine_part) + contract(imag_part, cosine),
    )


def last_section(real_part, imag_part, freq_index, row_index, modulus, length_all):
    cosine, sine_part = phase_table(freq_index, row_index, modulus)
    summed = jnp.einsum("bkjh,kn->bnjh", real_part, cosine, precision=PRECISE) - jnp.einsum(
        "bkjh,kn->bnjh", imag_part, sine_part, precision=PRECISE
    )
    return summed / length_all


def local_spectrum(series):
    seq_parts = series.shape[1]
    block_len = series.shape[2]
    freq_count = 2 * seq_parts
    modulus = freq_count * block_len
    freq_index = jnp.arange(freq_count)
    col_index = jnp.arange(block_len)
    real_part, imag_part = first_section(series, jnp.arange(seq_parts), freq_index, freq_count)
    real_part, imag_part = rotate(real_part, imag_part, freq_index, col_index, modulus, -1.0)
    return mix_columns(real_part, imag_part, col_index, col_index, block_len, -1.0)


def local_time(real_part, imag_part):
    freq_count = real_part.shape[1]
    block_len = real_part.shape[2]
    seq_parts = freq_count // 2
    modulus = freq_count * block_len
    freq_index = jnp.arange(freq_count)
    col_index = jnp.arange(block_len)
    real_part, imag_part = mix_columns(real_part, imag_part, col_index, col_index, block_len, 1.0)
    real_part, imag_part = rotate(real_part, imag_part, freq_index, col_index, modulus, 1.0)
    return last_section(
        real_part, imag_part, freq_index, jnp.arange(seq_parts), freq_count, modulus
    )


def channel_spectrum(series):
    seq_parts = lax.axis_size("seq")
    spread = lax.all_to_all(series, "seq", split_axis=2, concat_axis=1, tiled=True)
    batch_size, total_len, chan_count = spread.shape
    return local_spectrum(spread.reshape(batch_size, seq_parts, total_len // seq_parts, chan_count))


def token_blocks(series):
    batch_size, seq_parts, block_len, chan_count = series.shape
    flat_series = series.reshape(batch_size, seq_parts * block_len, chan_count)
    return lax.all_to_all(flat_series, "seq", split_axis=1, concat_axis=2, tiled=True)


def times_kernel(sig_real, sig_imag, ker_real, ker_imag):
    return (sig_real * ker_real - sig_imag * ker_imag, sig_real * ker_imag + sig_imag * ker_real)


def conj_products(sig_real, sig_imag, ker_real, ker_imag, grad_real, grad_imag):
    back_real = ker_real * grad_real + ker_imag * grad_imag
    back_imag = ker_real * grad_imag - ker_imag * grad_real
    kern_real = jnp.sum(sig_real * grad_real + sig_imag * grad_imag, axis=0, keepdims=True)
    kern_imag = jnp.sum(sig_real * grad_imag - sig_imag * grad_real, axis=0, keepdims=True)
    return (
        jnp.concatenate([back_real, kern_real], axis=0),
        jnp.concatenate([back_imag, kern_imag], axis=0),
    )


F32 = jnp.float32
BF16 = jnp.bfloat16
BLOCK = 128
STEP_LOW = 32
AXES = ("ctx", "seq")
VMEM_BYTES = 60 * 1024 * 1024


def params_of(*semantics, vmem=VMEM_BYTES):
    return pltpu.CompilerParams(dimension_semantics=semantics, vmem_limit_bytes=vmem)


def cost_of(flops, nbytes):
    return pl.CostEstimate(flops=int(flops), bytes_accessed=int(nbytes), transcendentals=0)


def split_high_low(table):
    high = table.astype(BF16)
    return high, (table - high.astype(F32)).astype(BF16)


def odd_tables():
    points = np.arange(BLOCK)
    turns = np.pi * np.outer(2 * points + 1, points) / (2 * BLOCK)
    ahead = np.concatenate([np.cos(turns), -np.sin(turns)], axis=0)
    back = ahead.T / BLOCK

    def halves(table):
        table = table.astype(np.float32)
        high = table.astype(BF16)
        return high, (table - high.astype(np.float32)).astype(BF16)

    return halves(ahead) + halves(back)


def dot_parts(high, low, operand):
    op_high = operand.astype(BF16)
    op_low = (operand - op_high.astype(F32)).astype(BF16)

    def one(left, right):
        return jnp.dot(left, right, preferred_element_type=F32)

    return one(high, op_high) + (one(high, op_low) + one(low, op_high))


def norm_rows(rows):
    centre = rows - jnp.mean(rows, axis=-1, keepdims=True)
    scale = lax.rsqrt(jnp.mean(centre * centre, axis=-1, keepdims=True) + EPSILON)
    return centre * scale, scale


def mask_column(meta_ref, context, contexts):
    places = lax.broadcasted_iota(jnp.int32, (BLOCK, 1), 0) + meta_ref[contexts] * BLOCK
    return (places < meta_ref[context]).astype(F32)


def signal_kernel(base, contexts, meta_ref, x_ref, gain_ref, shift_ref, out_ref):
    unit, _ = norm_rows(x_ref[0].astype(F32))
    mask = mask_column(meta_ref, pl.program_id(0) + base, contexts)
    signal = (unit * gain_ref[...] + shift_ref[...]) * mask
    for part in range(out_ref.shape[0]):
        out_ref[part, 0] = signal[:, part * BLOCK : (part + 1) * BLOCK]


def make_signal(meta, block_input, gain, shift, base, count):
    contexts, block_len, channels = block_input.shape
    parts = channels // BLOCK
    return pl.pallas_call(
        functools.partial(signal_kernel, base, contexts),
        grid_spec=pltpu.PrefetchScalarGridSpec(
            num_scalar_prefetch=1,
            grid=(count,),
            in_specs=[
                pl.BlockSpec((1, block_len, channels), lambda i, m: (base + i, 0, 0)),
                pl.BlockSpec((1, channels), lambda i, m: (0, 0)),
                pl.BlockSpec((1, channels), lambda i, m: (0, 0)),
            ],
            out_specs=pl.BlockSpec((parts, 1, block_len, BLOCK), lambda i, m: (0, i, 0, 0)),
        ),
        out_shape=jax.ShapeDtypeStruct((parts, count, block_len, BLOCK), F32),
        compiler_params=params_of("arbitrary"),
        cost_estimate=cost_of(0, count * block_len * channels * 6),
        name="signal",
    )(meta, block_input, gain, shift)


def mode_coefs(log_step, decay_log, turn_rate, read_real, read_imag):
    step_size = jnp.exp(log_step)[None, :]
    decay_rate = jnp.exp(decay_log)
    rate_step = -decay_rate * step_size
    turn_step = turn_rate * step_size
    growth = jnp.exp(rate_step)
    edge_real = growth * jnp.cos(turn_step) - 1.0
    edge_imag = growth * jnp.sin(turn_step)
    modulus = decay_rate * decay_rate + turn_rate * turn_rate
    ratio_real = (-edge_real * decay_rate + edge_imag * turn_rate) / modulus
    ratio_imag = (-edge_imag * decay_rate - edge_real * turn_rate) / modulus
    coef_real = read_real * ratio_real - read_imag * ratio_imag
    coef_imag = read_real * ratio_imag + read_imag * ratio_real
    return rate_step, turn_step, coef_real, coef_imag


def low_table(rate_ref, turn_ref, low_real, low_imag):
    places = lax.broadcasted_iota(jnp.int32, (STEP_LOW, 1), 0).astype(F32)

    def fill(mode, _):
        rate = rate_ref[pl.ds(mode, 1), :]
        turn = turn_ref[pl.ds(mode, 1), :]
        size = jnp.exp(rate * places)
        angle = turn * places
        low_real[mode] = size * jnp.cos(angle)
        low_imag[mode] = size * jnp.sin(angle)
        return 0

    lax.fori_loop(0, rate_ref.shape[0], fill, 0)


def high_table(rate_ref, turn_ref, start_real, start_imag, high_real, high_imag):
    size = jnp.exp(rate_ref[...] * STEP_LOW)
    angle = turn_ref[...] * STEP_LOW
    move_real = size * jnp.cos(angle)
    move_imag = size * jnp.sin(angle)

    def fill(place, carry):
        now_real, now_imag = carry
        high_real[place] = now_real
        high_imag[place] = now_imag
        return (
            now_real * move_real - now_imag * move_imag,
            now_real * move_imag + now_imag * move_real,
        )

    lax.fori_loop(0, high_real.shape[0], fill, (start_real, start_imag))


def alternate_sign(rows):
    place = lax.broadcasted_iota(jnp.int32, (rows, 1), 0)
    return (1 - 2 * (place & 1)).astype(F32)


def spectrum_kernel(
    rate_ref,
    turn_ref,
    coef_real_ref,
    coef_imag_ref,
    ahead_high,
    ahead_low,
    out_ref,
    low_real,
    low_imag,
    high_real,
    high_imag,
    taps,
):
    modes = rate_ref.shape[0]
    parts = out_ref.shape[0]
    low_table(rate_ref, turn_ref, low_real, low_imag)
    high_table(
        rate_ref, turn_ref, coef_real_ref[...], coef_imag_ref[...], high_real, high_imag
    )
    tile = 8

    def per_tile(index, _):
        first = index * tile

        def per_mode(mode, sums):
            base_real = low_real[mode]
            base_imag = low_imag[mode]
            row = pl.ds(mode, 1)
            return tuple(
                sums[k]
                + (
                    high_real[first + k, row, :] * base_real
                    - high_imag[first + k, row, :] * base_imag
                )
                for k in range(tile)
            )

        zeros = jnp.zeros((STEP_LOW, BLOCK), F32)
        sums = lax.fori_loop(0, modes, per_mode, (zeros,) * tile)
        for k in range(tile):
            taps[pl.ds(pl.multiple_of((first + k) * STEP_LOW, STEP_LOW), STEP_LOW), :] = (
                2.0 * sums[k]
            )
        return 0

    lax.fori_loop(0, high_real.shape[0] // tile, per_tile, 0)
    wide = jnp.concatenate([taps[d * BLOCK : (d + 1) * BLOCK, :] for d in range(parts)], axis=1)
    plain = dot_parts(ahead_high[...], ahead_low[...], wide)
    sign = alternate_sign(BLOCK)
    for d in range(parts):
        here = plain[:, d * BLOCK : (d + 1) * BLOCK]
        real_part, imag_part = here[:BLOCK], here[BLOCK:]
        if d > 0:
            before = plain[:, (d - 1) * BLOCK : d * BLOCK]
            real_part = real_part - sign * before[BLOCK:]
            imag_part = imag_part + sign * before[:BLOCK]
        out_ref[d, :BLOCK, :] = real_part
        out_ref[d, BLOCK:, :] = imag_part


def whole(shape):
    return pl.BlockSpec(shape, lambda *_: (0,) * len(shape))


def make_spectrum(coefs, tables, parts):
    modes = coefs[0].shape[0]
    high_count = parts * BLOCK // STEP_LOW
    return pl.pallas_call(
        spectrum_kernel,
        grid=(1,),
        in_specs=[whole((modes, BLOCK))] * 4 + [whole((2 * BLOCK, BLOCK))] * 2,
        out_specs=whole((parts, 2 * BLOCK, BLOCK)),
        out_shape=jax.ShapeDtypeStruct((parts, 2 * BLOCK, BLOCK), F32),
        scratch_shapes=[
            pltpu.VMEM((modes, STEP_LOW, BLOCK), F32),
            pltpu.VMEM((modes, STEP_LOW, BLOCK), F32),
            pltpu.VMEM((high_count, modes, BLOCK), F32),
            pltpu.VMEM((high_count, modes, BLOCK), F32),
            pltpu.VMEM((parts * BLOCK, BLOCK), F32),
        ],
        compiler_params=params_of("arbitrary"),
        cost_estimate=cost_of(2e9, 2e6),
        name="taps_spectrum",
    )(*coefs, tables[0], tables[1])


def gather_lanes(ref, parts):
    return jnp.concatenate([ref[t, 0] for t in range(parts)], axis=1)


def conv_kernel(
    parts, u_ref, taps_ref, ahead_high, ahead_low, back_high, back_low, y_ref, spec_ref, mixed
):
    spec_ref[0] = dot_parts(ahead_high[...], ahead_low[...], gather_lanes(u_ref, parts))

    def per_tile(index, _):
        real_rows = pl.ds(pl.multiple_of(index * 8, 8), 8)
        imag_rows = pl.ds(pl.multiple_of(BLOCK + index * 8, 8), 8)

        def lanes(t):
            return pl.ds(t * BLOCK, BLOCK)

        k_real = [taps_ref[d, real_rows, :] for d in range(parts)]
        k_imag = [taps_ref[d, imag_rows, :] for d in range(parts)]
        u_real = [spec_ref[0, real_rows, lanes(t)] for t in range(parts)]
        u_imag = [spec_ref[0, imag_rows, lanes(t)] for t in range(parts)]
        for s in range(parts):
            sum_real = jnp.zeros((8, BLOCK), F32)
            sum_imag = jnp.zeros((8, BLOCK), F32)
            for t in range(s + 1):
                d = s - t
                sum_real += k_real[d] * u_real[t] - k_imag[d] * u_imag[t]
                sum_imag += k_real[d] * u_imag[t] + k_imag[d] * u_real[t]
            mixed[real_rows, lanes(s)] = sum_real
            mixed[imag_rows, lanes(s)] = sum_imag
        return 0

    lax.fori_loop(0, BLOCK // 8, per_tile, 0)
    result = dot_parts(back_high[...], back_low[...], mixed[...])
    for s in range(parts):
        y_ref[s, 0] = result[:, s * BLOCK : (s + 1) * BLOCK]


def convolve(series, taps, tables):
    parts, count = series.shape[:2]
    wide = parts * BLOCK
    return pl.pallas_call(
        functools.partial(conv_kernel, parts),
        grid=(count,),
        in_specs=[
            pl.BlockSpec((parts, 1, BLOCK, BLOCK), lambda i: (0, i, 0, 0)),
            whole((parts, 2 * BLOCK, BLOCK)),
            whole((2 * BLOCK, BLOCK)),
            whole((2 * BLOCK, BLOCK)),
            whole((BLOCK, 2 * BLOCK)),
            whole((BLOCK, 2 * BLOCK)),
        ],
        out_specs=[
            pl.BlockSpec((parts, 1, BLOCK, BLOCK), lambda i: (0, i, 0, 0)),
            pl.BlockSpec((1, 2 * BLOCK, wide), lambda i: (i, 0, 0)),
        ],
        out_shape=[
            jax.ShapeDtypeStruct((parts, count, BLOCK, BLOCK), F32),
            jax.ShapeDtypeStruct((count, 2 * BLOCK, wide), F32),
        ],
        scratch_shapes=[pltpu.VMEM((2 * BLOCK, wide), F32)],
        compiler_params=params_of("arbitrary"),
        cost_estimate=cost_of(count * 6e8, count * 2.5e6),
        name="convolve",
    )(series, taps, *tables)


def conv_back_kernel(
    parts,
    count,
    g_ref,
    spec_ref,
    taps_ref,
    ahead_high,
    ahead_low,
    back_high,
    back_low,
    y_ref,
    taps_grad_ref,
    grad_spec,
    mixed,
    pairs,
):
    step = pl.program_id(0)

    @pl.when(step == 0)
    def _():
        pairs[...] = jnp.zeros_like(pairs)

    grad_spec[...] = dot_parts(ahead_high[...], ahead_low[...], gather_lanes(g_ref, parts))

    def per_tile(index, _):
        real_rows = pl.ds(pl.multiple_of(index * 8, 8), 8)
        imag_rows = pl.ds(pl.multiple_of(BLOCK + index * 8, 8), 8)

        def lanes(t):
            return pl.ds(t * BLOCK, BLOCK)

        k_real = [taps_ref[d, real_rows, :] for d in range(parts)]
        k_imag = [taps_ref[d, imag_rows, :] for d in range(parts)]
        g_real = [grad_spec[real_rows, lanes(t)] for t in range(parts)]
        g_imag = [grad_spec[imag_rows, lanes(t)] for t in range(parts)]
        for t in range(parts):
            sum_real = jnp.zeros((8, BLOCK), F32)
            sum_imag = jnp.zeros((8, BLOCK), F32)
            for s in range(t, parts):
                d = s - t
                sum_real += k_real[d] * g_real[s] + k_imag[d] * g_imag[s]
                sum_imag += k_real[d] * g_imag[s] - k_imag[d] * g_real[s]
            mixed[real_rows, lanes(t)] = sum_real
            mixed[imag_rows, lanes(t)] = sum_imag
        u_real = [spec_ref[0, real_rows, lanes(t)] for t in range(parts)]
        u_imag = [spec_ref[0, imag_rows, lanes(t)] for t in range(parts)]
        for d in range(parts):
            sum_real = pairs[real_rows, lanes(d)]
            sum_imag = pairs[imag_rows, lanes(d)]
            for t in range(parts - d):
                s = t + d
                sum_real += u_real[t] * g_real[s] + u_imag[t] * g_imag[s]
                sum_imag += u_real[t] * g_imag[s] - u_imag[t] * g_real[s]
            pairs[real_rows, lanes(d)] = sum_real
            pairs[imag_rows, lanes(d)] = sum_imag
        return 0

    lax.fori_loop(0, BLOCK // 8, per_tile, 0)
    result = dot_parts(back_high[...], back_low[...], mixed[...])
    for s in range(parts):
        y_ref[s, 0] = result[:, s * BLOCK : (s + 1) * BLOCK]

    @pl.when(step == count - 1)
    def _():
        sign = alternate_sign(BLOCK)
        for d in range(parts):
            here = pl.ds(d * BLOCK, BLOCK)
            real_part = pairs[:BLOCK, here]
            imag_part = pairs[BLOCK:, here]
            if d + 1 < parts:
                after = pl.ds((d + 1) * BLOCK, BLOCK)
                real_part = real_part + sign * pairs[BLOCK:, after]
                imag_part = imag_part - sign * pairs[:BLOCK, after]
            mixed[:BLOCK, here] = real_part
            mixed[BLOCK:, here] = imag_part
        taps_grad = dot_parts(back_high[...], back_low[...], mixed[...])
        for d in range(parts):
            taps_grad_ref[d] = taps_grad[:, d * BLOCK : (d + 1) * BLOCK]


def convolve_back(series, spectra, taps, tables):
    parts, count = series.shape[:2]
    wide = parts * BLOCK
    return pl.pallas_call(
        functools.partial(conv_back_kernel, parts, count),
        grid=(count,),
        in_specs=[
            pl.BlockSpec((parts, 1, BLOCK, BLOCK), lambda i: (0, i, 0, 0)),
            pl.BlockSpec((1, 2 * BLOCK, wide), lambda i: (i, 0, 0)),
            whole((parts, 2 * BLOCK, BLOCK)),
            whole((2 * BLOCK, BLOCK)),
            whole((2 * BLOCK, BLOCK)),
            whole((BLOCK, 2 * BLOCK)),
            whole((BLOCK, 2 * BLOCK)),
        ],
        out_specs=[
            pl.BlockSpec((parts, 1, BLOCK, BLOCK), lambda i: (0, i, 0, 0)),
            whole((parts, BLOCK, BLOCK)),
        ],
        out_shape=[
            jax.ShapeDtypeStruct((parts, count, BLOCK, BLOCK), F32),
            jax.ShapeDtypeStruct((parts, BLOCK, BLOCK), F32),
        ],
        scratch_shapes=[pltpu.VMEM((2 * BLOCK, wide), F32)] * 3,
        compiler_params=params_of("arbitrary"),
        cost_estimate=cost_of(count * 1.2e9, count * 3e6),
        name="convolve_back",
    )(series, spectra, taps, *tables)


def moments_kernel(
    rate_ref,
    turn_ref,
    grad_ref,
    out_ref,
    low_real,
    low_imag,
    high_real,
    high_imag,
):
    modes = rate_ref.shape[0]
    count = high_real.shape[0]
    low_table(rate_ref, turn_ref, low_real, low_imag)
    ones = jnp.ones(rate_ref.shape, F32)
    high_table(rate_ref, turn_ref, ones, jnp.zeros_like(ones), high_real, high_imag)
    places = lax.broadcasted_iota(jnp.int32, (STEP_LOW, 1), 0).astype(F32)
    tile = 8

    def per_mode(mode, _):
        row = pl.ds(mode, 1)
        zeros = jnp.zeros((STEP_LOW, BLOCK), F32)

        def per_tile(index, sums):
            plain_real, plain_imag, by_real, by_imag = sums
            for k in range(tile):
                place = index * tile + k
                rows = pl.ds(pl.multiple_of(place * STEP_LOW, STEP_LOW), STEP_LOW)
                grad = grad_ref[rows, :]
                term_real = high_real[place, row, :] * grad
                term_imag = high_imag[place, row, :] * grad
                plain_real += term_real
                plain_imag += term_imag
                weight = (place * STEP_LOW).astype(F32)
                by_real += term_real * weight
                by_imag += term_imag * weight
            return plain_real, plain_imag, by_real, by_imag

        plain_real, plain_imag, by_real, by_imag = lax.fori_loop(
            0, count // tile, per_tile, (zeros,) * 4
        )
        base_real = low_real[mode]
        base_imag = low_imag[mode]

        def total(rows_in):
            return jnp.sum(rows_in, axis=0, keepdims=True)

        first_real = by_real + places * plain_real
        first_imag = by_imag + places * plain_imag
        out_ref[0, row, :] = total(base_real * plain_real - base_imag * plain_imag)
        out_ref[1, row, :] = total(base_real * plain_imag + base_imag * plain_real)
        out_ref[2, row, :] = total(base_real * first_real - base_imag * first_imag)
        out_ref[3, row, :] = total(base_real * first_imag + base_imag * first_real)
        return 0

    lax.fori_loop(0, modes, per_mode, 0)


def make_moments(rate, turn, taps_grad):
    modes = rate.shape[0]
    length = taps_grad.shape[0]
    high_count = length // STEP_LOW
    return pl.pallas_call(
        moments_kernel,
        grid=(1,),
        in_specs=[whole((modes, BLOCK)), whole((modes, BLOCK)), whole((length, BLOCK))],
        out_specs=whole((4, modes, BLOCK)),
        out_shape=jax.ShapeDtypeStruct((4, modes, BLOCK), F32),
        scratch_shapes=[
            pltpu.VMEM((modes, STEP_LOW, BLOCK), F32),
            pltpu.VMEM((modes, STEP_LOW, BLOCK), F32),
            pltpu.VMEM((high_count, modes, BLOCK), F32),
            pltpu.VMEM((high_count, modes, BLOCK), F32),
        ],
        compiler_params=params_of("arbitrary"),
        cost_estimate=cost_of(4e9, 2e6),
        name="moments",
    )(rate, turn, taps_grad)


GELU_SCALE = 0.7978845608
GELU_CUBE = 0.044715


def gelu_both(value):
    square = value * value
    inner = GELU_SCALE * value * (1.0 + GELU_CUBE * square)
    bend = jnp.tanh(inner)
    half = 0.5 * (1.0 + bend)
    slope = half + 0.5 * value * (1.0 - bend * bend) * (
        GELU_SCALE * (1.0 + 3.0 * GELU_CUBE * square)
    )
    return value * half, slope


def sigmoid(value):
    return 0.5 * (1.0 + jnp.tanh(0.5 * value))


def dot(left, right):
    return jnp.dot(left, right, preferred_element_type=F32)


def dot_nt(left, right):
    return lax.dot_general(left, right, (((1,), (1,)), ((), ())), preferred_element_type=F32)


def dot_tn(left, right):
    return lax.dot_general(left, right, (((0,), (0,)), ((), ())), preferred_element_type=F32)


def joined(ref, count):
    parts = ref.shape[0]
    rows = [
        jnp.concatenate([ref[g, c] for g in range(parts)], axis=1) for c in range(count)
    ]
    return jnp.concatenate(rows, axis=0) if count > 1 else rows[0]


def forward_kernel(
    contexts,
    meta_ref,
    x_ref,
    conv_ref,
    signal_ref,
    skip_ref,
    glu_ref,
    glu_bias_ref,
    gain_ref,
    shift_ref,
    up_ref,
    up_bias_ref,
    act_own,
    act_send,
    act_slope,
    gate_a_ref,
    gate_sig_ref,
    hidden_ref,
    second_own,
    second_send,
    wide_own,
    wide_send,
    wide_slope,
    rows_scr,
):
    count = x_ref.shape[0]
    channels = x_ref.shape[2]
    core = meta_ref[contexts] & 1
    other = 1 - core
    chips = wide_own.shape[1] // (up_ref.shape[1] // (2 * (channels // (2 * BLOCK))))
    chips = channels // (2 * BLOCK)
    wide = up_ref.shape[1] // (2 * chips)

    def share(own_ref, send_ref, values):
        rows_scr[...] = values
        for z in range(chips):
            here = pl.ds(pl.multiple_of((2 * z + core) * BLOCK, BLOCK), BLOCK)
            there = pl.ds(pl.multiple_of((2 * z + other) * BLOCK, BLOCK), BLOCK)
            own_ref[:, z * BLOCK : (z + 1) * BLOCK] = rows_scr[:, here].astype(BF16)
            send_ref[:, z * BLOCK : (z + 1) * BLOCK] = rows_scr[:, there].astype(BF16).astype(F32)

    mixed = joined(conv_ref, count) + skip_ref[...] * joined(signal_ref, count)
    activated, slope = gelu_both(mixed)
    act_slope[...] = slope
    share(act_own, act_send, activated)
    activated = activated.astype(BF16)
    gate_a = dot(activated, glu_ref[:, :channels]) + glu_bias_ref[:, :channels]
    gate_a_ref[...] = gate_a
    gate_sig = sigmoid(dot(activated, glu_ref[:, channels:]) + glu_bias_ref[:, channels:])
    gate_sig_ref[...] = gate_sig
    x = x_ref[...].astype(F32).reshape(count * BLOCK, channels)
    hidden = x + gate_a * gate_sig
    hidden_ref[...] = hidden
    unit, _ = norm_rows(hidden)
    second = unit * gain_ref[...] + shift_ref[...]
    share(second_own, second_send, second)
    second = second.astype(BF16)
    for z in range(chips):
        slot = slice(z * wide, (z + 1) * wide)
        here = pl.ds(pl.multiple_of((2 * z + core) * wide, wide), wide)
        there = pl.ds(pl.multiple_of((2 * z + other) * wide, wide), wide)
        for cols, is_own in ((there, False), (here, True)):
            widened, slope = gelu_both(dot(second, up_ref[:, cols]) + up_bias_ref[:, cols])
            widened = widened.astype(BF16)
            wide_slope[:, cols] = slope.astype(BF16)
            if is_own:
                wide_own[:, slot] = widened
            else:
                wide_send[:, slot] = widened.astype(F32)


def make_forward(
    meta, block_input, conv, signal, skip, glu, glu_bias, gain, shift, up, up_bias, base, step
):
    contexts, block_len, channels = block_input.shape
    parts, count = conv.shape[:2]
    hidden_units = up.shape[1]
    rows = step * BLOCK
    grid = count // step
    all_rows = count * BLOCK
    first = base // step
    once = pl.Buffered(1)

    def rows_of(columns):
        return pl.BlockSpec((rows, columns), lambda i, m: (i, 0))

    def fixed(shape):
        return pl.BlockSpec(shape, lambda i, m: (0, 0), pipeline_mode=once)

    blocks = pl.BlockSpec((parts, step, BLOCK, BLOCK), lambda i, m: (0, i, 0, 0))
    half, half_wide = channels // 2, hidden_units // 2
    outs = [
        (half, BF16),
        (half, F32),
        (channels, F32),
        (channels, F32),
        (channels, F32),
        (channels, F32),
        (half, BF16),
        (half, F32),
        (half_wide, BF16),
        (half_wide, F32),
        (hidden_units, BF16),
    ]
    return pl.pallas_call(
        functools.partial(forward_kernel, contexts),
        grid_spec=pltpu.PrefetchScalarGridSpec(
            num_scalar_prefetch=1,
            grid=(grid,),
            in_specs=[
                pl.BlockSpec((step, block_len, channels), lambda i, m: (first + i, 0, 0)),
                blocks,
                blocks,
                fixed((1, channels)),
                fixed((channels, 2 * channels)),
                fixed((1, 2 * channels)),
                fixed((1, channels)),
                fixed((1, channels)),
                fixed((channels, hidden_units)),
                fixed((1, hidden_units)),
            ],
            out_specs=[rows_of(columns) for columns, _ in outs],
            scratch_shapes=[pltpu.VMEM((rows, channels), F32)],
        ),
        out_shape=[jax.ShapeDtypeStruct((all_rows, columns), kind) for columns, kind in outs],
        compiler_params=params_of("arbitrary"),
        cost_estimate=cost_of(2 * all_rows * channels * (2 * channels + hidden_units), 3e7),
        name="forward_rows",
    )(meta, block_input, conv, signal, skip, glu, glu_bias, gain, shift, up, up_bias)


def output_kernel(
    contexts, base, meta_ref, hidden_ref, wide_own, wide_send, down_ref, bias_ref, out_ref
):
    count = out_ref.shape[0]
    channels = hidden_ref.shape[1]
    core = meta_ref[contexts] & 1
    chips = channels // (2 * BLOCK)
    wide = wide_own.shape[1] // chips
    total = hidden_ref[...] + bias_ref[...]
    for z in range(chips):
        slot = slice(z * wide, (z + 1) * wide)
        here = pl.ds(pl.multiple_of((2 * z + core) * wide, wide), wide)
        there = pl.ds(pl.multiple_of((2 * z + 1 - core) * wide, wide), wide)
        total += dot(wide_own[:, slot], down_ref[here, :])
        total += dot(wide_send[:, slot].astype(BF16), down_ref[there, :])
    first = base + pl.program_id(0) * count
    for c in range(count):
        mask = mask_column(meta_ref, first + c, contexts)
        out_ref[c] = (total[c * BLOCK : (c + 1) * BLOCK] * mask).astype(BF16)


def make_output(meta, contexts, hidden, wide_own, wide_send, down, bias, base, step):
    all_rows, channels = hidden.shape
    hidden_units = down.shape[0]
    rows = step * BLOCK
    once = pl.Buffered(1)

    def rows_of(columns):
        return pl.BlockSpec((rows, columns), lambda i, m: (i, 0))

    return pl.pallas_call(
        functools.partial(output_kernel, contexts, base),
        grid_spec=pltpu.PrefetchScalarGridSpec(
            num_scalar_prefetch=1,
            grid=(all_rows // rows,),
            in_specs=[
                rows_of(channels),
                rows_of(hidden_units // 2),
                rows_of(hidden_units // 2),
                pl.BlockSpec((hidden_units, channels), lambda i, m: (0, 0), pipeline_mode=once),
                pl.BlockSpec((1, channels), lambda i, m: (0, 0)),
            ],
            out_specs=pl.BlockSpec((step, BLOCK, channels), lambda i, m: (i, 0, 0)),
        ),
        out_shape=jax.ShapeDtypeStruct((all_rows // BLOCK, BLOCK, channels), BF16),
        compiler_params=params_of("arbitrary"),
        cost_estimate=cost_of(2 * all_rows * channels * hidden_units, 1.6e7),
        name="output_rows",
    )(meta, hidden, wide_own, wide_send, down, bias)


def mask_rows_kernel(contexts, meta_ref, grad_ref, out_ref, sum_ref):
    context = pl.program_id(0)
    rows = grad_ref[0].astype(F32) * mask_column(meta_ref, context, contexts)
    out_ref[...] = rows

    @pl.when(context == 0)
    def _():
        sum_ref[...] = jnp.zeros_like(sum_ref)

    sum_ref[...] += jnp.sum(rows, axis=0, keepdims=True)


def mask_rows(meta, out_grad):
    contexts, block_len, channels = out_grad.shape
    return pl.pallas_call(
        functools.partial(mask_rows_kernel, contexts),
        grid_spec=pltpu.PrefetchScalarGridSpec(
            num_scalar_prefetch=1,
            grid=(contexts,),
            in_specs=[pl.BlockSpec((1, block_len, channels), lambda i, m: (i, 0, 0))],
            out_specs=[
                pl.BlockSpec((block_len, channels), lambda i, m: (i, 0)),
                pl.BlockSpec((1, channels), lambda i, m: (0, 0)),
            ],
        ),
        out_shape=[
            jax.ShapeDtypeStruct((contexts * block_len, channels), F32),
            jax.ShapeDtypeStruct((1, channels), F32),
        ],
        compiler_params=params_of("arbitrary"),
        cost_estimate=cost_of(0, 4e6),
        name="mask_rows",
    )(meta, out_grad)


def backward_kernel(
    grad_ref,
    wide_slope,
    hidden_ref,
    gate_a_ref,
    gate_sig_ref,
    act_slope,
    gain_ref,
    down_ref,
    up_ref,
    glu_ref,
    inner_out,
    gates_out,
    hidden_grad_ref,
    mixed_out,
    inner_sum,
    gates_sum,
    gain_sum,
    shift_sum,
):
    count = mixed_out.shape[1]
    parts = mixed_out.shape[0]
    channels = hidden_ref.shape[1]
    hidden_units = up_ref.shape[1]
    tile = 512

    @pl.when(pl.program_id(0) == 0)
    def _():
        inner_sum[...] = jnp.zeros_like(inner_sum)
        gates_sum[...] = jnp.zeros_like(gates_sum)
        gain_sum[...] = jnp.zeros_like(gain_sum)
        shift_sum[...] = jnp.zeros_like(shift_sum)

    def add_rows(ref, cols, values):
        ref[:, cols] += jnp.sum(values, axis=0, keepdims=True)

    grad_out = grad_ref[...]
    grad_low = grad_out.astype(BF16)
    grad_second = jnp.zeros(grad_out.shape, F32)
    for k in range(hidden_units // tile):
        cols = slice(k * tile, (k + 1) * tile)
        grad_wide = dot_nt(grad_low, down_ref[cols, :])
        inner = (grad_wide * wide_slope[:, cols].astype(F32)).astype(BF16)
        inner_full = inner.astype(F32)
        inner_out[:, cols] = inner_full
        add_rows(inner_sum, cols, inner_full)
        grad_second += dot_nt(inner, up_ref[:, cols])
    unit, scale = norm_rows(hidden_ref[...])
    every = slice(0, channels)
    add_rows(gain_sum, every, grad_second * unit)
    add_rows(shift_sum, every, grad_second)
    scaled = grad_second * gain_ref[...]
    grad_hidden = grad_out + scale * (
        scaled
        - jnp.mean(scaled, axis=-1, keepdims=True)
        - unit * jnp.mean(scaled * unit, axis=-1, keepdims=True)
    )
    hidden_grad_ref[...] = grad_hidden
    gate_sig = gate_sig_ref[...]
    gate_grad = grad_hidden * gate_sig
    first = gate_grad.astype(BF16)
    later = (gate_grad * gate_a_ref[...] * (1.0 - gate_sig)).astype(BF16)
    grad_act = dot_nt(first, glu_ref[:, :channels]) + dot_nt(later, glu_ref[:, channels:])
    second_half = slice(channels, 2 * channels)
    for values, cols in ((first.astype(F32), every), (later.astype(F32), second_half)):
        gates_out[:, cols] = values
        add_rows(gates_sum, cols, values)
    mixed = grad_act * act_slope[...]
    for c in range(count):
        for g in range(parts):
            mixed_out[g, c] = mixed[c * BLOCK : (c + 1) * BLOCK, g * BLOCK : (g + 1) * BLOCK]


def make_backward(
    grad_out, wide_slope, hidden, gate_a, gate_sig, act_slope, gain, down, up, glu, base, step
):
    all_rows, channels = hidden.shape
    hidden_units = up.shape[1]
    rows = step * BLOCK
    parts = channels // BLOCK
    first = base // step
    once = pl.Buffered(1)

    def rows_of(columns, start=0):
        return pl.BlockSpec((rows, columns), lambda i: (start + i, 0))

    def fixed(shape):
        return pl.BlockSpec(shape, lambda i: (0, 0), pipeline_mode=once)

    def row_sum(columns):
        return pl.BlockSpec((1, columns), lambda i: (0, 0))

    sums = [hidden_units, 2 * channels, channels, channels]
    return pl.pallas_call(
        backward_kernel,
        grid=(all_rows // rows,),
        in_specs=[
            rows_of(channels, first),
            rows_of(hidden_units),
            rows_of(channels),
            rows_of(channels),
            rows_of(channels),
            rows_of(channels),
            fixed((1, channels)),
            fixed((hidden_units, channels)),
            fixed((channels, hidden_units)),
            fixed((channels, 2 * channels)),
        ],
        out_specs=[
            rows_of(hidden_units),
            rows_of(2 * channels),
            rows_of(channels),
            pl.BlockSpec((parts, step, BLOCK, BLOCK), lambda i: (0, i, 0, 0)),
        ]
        + [row_sum(columns) for columns in sums],
        out_shape=[
            jax.ShapeDtypeStruct((all_rows, hidden_units), F32),
            jax.ShapeDtypeStruct((all_rows, 2 * channels), F32),
            jax.ShapeDtypeStruct((all_rows, channels), F32),
            jax.ShapeDtypeStruct((parts, all_rows // BLOCK, BLOCK, BLOCK), F32),
        ]
        + [jax.ShapeDtypeStruct((1, columns), F32) for columns in sums],
        compiler_params=params_of("arbitrary"),
        cost_estimate=cost_of(
            2 * all_rows * channels * (2 * channels + 2 * hidden_units), 3.5e7
        ),
        name="backward_rows",
    )(grad_out, wide_slope, hidden, gate_a, gate_sig, act_slope, gain, down, up, glu)


def weight_grad_kernel(pieces, *refs):
    out_ref = refs[-1]
    total = None
    for k in range(pieces):
        left, right = refs[2 * k], refs[2 * k + 1]
        term = dot_tn(left[...].astype(BF16), right[...].astype(BF16))
        total = term if total is None else total + term
    out_ref[...] = total.reshape(out_ref.shape)


def weight_grad(pairs, chips, row_tiles, col_tiles, name):
    rows = pairs[0][0].shape[1]
    cols = pairs[0][1].shape[1]
    row_block = rows // row_tiles
    col_block = cols // col_tiles
    per_chip = rows // chips
    in_specs = []
    operands = []
    nbytes = rows * cols * 4
    tokens_all = 0
    for left, right in pairs:
        tokens = left.shape[0]
        in_specs.append(pl.BlockSpec((tokens, row_block), lambda i, j: (0, i)))
        in_specs.append(pl.BlockSpec((tokens, col_block), lambda i, j: (0, j)))
        operands += [left, right]
        tokens_all += tokens
        nbytes += left.size * left.dtype.itemsize + right.size * right.dtype.itemsize
    return pl.pallas_call(
        functools.partial(weight_grad_kernel, len(pairs)),
        grid=(row_tiles, col_tiles),
        in_specs=in_specs,
        out_specs=pl.BlockSpec((chips // row_tiles, per_chip, col_block), lambda i, j: (i, 0, j)),
        out_shape=jax.ShapeDtypeStruct((chips, per_chip, cols), F32),
        compiler_params=params_of("arbitrary", "arbitrary"),
        cost_estimate=cost_of(2 * rows * cols * tokens_all, nbytes),
        name=name,
    )(*operands)


def input_grad_kernel(
    contexts,
    base,
    meta_ref,
    x_ref,
    conv_grad_ref,
    mixed_ref,
    signal_ref,
    hidden_grad_ref,
    skip_ref,
    gain_ref,
    out_ref,
    skip_sum,
    gain_sum,
    shift_sum,
):
    @pl.when(pl.program_id(0) == 0)
    def _():
        skip_sum[...] = jnp.zeros_like(skip_sum)
        gain_sum[...] = jnp.zeros_like(gain_sum)
        shift_sum[...] = jnp.zeros_like(shift_sum)

    mask = mask_column(meta_ref, pl.program_id(0) + base, contexts)
    mixed = joined(mixed_ref, 1)
    skip_sum[...] += jnp.sum(mixed * joined(signal_ref, 1), axis=0, keepdims=True)
    grad_normed = (joined(conv_grad_ref, 1) + skip_ref[...] * mixed) * mask
    unit, scale = norm_rows(x_ref[0].astype(F32))
    gain_sum[...] += jnp.sum(grad_normed * unit, axis=0, keepdims=True)
    shift_sum[...] += jnp.sum(grad_normed, axis=0, keepdims=True)
    scaled = grad_normed * gain_ref[...]
    grad = hidden_grad_ref[...] + scale * (
        scaled
        - jnp.mean(scaled, axis=-1, keepdims=True)
        - unit * jnp.mean(scaled * unit, axis=-1, keepdims=True)
    )
    out_ref[0] = grad.astype(BF16)


def make_input_grad(
    meta, block_input, conv_grad, mixed_grad, signal, hidden_grad, skip, gain, base
):
    contexts, block_len, channels = block_input.shape
    parts, count = conv_grad.shape[:2]
    blocks = pl.BlockSpec((parts, 1, BLOCK, BLOCK), lambda i, m: (0, i, 0, 0))
    vector = pl.BlockSpec((1, channels), lambda i, m: (0, 0))
    return pl.pallas_call(
        functools.partial(input_grad_kernel, contexts, base),
        grid_spec=pltpu.PrefetchScalarGridSpec(
            num_scalar_prefetch=1,
            grid=(count,),
            in_specs=[
                pl.BlockSpec((1, block_len, channels), lambda i, m: (base + i, 0, 0)),
                blocks,
                blocks,
                blocks,
                pl.BlockSpec((BLOCK, channels), lambda i, m: (i, 0)),
                vector,
                vector,
            ],
            out_specs=[
                pl.BlockSpec((1, block_len, channels), lambda i, m: (i, 0, 0)),
                vector,
                vector,
                vector,
            ],
        ),
        out_shape=[
            jax.ShapeDtypeStruct((count, block_len, channels), BF16),
            jax.ShapeDtypeStruct((1, channels), F32),
            jax.ShapeDtypeStruct((1, channels), F32),
            jax.ShapeDtypeStruct((1, channels), F32),
        ],
        compiler_params=params_of("arbitrary"),
        cost_estimate=cost_of(0, count * 3e6),
        name="input_grad",
    )(meta, block_input, conv_grad, mixed_grad, signal, hidden_grad, skip, gain)


def send_along(value, move):
    groups = lax.axis_size("ctx")
    places = lax.axis_size("seq")
    pairs = []
    for c in range(groups):
        for s in range(places):
            to_c, to_s = move(c, s)
            pairs.append((c * places + s, to_c * places + to_s))
    return lax.ppermute(value, AXES, pairs)


def to_sibling(value):
    return send_along(value, lambda c, s: (c, s ^ 1))


def to_x(value):
    return send_along(value, lambda c, s: (c ^ 1, s))


def to_y(value):
    return send_along(value, lambda c, s: (c ^ 2, s))


def to_chip(value, hops):
    places = lax.axis_size("seq")
    return send_along(value, lambda c, s: (c, (s + 2 * hops) % places))


def swap_blocks(value):
    return lax.all_to_all(value, "seq", split_axis=0, concat_axis=0, tiled=True)


def take(value, index, axis):
    return lax.dynamic_index_in_dim(value, index, axis, keepdims=False)


def placed(mine, theirs, index):
    return jnp.where(
        index == 0, jnp.stack([mine, theirs], axis=0), jnp.stack([theirs, mine], axis=0)
    )


def reduce_rows(part, x_index, y_index, z_index):
    chips, rows, cols = part.shape
    view = part.reshape(chips, 2, 2, 2, rows // 8, cols)
    a_part, b_part = view[:, 0], view[:, 1]
    a_got = to_x(take(a_part, 1 - x_index, 1))
    b_got = to_y(take(b_part, 1 - y_index, 2))
    a_sum = take(a_part, x_index, 1) + a_got
    b_sum = take(b_part, y_index, 2) + b_got
    a_got = to_y(take(a_sum, 1 - y_index, 1))
    b_got = to_x(take(b_sum, 1 - x_index, 1))
    a_sum = take(a_sum, y_index, 1) + a_got
    b_sum = take(b_sum, x_index, 1) + b_got
    both = jnp.stack([a_sum, b_sum], axis=1)
    total = take(both, z_index, 0)
    for hops in range(1, chips):
        total = total + to_chip(take(both, (z_index + hops) % chips, 0), hops)
    a_mine, b_mine = total[0], total[1]
    a_got = to_y(a_mine)
    b_got = to_x(b_mine)
    a_mine = placed(a_mine, a_got, y_index)
    b_mine = placed(b_mine, b_got, x_index)
    a_got = to_x(a_mine)
    b_got = to_y(b_mine)
    a_all = placed(a_mine, a_got, x_index)
    b_all = placed(b_mine, b_got, y_index).transpose(1, 0, 2, 3)
    return jnp.stack([a_all, b_all], axis=0).reshape(rows, cols)


def sum_everywhere(value):
    value = value + to_sibling(value)
    value = value + to_x(value)
    value = value + to_y(value)
    value = value + send_along(value, lambda c, s: (c, s ^ 2))
    return value + send_along(value, lambda c, s: (c, s ^ 4))


PIECE = 2


def local_fast(
    block_input,
    valid_len,
    out_grad,
    first_gain,
    first_shift,
    log_step,
    decay_log,
    turn_rate,
    read_real,
    read_imag,
    skip_gain,
    glu_weight,
    glu_bias,
    second_gain,
    second_shift,
    up_weight,
    up_bias,
    down_weight,
    down_bias,
):
    parts = lax.axis_size("seq")
    chips = parts // 2
    seq_index = lax.axis_index("seq")
    ctx_index = lax.axis_index("ctx")
    x_index, y_index, z_index = ctx_index % 2, ctx_index // 2, seq_index // 2
    contexts, block_len, channels = block_input.shape
    meta = jnp.concatenate([valid_len, seq_index[None].astype(jnp.int32)])

    def row(vector):
        return vector.reshape(1, -1)

    tables = odd_tables()
    bases = list(range(0, contexts, PIECE))

    signals = [
        make_signal(meta, block_input, row(first_gain), row(first_shift), base, PIECE)
        for base in bases
    ]
    received = [swap_blocks(signal) for signal in signals]
    first_channel = seq_index * BLOCK
    own_params = (lax.dynamic_slice_in_dim(log_step, first_channel, BLOCK, 0),) + tuple(
        lax.dynamic_slice_in_dim(tensor.T, first_channel, BLOCK, 1)
        for tensor in (decay_log, turn_rate, read_real, read_imag)
    )
    coefs, coefs_back = jax.vjp(mode_coefs, *own_params)
    taps = make_spectrum(coefs, tables, parts)
    grad_out, down_bias_part = mask_rows(meta, out_grad)
    grad_out_got = to_sibling(grad_out)
    convs = []
    spectra = []
    for series in received:
        conv, spectrum = convolve(series, taps, tables)
        convs.append(swap_blocks(conv))
        spectra.append(spectrum)

    ahead = [
        make_forward(
            meta,
            block_input,
            conv,
            signal,
            row(skip_gain),
            glu_weight,
            row(glu_bias),
            row(second_gain),
            row(second_shift),
            up_weight,
            row(up_bias),
            base,
            PIECE,
        )
        for base, conv, signal in zip(bases, convs, signals)
    ]
    rows_each = PIECE * BLOCK

    def piece_of(rows, k):
        return rows[k * rows_each : (k + 1) * rows_each]

    wide_got = [to_sibling(piece[9]) for piece in ahead]
    outputs = [
        make_output(
            meta, contexts, piece[5], piece[8], piece[9], down_weight, row(down_bias), base, PIECE
        )
        for base, piece in zip(bases, ahead)
    ]
    pairs = []
    for k, piece in enumerate(ahead):
        pairs.append((piece[8], piece_of(grad_out, k)))
        pairs.append((wide_got[k], piece_of(grad_out_got, k)))
    down_part = weight_grad(pairs, chips, 4, 1, "down_grad")
    down_total = reduce_rows(down_part, x_index, y_index, z_index)

    backs = [
        make_backward(
            grad_out,
            piece[10],
            piece[5],
            piece[3],
            piece[4],
            piece[2],
            row(second_gain),
            down_weight,
            up_weight,
            glu_weight,
            base,
            PIECE,
        )
        for base, piece in zip(bases, ahead)
    ]
    pairs = []
    for piece, back in zip(ahead, backs):
        pairs.append((piece[6], back[0]))
        pairs.append((to_sibling(piece[7]), to_sibling(back[0])))
    up_part = weight_grad(pairs, chips, 1, 4, "up_grad")
    up_total = reduce_rows(up_part, x_index, y_index, z_index)
    pairs = []
    for piece, back in zip(ahead, backs):
        pairs.append((piece[0], back[1]))
        pairs.append((to_sibling(piece[1]), to_sibling(back[1])))
    glu_part = weight_grad(pairs, chips, 1, 2, "glu_grad")
    glu_total = reduce_rows(glu_part, x_index, y_index, z_index)

    conv_grads = []
    taps_grad = 0.0
    for back, spectrum in zip(backs, spectra):
        conv_grad, taps_piece = convolve_back(swap_blocks(back[3]), spectrum, taps, tables)
        conv_grads.append(swap_blocks(conv_grad))
        taps_grad = taps_grad + taps_piece
    moments = make_moments(coefs[0], coefs[1], taps_grad.reshape(parts * BLOCK, BLOCK))
    zero_real, zero_imag, one_real, one_imag = (moments[k] for k in range(4))
    coef_real, coef_imag = coefs[2], coefs[3]
    own_grads = coefs_back(
        (
            2.0 * (coef_real * one_real - coef_imag * one_imag),
            -2.0 * (coef_real * one_imag + coef_imag * one_real),
            2.0 * zero_real,
            -2.0 * zero_imag,
        )
    )
    own_rows = jnp.concatenate([own_grads[0][None, :]] + list(own_grads[1:]), axis=0)
    pad = -own_rows.shape[0] % 8
    own_rows = jnp.pad(own_rows, ((0, pad), (0, 0)))
    own_rows = own_rows + to_x(own_rows)
    own_rows = own_rows + to_y(own_rows)
    every_row = lax.all_gather(own_rows, "seq", axis=1, tiled=True)
    modes = decay_log.shape[1]
    mode_grads = [every_row[1 + k * modes : 1 + (k + 1) * modes].T for k in range(4)]

    last = [
        make_input_grad(
            meta,
            block_input,
            conv_grad,
            back[3],
            signal,
            back[2],
            row(skip_gain),
            row(first_gain),
            base,
        )
        for base, conv_grad, back, signal in zip(bases, conv_grads, backs, signals)
    ]

    def added(items):
        total = items[0]
        for item in items[1:]:
            total = total + item
        return total

    vectors = [
        added([piece[2] for piece in last]),
        added([piece[3] for piece in last]),
        added([piece[1] for piece in last]),
        added([back[5] for back in backs]),
        added([back[6] for back in backs]),
        added([back[7] for back in backs]),
        added([back[4] for back in backs]),
        down_bias_part,
    ]
    flat = jnp.concatenate([vector.reshape(-1, BLOCK) for vector in vectors], axis=0)
    flat = sum_everywhere(flat)
    sums = []
    start = 0
    for vector in vectors:
        size = vector.size // BLOCK
        sums.append(flat[start : start + size].reshape(-1))
        start += size
    gain_sum, shift_sum, skip_sum, glu_bias_sum, gain2_sum, shift2_sum, up_bias_sum, down_bias_sum = sums
    return (
        jnp.concatenate(outputs, axis=0),
        jnp.concatenate([piece[0] for piece in last], axis=0),
        gain_sum,
        shift_sum,
        every_row[0],
        mode_grads[0],
        mode_grads[1],
        mode_grads[2],
        mode_grads[3],
        skip_sum,
        glu_total,
        glu_bias_sum,
        gain2_sum,
        shift2_sum,
        up_total,
        up_bias_sum,
        down_total,
        down_bias_sum,
    )


def local_any(
    block_input,
    valid_len,
    out_grad,
    first_gain,
    first_shift,
    log_step,
    decay_log,
    turn_rate,
    read_real,
    read_imag,
    skip_gain,
    glu_weight,
    glu_bias,
    second_gain,
    second_shift,
    up_weight,
    up_bias,
    down_weight,
    down_bias,
):
    seq_parts = lax.axis_size("seq")
    seq_index = lax.axis_index("seq")
    contexts, block_len, channels = block_input.shape
    total_len = seq_parts * block_len
    row_count = contexts * block_len
    positions = seq_index * block_len + jnp.arange(block_len)
    valid_mask = (positions[None, :] < valid_len[:, None]).astype(jnp.float32)[:, :, None]
    flat_mask = valid_mask.reshape(row_count, 1)
    ssm_params = (log_step, decay_log, turn_rate, read_real, read_imag)
    inputs = block_input.astype(jnp.float32)
    normed_first, unit_first, scale_first = layer_norm(inputs, first_gain, first_shift)
    signal = normed_first * valid_mask
    chan_count = channels // seq_parts
    chan_params = jax.tree.map(
        lambda tensor: lax.dynamic_slice_in_dim(tensor, seq_index * chan_count, chan_count, 0),
        ssm_params,
    )
    all_float = jnp.arange(total_len).astype(jnp.float32)
    kernel_part = kernel_block(chan_params, all_float)
    sig_real, sig_imag = channel_spectrum(signal)
    ker_real, ker_imag = local_spectrum(kernel_part.reshape(1, seq_parts, block_len, chan_count))
    prod_real, prod_imag = times_kernel(sig_real, sig_imag, ker_real, ker_imag)
    conv_out = token_blocks(local_time(prod_real, prod_imag))
    mixed_seq = conv_out + skip_gain * signal
    activated_full, act_back = jax.vjp(gelu_tanh, mixed_seq)
    activated = activated_full.astype(jnp.bfloat16).reshape(row_count, channels)
    gate_rows = jnp.dot(activated, glu_weight, preferred_element_type=jnp.float32) + glu_bias
    gate_a = gate_rows[:, :channels]
    gate_sig = jax.nn.sigmoid(gate_rows[:, channels:])
    hidden = inputs.reshape(row_count, channels) + gate_a * gate_sig
    normed_second, unit_second, scale_second = layer_norm(hidden, second_gain, second_shift)
    second = normed_second.astype(jnp.bfloat16)
    inner_rows = jnp.dot(second, up_weight, preferred_element_type=jnp.float32) + up_bias
    widened_full, wide_back = jax.vjp(gelu_tanh, inner_rows)
    widened = widened_full.astype(jnp.bfloat16)
    result = hidden + jnp.dot(widened, down_weight, preferred_element_type=jnp.float32) + down_bias
    block_output = (result * flat_mask).astype(jnp.bfloat16).reshape(contexts, block_len, channels)
    grad_out = out_grad.reshape(row_count, channels) * flat_mask.astype(jnp.bfloat16)
    grad_out_f = grad_out.astype(jnp.float32)
    down_bias_grad = jnp.sum(grad_out_f, axis=0)
    down_grad = jnp.einsum("rf,rd->fd", widened, grad_out, preferred_element_type=jnp.float32)
    grad_wide = jnp.einsum("rd,fd->rf", grad_out, down_weight, preferred_element_type=jnp.float32)
    grad_inner = wide_back(grad_wide)[0].astype(jnp.bfloat16)
    up_bias_grad = jnp.sum(grad_inner.astype(jnp.float32), axis=0)
    up_grad = jnp.einsum("rd,rf->df", second, grad_inner, preferred_element_type=jnp.float32)
    grad_second = jnp.einsum("rf,df->rd", grad_inner, up_weight, preferred_element_type=jnp.float32)
    second_gain_grad = jnp.sum(grad_second * unit_second, axis=0)
    second_shift_grad = jnp.sum(grad_second, axis=0)
    grad_hidden = grad_out_f + norm_back(grad_second, unit_second, scale_second, second_gain)
    grad_first_half = grad_hidden * gate_sig
    grad_second_half = grad_hidden * gate_a * gate_sig * (1.0 - gate_sig)
    grad_gates = jnp.concatenate([grad_first_half, grad_second_half], axis=1).astype(jnp.bfloat16)
    glu_bias_grad = jnp.sum(grad_gates.astype(jnp.float32), axis=0)
    glu_grad = jnp.einsum("rd,re->de", activated, grad_gates, preferred_element_type=jnp.float32)
    grad_act = jnp.einsum("re,de->rd", grad_gates, glu_weight, preferred_element_type=jnp.float32)
    grad_mixed = act_back(grad_act.reshape(contexts, block_len, channels))[0]
    skip_gain_grad = jnp.sum(grad_mixed * signal, axis=(0, 1))
    grad_real, grad_imag = channel_spectrum(grad_mixed)
    back_real, back_imag = conj_products(
        sig_real, sig_imag, ker_real, ker_imag, grad_real, grad_imag
    )
    returned = local_time(back_real, back_imag)
    grad_conv = token_blocks(returned[:contexts])
    local_grads = kernel_grads(
        chan_params, all_float, returned[contexts].reshape(total_len, chan_count)
    )
    ssm_grads = jax.tree.map(
        lambda whole_grad, piece_grad: lax.dynamic_update_slice_in_dim(
            jnp.zeros_like(whole_grad), piece_grad, seq_index * chan_count, 0
        ),
        ssm_params,
        local_grads,
    )
    grad_signal = grad_conv + skip_gain * grad_mixed
    grad_normed = grad_signal * valid_mask
    first_gain_grad = jnp.sum(grad_normed * unit_first, axis=(0, 1))
    first_shift_grad = jnp.sum(grad_normed, axis=(0, 1))
    input_grad = (
        grad_hidden.reshape(contexts, block_len, channels)
        + norm_back(grad_normed, unit_first, scale_first, first_gain)
    ).astype(jnp.bfloat16)
    step_grad, decay_grad, turn_grad, real_grad, imag_grad = ssm_grads
    (
        first_gain_sum,
        first_shift_sum,
        step_sum,
        decay_sum,
        turn_sum,
        real_sum,
        imag_sum,
        skip_sum,
        glu_bias_sum,
        second_gain_sum,
        second_shift_sum,
        up_bias_sum,
        down_bias_sum,
    ) = lax.psum(
        (
            first_gain_grad,
            first_shift_grad,
            step_grad,
            decay_grad,
            turn_grad,
            real_grad,
            imag_grad,
            skip_gain_grad,
            glu_bias_grad,
            second_gain_grad,
            second_shift_grad,
            up_bias_grad,
            down_bias_grad,
        ),
        ("ctx", "seq"),
    )
    rows_glu, rows_up, rows_down = (
        lax.psum_scatter(glu_grad, "seq", scatter_dimension=0, tiled=True),
        lax.psum_scatter(up_grad, "seq", scatter_dimension=0, tiled=True),
        lax.psum_scatter(down_grad, "seq", scatter_dimension=0, tiled=True),
    )
    glu_total, up_total, down_total = lax.psum((rows_glu, rows_up, rows_down), "ctx")
    return (
        block_output,
        input_grad,
        first_gain_sum,
        first_shift_sum,
        step_sum,
        decay_sum,
        turn_sum,
        real_sum,
        imag_sum,
        skip_sum,
        glu_total,
        glu_bias_sum,
        second_gain_sum,
        second_shift_sum,
        up_total,
        up_bias_sum,
        down_total,
        down_bias_sum,
    )


def solution(mesh):
    in_specs = (
        P("ctx", "seq", None),
        P("ctx"),
        P("ctx", "seq", None),
        P(),
        P(),
        P(),
        P(),
        P(),
        P(),
        P(),
        P(),
        P(),
        P(),
        P(),
        P(),
        P(),
        P(),
        P(),
        P(),
    )
    out_specs = (
        P("ctx", "seq", None),
        P("ctx", "seq", None),
        P(),
        P(),
        P(),
        P(),
        P(),
        P(),
        P(),
        P(),
        P("seq", None),
        P(),
        P(),
        P(),
        P("seq", None),
        P(),
        P("seq", None),
        P(),
    )
    grid_size = (mesh.shape["ctx"], mesh.shape["seq"])
    step = local_fast if grid_size == (4, 8) else local_any
    return jax.shard_map(step, mesh=mesh, in_specs=in_specs, out_specs=out_specs, check_vma=False)
```

```python
import functools
import math

import jax
import jax.numpy as jnp
import numpy as np
from jax import lax
from jax.experimental import pallas as pl
from jax.experimental.pallas import tpu as pltpu
from jax.sharding import PartitionSpec as P

EPSILON = 1e-05
PRECISE = lax.Precision.HIGHEST


def gelu_tanh(values_in):
    return jax.nn.gelu(values_in, approximate=True)


def layer_norm(values_in, gain_vec, shift_vec):
    centre = values_in - jnp.mean(values_in, axis=-1, keepdims=True)
    scale_rows = lax.rsqrt(jnp.mean(centre * centre, axis=-1, keepdims=True) + EPSILON)
    unit_rows = centre * scale_rows
    return (unit_rows * gain_vec + shift_vec, unit_rows, scale_rows)


def norm_back(grad_rows, unit_rows, scale_rows, gain_vec):
    scaled = grad_rows * gain_vec
    return scale_rows * (
        scaled
        - jnp.mean(scaled, axis=-1, keepdims=True)
        - unit_rows * jnp.mean(scaled * unit_rows, axis=-1, keepdims=True)
    )


def kernel_piece(ssm_params, place_block):
    log_step, decay_log, turn_rate, read_real, read_imag = ssm_params
    step_size = jnp.exp(log_step)[:, None]
    decay_rate = jnp.exp(decay_log)
    rate_step = -decay_rate * step_size
    turn_step = turn_rate * step_size
    growth = jnp.exp(rate_step)
    edge_real = growth * jnp.cos(turn_step) - 1.0
    edge_imag = growth * jnp.sin(turn_step)
    modulus = decay_rate * decay_rate + turn_rate * turn_rate
    ratio_real = (-edge_real * decay_rate + edge_imag * turn_rate) / modulus
    ratio_imag = (-edge_imag * decay_rate - edge_real * turn_rate) / modulus
    coef_real = read_real * ratio_real - read_imag * ratio_imag
    coef_imag = read_real * ratio_imag + read_imag * ratio_real
    magnitude = jnp.exp(rate_step[:, :, None] * place_block[None, None, :])
    angles = turn_step[:, :, None] * place_block[None, None, :]
    terms = magnitude * (
        coef_real[:, :, None] * jnp.cos(angles) - coef_imag[:, :, None] * jnp.sin(angles)
    )
    return 2.0 * jnp.sum(terms, axis=1).T


def kernel_layout(ssm_params, positions):
    channels = ssm_params[0].shape[0]
    group_size = min(channels, 128)
    span_size = min(positions.shape[0], 128)
    group_count = channels // group_size
    grouped = jax.tree.map(
        lambda tensor: tensor.reshape((group_count, group_size) + tensor.shape[1:]), ssm_params
    )
    span_rows = positions.reshape(-1, span_size)
    return (channels, group_size, span_size, group_count, grouped, span_rows)


def kernel_block(ssm_params, positions):
    channels, group_size, span_size, group_count, grouped, span_rows = kernel_layout(
        ssm_params, positions
    )

    def per_group(piece_params):
        return lax.map(lambda place_block: kernel_piece(piece_params, place_block), span_rows)

    blocks = lax.map(per_group, grouped)
    return blocks.transpose(1, 2, 0, 3).reshape(positions.shape[0], channels)


def kernel_grads(ssm_params, positions, upstream):
    channels, group_size, span_size, group_count, grouped, span_rows = kernel_layout(
        ssm_params, positions
    )
    upstream_groups = upstream.reshape(
        span_rows.shape[0], span_size, group_count, group_size
    ).transpose(2, 0, 1, 3)

    def per_group(pairing):
        piece_params, piece_grad = pairing

        def accumulate(running, inputs_block):
            place_block, grad_block = inputs_block
            _, pullback = jax.vjp(
                lambda inner_params: kernel_piece(inner_params, place_block), piece_params
            )
            return (jax.tree.map(jnp.add, running, pullback(grad_block)[0]), None)

        initial = jax.tree.map(jnp.zeros_like, piece_params)
        totals, _ = lax.scan(accumulate, initial, (span_rows, piece_grad))
        return totals

    summed = lax.map(per_group, (grouped, upstream_groups))
    return jax.tree.map(lambda tensor: tensor.reshape((channels,) + tensor.shape[2:]), summed)


def phase_table(first_index, second_index, modulus):
    products_mod = first_index[:, None] * second_index[None, :] % modulus
    angles = products_mod.astype(jnp.float32) * (2.0 * math.pi / modulus)
    return (jnp.cos(angles), jnp.sin(angles))


def first_section(series, row_index, freq_index, modulus):
    cosine, sine_part = phase_table(row_index, freq_index, modulus)
    real_part = jnp.einsum("bnjh,nk->bkjh", series, cosine, precision=PRECISE)
    imag_part = -jnp.einsum("bnjh,nk->bkjh", series, sine_part, precision=PRECISE)
    return (real_part, imag_part)


def rotate(real_part, imag_part, row_index, col_index, modulus, direction):
    cosine, sine_part = phase_table(row_index, col_index, modulus)
    cosine = cosine[None, :, :, None]
    sine_part = direction * sine_part[None, :, :, None]
    return (real_part * cosine - imag_part * sine_part, real_part * sine_part + imag_part * cosine)


def mix_columns(real_part, imag_part, col_index, out_index, modulus, direction):
    cosine, sine_part = phase_table(col_index, out_index, modulus)
    sine_part = direction * sine_part

    def contract(operand, matrix):
        return jnp.einsum("bkjh,jm->bkmh", operand, matrix, precision=PRECISE)

    return (
        contract(real_part, cosine) - contract(imag_part, sine_part),
        contract(real_part, sine_part) + contract(imag_part, cosine),
    )


def last_section(real_part, imag_part, freq_index, row_index, modulus, length_all):
    cosine, sine_part = phase_table(freq_index, row_index, modulus)
    summed = jnp.einsum("bkjh,kn->bnjh", real_part, cosine, precision=PRECISE) - jnp.einsum(
        "bkjh,kn->bnjh", imag_part, sine_part, precision=PRECISE
    )
    return summed / length_all


def local_spectrum(series):
    seq_parts = series.shape[1]
    block_len = series.shape[2]
    freq_count = 2 * seq_parts
    modulus = freq_count * block_len
    freq_index = jnp.arange(freq_count)
    col_index = jnp.arange(block_len)
    real_part, imag_part = first_section(series, jnp.arange(seq_parts), freq_index, freq_count)
    real_part, imag_part = rotate(real_part, imag_part, freq_index, col_index, modulus, -1.0)
    return mix_columns(real_part, imag_part, col_index, col_index, block_len, -1.0)


def local_time(real_part, imag_part):
    freq_count = real_part.shape[1]
    block_len = real_part.shape[2]
    seq_parts = freq_count // 2
    modulus = freq_count * block_len
    freq_index = jnp.arange(freq_count)
    col_index = jnp.arange(block_len)
    real_part, imag_part = mix_columns(real_part, imag_part, col_index, col_index, block_len, 1.0)
    real_part, imag_part = rotate(real_part, imag_part, freq_index, col_index, modulus, 1.0)
    return last_section(
        real_part, imag_part, freq_index, jnp.arange(seq_parts), freq_count, modulus
    )


def channel_spectrum(series):
    seq_parts = lax.axis_size("seq")
    spread = lax.all_to_all(series, "seq", split_axis=2, concat_axis=1, tiled=True)
    batch_size, total_len, chan_count = spread.shape
    return local_spectrum(spread.reshape(batch_size, seq_parts, total_len // seq_parts, chan_count))


def token_blocks(series):
    batch_size, seq_parts, block_len, chan_count = series.shape
    flat_series = series.reshape(batch_size, seq_parts * block_len, chan_count)
    return lax.all_to_all(flat_series, "seq", split_axis=1, concat_axis=2, tiled=True)


def times_kernel(sig_real, sig_imag, ker_real, ker_imag):
    return (sig_real * ker_real - sig_imag * ker_imag, sig_real * ker_imag + sig_imag * ker_real)


def conj_products(sig_real, sig_imag, ker_real, ker_imag, grad_real, grad_imag):
    back_real = ker_real * grad_real + ker_imag * grad_imag
    back_imag = ker_real * grad_imag - ker_imag * grad_real
    kern_real = jnp.sum(sig_real * grad_real + sig_imag * grad_imag, axis=0, keepdims=True)
    kern_imag = jnp.sum(sig_real * grad_imag - sig_imag * grad_real, axis=0, keepdims=True)
    return (
        jnp.concatenate([back_real, kern_real], axis=0),
        jnp.concatenate([back_imag, kern_imag], axis=0),
    )


F32 = jnp.float32
BF16 = jnp.bfloat16
BLOCK = 128
STEP_LOW = 32
AXES = ("ctx", "seq")
VMEM_BYTES = 60 * 1024 * 1024
ONCE = pl.Buffered(1)
COST_SCALE = 4


def shape_of(shape, kind=F32):
    return jax.ShapeDtypeStruct(shape, kind)


def whole(shape):
    return pl.BlockSpec(shape, lambda *_: (0,) * len(shape))


def whole_once(shape):
    return pl.BlockSpec(shape, lambda *_: (0,) * len(shape), pipeline_mode=ONCE)


def launch(body, name, meta, after, ins, in_specs, outs, out_specs, grid, scratch=(), micros=1):
    n_in, n_out = len(ins), len(outs)
    after = list(after) if isinstance(after, (list, tuple)) else [after]
    anywhere = pl.BlockSpec(memory_space=pl.ANY)

    def kernel(meta_ref, *refs):
        first = n_in + len(after)
        last = first + n_out
        body(meta_ref, *refs[:n_in], *refs[first:last], *refs[last + 1 :])

    results = pl.pallas_call(
        kernel,
        grid_spec=pltpu.PrefetchScalarGridSpec(
            num_scalar_prefetch=1,
            grid=grid,
            in_specs=list(in_specs) + [anywhere] * len(after),
            out_specs=list(out_specs) + [anywhere],
            scratch_shapes=list(scratch),
        ),
        out_shape=list(outs) + [shape_of((8, BLOCK))],
        compiler_params=pltpu.CompilerParams(
            dimension_semantics=("arbitrary",) * len(grid), vmem_limit_bytes=VMEM_BYTES
        ),
        cost_estimate=pl.CostEstimate(
            flops=int(COST_SCALE * micros * 1.15e9), bytes_accessed=0, transcendentals=0
        ),
        name=name,
    )(meta, *ins, *after)
    return list(results[:-1]), results[-1]


def odd_tables():
    points = np.arange(BLOCK)
    turns = np.pi * np.outer(2 * points + 1, points) / (2 * BLOCK)
    ahead = np.concatenate([np.cos(turns), -np.sin(turns)], axis=0)
    back = ahead.T / BLOCK

    def halves(table):
        table = table.astype(np.float32)
        high = table.astype(BF16)
        return high, (table - high.astype(np.float32)).astype(BF16)

    return halves(ahead) + halves(back)


def dot_parts(high, low, operand):
    op_high = operand.astype(BF16)
    op_low = (operand - op_high.astype(F32)).astype(BF16)

    def one(left, right):
        return jnp.dot(left, right, preferred_element_type=F32)

    return one(high, op_high) + (one(high, op_low) + one(low, op_high))


def moves_of(chips):
    return [(h, d) for h in range(chips) for d in (0, 1)]


def partner(meta_ref, contexts, chips, move, ahead):
    place = meta_ref[contexts]
    chip, core = place // 2, place % 2
    hops = move[0] if ahead else chips - move[0]
    other = core if move[1] == 0 else 1 - core
    return ((chip + hops) % chips) * 2 + other


def lane_block(index, size=BLOCK):
    return pl.ds(pl.multiple_of(index * size, size), size)


def send_along(value, move):
    groups = lax.axis_size("ctx")
    places = lax.axis_size("seq")
    pairs = []
    for c in range(groups):
        for s in range(places):
            to_c, to_s = move(c, s)
            pairs.append((c * places + s, to_c * places + to_s))
    return lax.ppermute(value, AXES, pairs)


def to_sibling(value):
    return send_along(value, lambda c, s: (c, s ^ 1))


def to_x(value):
    return send_along(value, lambda c, s: (c ^ 1, s))


def to_y(value):
    return send_along(value, lambda c, s: (c ^ 2, s))


def to_partner(value, move):
    chips = lax.axis_size("seq") // 2
    return send_along(value, lambda c, s: (c, ((s // 2 + move[0]) % chips) * 2 + (s % 2 ^ move[1])))


def swap_blocks(blocks):
    moves = moves_of(len(blocks) // 2)
    chips = len(blocks) // 2
    order = sorted(range(len(moves)), key=lambda k: -min(moves[k][0], chips - moves[k][0]))
    got = {k: blocks[k] if k == 0 else to_partner(blocks[k], moves[k]) for k in order}
    return [got[k] for k in range(len(moves))]


def swap_parts(parts_array):
    return lax.all_to_all(parts_array, "seq", split_axis=0, concat_axis=0, tiled=True)


def part_spec(parts, step):
    return pl.BlockSpec((parts, step, BLOCK, BLOCK), lambda i, m: (0, i, 0, 0))


def block_specs(parts, step, first=0):
    return [pl.BlockSpec((step, BLOCK, BLOCK), lambda i, m: (first + i, 0, 0))] * parts


def block_shapes(parts, count):
    return [shape_of((count, BLOCK, BLOCK))] * parts


def hand_out(meta_ref, contexts, chips, rows_ref, outs):
    for move, out in zip(moves_of(chips), outs):
        where = lane_block(partner(meta_ref, contexts, chips, move, True))
        for c in range(out.shape[0]):
            out[c] = rows_ref[c * BLOCK : (c + 1) * BLOCK, where]


def norm_rows(rows):
    centre = rows - jnp.mean(rows, axis=-1, keepdims=True)
    scale = lax.rsqrt(jnp.mean(centre * centre, axis=-1, keepdims=True) + EPSILON)
    return centre * scale, scale


def mask_column(meta_ref, context, contexts):
    places = lax.broadcasted_iota(jnp.int32, (BLOCK, 1), 0) + meta_ref[contexts] * BLOCK
    return (places < meta_ref[context]).astype(F32)


def make_signal(meta, after, block_input, gain, shift, base, count):
    contexts, block_len, channels = block_input.shape
    parts = channels // BLOCK
    chips = parts // 2

    def body(meta_ref, x_ref, gain_ref, shift_ref, rows_ref, *outs):
        unit, _ = norm_rows(x_ref[0].astype(F32))
        mask = mask_column(meta_ref, pl.program_id(0) + base, contexts)
        rows_ref[...] = (unit * gain_ref[...] + shift_ref[...]) * mask
        hand_out(meta_ref, contexts, chips, rows_ref, outs)

    outs, token = launch(
        body,
        "signal",
        meta,
        after,
        [block_input, gain, shift],
        [
            pl.BlockSpec((1, block_len, channels), lambda i, m: (base + i, 0, 0)),
            whole((1, channels)),
            whole((1, channels)),
        ],
        [shape_of((count * block_len, channels))] + block_shapes(parts, count),
        [rows_spec(block_len, channels)] + block_specs(parts, 1),
        (count,),
        micros=5,
    )
    return outs[0], outs[1:], token


def mode_coefs(log_step, decay_log, turn_rate, read_real, read_imag):
    step_size = jnp.exp(log_step)[None, :]
    decay_rate = jnp.exp(decay_log)
    rate_step = -decay_rate * step_size
    turn_step = turn_rate * step_size
    growth = jnp.exp(rate_step)
    edge_real = growth * jnp.cos(turn_step) - 1.0
    edge_imag = growth * jnp.sin(turn_step)
    modulus = decay_rate * decay_rate + turn_rate * turn_rate
    ratio_real = (-edge_real * decay_rate + edge_imag * turn_rate) / modulus
    ratio_imag = (-edge_imag * decay_rate - edge_real * turn_rate) / modulus
    coef_real = read_real * ratio_real - read_imag * ratio_imag
    coef_imag = read_real * ratio_imag + read_imag * ratio_real
    return rate_step, turn_step, coef_real, coef_imag


def times(a, b):
    return a[0] * b[0] - a[1] * b[1], a[0] * b[1] + a[1] * b[0]


def low_table(rate_ref, turn_ref, low_real, low_imag):
    place = lax.broadcasted_iota(jnp.int32, (8, BLOCK), 0)
    size = jnp.exp(rate_ref[...])
    low_real[:, 0, :] = size * jnp.cos(turn_ref[...])
    low_imag[:, 0, :] = size * jnp.sin(turn_ref[...])

    def fill(mode, _):
        power = (low_real[mode, 0:1, :], low_imag[mode, 0:1, :])
        piece = (jnp.ones((8, BLOCK), F32), jnp.zeros((8, BLOCK), F32))
        for bit in range(3):
            chosen = ((place >> bit) & 1) == 1
            moved = times(piece, power)
            piece = (jnp.where(chosen, moved[0], piece[0]), jnp.where(chosen, moved[1], piece[1]))
            power = times(power, power)
        for block in range(STEP_LOW // 8):
            low_real[mode, block * 8 : (block + 1) * 8, :] = piece[0]
            low_imag[mode, block * 8 : (block + 1) * 8, :] = piece[1]
            piece = times(piece, power)
        return 0

    lax.fori_loop(0, rate_ref.shape[0], fill, 0)


def high_table(rate_ref, turn_ref, start_real, start_imag, high_real, high_imag):
    size = jnp.exp(rate_ref[...] * STEP_LOW)
    angle = turn_ref[...] * STEP_LOW
    move_real = size * jnp.cos(angle)
    move_imag = size * jnp.sin(angle)

    def fill(place, carry):
        now_real, now_imag = carry
        high_real[place] = now_real
        high_imag[place] = now_imag
        return (
            now_real * move_real - now_imag * move_imag,
            now_real * move_imag + now_imag * move_real,
        )

    lax.fori_loop(0, high_real.shape[0], fill, (start_real, start_imag))


def alternate_sign(rows):
    place = lax.broadcasted_iota(jnp.int32, (rows, 1), 0)
    return (1 - 2 * (place & 1)).astype(F32)


def spectrum_body(
    meta_ref,
    rate_ref,
    turn_ref,
    coef_real_ref,
    coef_imag_ref,
    ahead_high,
    ahead_low,
    out_ref,
    low_real,
    low_imag,
    high_real,
    high_imag,
    taps,
):
    modes = rate_ref.shape[0]
    parts = out_ref.shape[0]
    low_table(rate_ref, turn_ref, low_real, low_imag)
    high_table(rate_ref, turn_ref, coef_real_ref[...], coef_imag_ref[...], high_real, high_imag)
    tile = 8

    def per_tile(index, _):
        first = index * tile

        def per_mode(mode, sums):
            base_real = low_real[mode]
            base_imag = low_imag[mode]
            row = pl.ds(mode, 1)
            return tuple(
                sums[k]
                + (
                    high_real[first + k, row, :] * base_real
                    - high_imag[first + k, row, :] * base_imag
                )
                for k in range(tile)
            )

        zeros = jnp.zeros((STEP_LOW, BLOCK), F32)
        sums = lax.fori_loop(0, modes, per_mode, (zeros,) * tile)
        for k in range(tile):
            taps[pl.ds(pl.multiple_of((first + k) * STEP_LOW, STEP_LOW), STEP_LOW), :] = (
                2.0 * sums[k]
            )
        return 0

    lax.fori_loop(0, high_real.shape[0] // tile, per_tile, 0)
    wide = jnp.concatenate([taps[d * BLOCK : (d + 1) * BLOCK, :] for d in range(parts)], axis=1)
    plain = dot_parts(ahead_high[...], ahead_low[...], wide)
    sign = alternate_sign(BLOCK)
    for d in range(parts):
        here = plain[:, d * BLOCK : (d + 1) * BLOCK]
        real_part, imag_part = here[:BLOCK], here[BLOCK:]
        if d > 0:
            before = plain[:, (d - 1) * BLOCK : d * BLOCK]
            real_part = real_part - sign * before[BLOCK:]
            imag_part = imag_part + sign * before[:BLOCK]
        out_ref[d, :BLOCK, :] = real_part
        out_ref[d, BLOCK:, :] = imag_part


def mode_scratch(modes, high_count):
    return [
        pltpu.VMEM((modes, STEP_LOW, BLOCK), F32),
        pltpu.VMEM((modes, STEP_LOW, BLOCK), F32),
        pltpu.VMEM((high_count, modes, BLOCK), F32),
        pltpu.VMEM((high_count, modes, BLOCK), F32),
    ]


def make_spectrum(meta, after, coefs, tables, parts):
    modes = coefs[0].shape[0]
    high_count = parts * BLOCK // STEP_LOW
    outs, token = launch(
        spectrum_body,
        "taps_spectrum",
        meta,
        after,
        list(coefs) + [tables[0], tables[1]],
        [whole((modes, BLOCK))] * 4 + [whole((2 * BLOCK, BLOCK))] * 2,
        [shape_of((parts, 2 * BLOCK, BLOCK))],
        [whole((parts, 2 * BLOCK, BLOCK))],
        (1,),
        mode_scratch(modes, high_count) + [pltpu.VMEM((parts * BLOCK, BLOCK), F32)],
        micros=12,
    )
    return outs[0], token


def spectra_of(meta_ref, contexts, chips, tables, series, write):
    wide = jnp.concatenate([ref[0] for ref in series], axis=1)
    result = dot_parts(tables[0][...], tables[1][...], wide)
    for k, move in enumerate(moves_of(chips)):
        here = partner(meta_ref, contexts, chips, move, False)
        write(lane_block(here), result[:, k * BLOCK : (k + 1) * BLOCK])


def lanes(t):
    return pl.ds(t * BLOCK, BLOCK)


def convolve(meta, after, contexts, series, taps, tables, base, count):
    parts = len(series)
    chips = parts // 2
    wide = parts * BLOCK

    def body(meta_ref, *refs):
        blocks = refs[:parts]
        taps_ref = refs[parts]
        maps = refs[parts + 1 : parts + 5]
        outs = refs[parts + 5 : 2 * parts + 5]
        spec_ref, mixed, rows = refs[2 * parts + 5 :]

        def write(where, values):
            spec_ref[0, :, where] = values

        spectra_of(meta_ref, contexts, chips, maps[:2], blocks, write)

        def per_tile(index, _):
            real_rows = pl.ds(pl.multiple_of(index * 8, 8), 8)
            imag_rows = pl.ds(pl.multiple_of(BLOCK + index * 8, 8), 8)
            k_real = [taps_ref[d, real_rows, :] for d in range(parts)]
            k_imag = [taps_ref[d, imag_rows, :] for d in range(parts)]
            u_real = [spec_ref[0, real_rows, lanes(t)] for t in range(parts)]
            u_imag = [spec_ref[0, imag_rows, lanes(t)] for t in range(parts)]
            for s in range(parts):
                sum_real = jnp.zeros((8, BLOCK), F32)
                sum_imag = jnp.zeros((8, BLOCK), F32)
                for t in range(s + 1):
                    d = s - t
                    sum_real += k_real[d] * u_real[t] - k_imag[d] * u_imag[t]
                    sum_imag += k_real[d] * u_imag[t] + k_imag[d] * u_real[t]
                mixed[real_rows, lanes(s)] = sum_real
                mixed[imag_rows, lanes(s)] = sum_imag
            return 0

        lax.fori_loop(0, BLOCK // 8, per_tile, 0)
        rows[...] = dot_parts(maps[2][...], maps[3][...], mixed[...])
        hand_out(meta_ref, contexts, chips, rows, outs)

    outs, token = launch(
        body,
        "convolve",
        meta,
        after,
        list(series) + [taps] + list(tables),
        block_specs(parts, 1, base)
        + [whole((parts, 2 * BLOCK, BLOCK))]
        + [whole((2 * BLOCK, BLOCK))] * 2
        + [whole((BLOCK, 2 * BLOCK))] * 2,
        block_shapes(parts, count) + [shape_of((count, 2 * BLOCK, wide))],
        block_specs(parts, 1) + [pl.BlockSpec((1, 2 * BLOCK, wide), lambda i, m: (i, 0, 0))],
        (count,),
        [pltpu.VMEM((2 * BLOCK, wide), F32), pltpu.VMEM((BLOCK, wide), F32)],
        micros=7,
    )
    return outs[:parts], outs[parts], token


def convolve_back(meta, after, contexts, series, spectra, taps, tables):
    parts, count = series.shape[:2]
    wide = parts * BLOCK
    pieces = len(spectra)
    each = count // pieces

    def body(meta_ref, *refs):
        series_ref = refs[0]
        refs = refs[1:]
        spec_refs = refs[:pieces]
        refs = refs[pieces:]
        taps_ref = refs[0]
        maps = refs[1:5]
        out_ref, taps_grad_ref, grad_spec, mixed, pairs, spec_ref = refs[5:]
        step = pl.program_id(0)
        for k in range(pieces):

            @pl.when(step // each == k)
            def _(k=k):
                spec_ref[...] = spec_refs[k][...]

        @pl.when(step == 0)
        def _():
            pairs[...] = jnp.zeros_like(pairs)

        series_wide = jnp.concatenate([series_ref[t, 0] for t in range(parts)], axis=1)
        grad_spec[...] = dot_parts(maps[0][...], maps[1][...], series_wide)

        def per_tile(index, _):
            real_rows = pl.ds(pl.multiple_of(index * 8, 8), 8)
            imag_rows = pl.ds(pl.multiple_of(BLOCK + index * 8, 8), 8)
            k_real = [taps_ref[d, real_rows, :] for d in range(parts)]
            k_imag = [taps_ref[d, imag_rows, :] for d in range(parts)]
            g_real = [grad_spec[real_rows, lanes(t)] for t in range(parts)]
            g_imag = [grad_spec[imag_rows, lanes(t)] for t in range(parts)]
            for t in range(parts):
                sum_real = jnp.zeros((8, BLOCK), F32)
                sum_imag = jnp.zeros((8, BLOCK), F32)
                for s in range(t, parts):
                    d = s - t
                    sum_real += k_real[d] * g_real[s] + k_imag[d] * g_imag[s]
                    sum_imag += k_real[d] * g_imag[s] - k_imag[d] * g_real[s]
                mixed[real_rows, lanes(t)] = sum_real
                mixed[imag_rows, lanes(t)] = sum_imag
            u_real = [spec_ref[0, real_rows, lanes(t)] for t in range(parts)]
            u_imag = [spec_ref[0, imag_rows, lanes(t)] for t in range(parts)]
            for d in range(parts):
                sum_real = pairs[real_rows, lanes(d)]
                sum_imag = pairs[imag_rows, lanes(d)]
                for t in range(parts - d):
                    s = t + d
                    sum_real += u_real[t] * g_real[s] + u_imag[t] * g_imag[s]
                    sum_imag += u_real[t] * g_imag[s] - u_imag[t] * g_real[s]
                pairs[real_rows, lanes(d)] = sum_real
                pairs[imag_rows, lanes(d)] = sum_imag
            return 0

        lax.fori_loop(0, BLOCK // 8, per_tile, 0)
        rows = dot_parts(maps[2][...], maps[3][...], mixed[...])
        for t in range(parts):
            out_ref[t, 0] = rows[:, t * BLOCK : (t + 1) * BLOCK]

        @pl.when(step == count - 1)
        def _():
            sign = alternate_sign(BLOCK)
            for d in range(parts):
                real_part = pairs[:BLOCK, lanes(d)]
                imag_part = pairs[BLOCK:, lanes(d)]
                if d + 1 < parts:
                    real_part = real_part + sign * pairs[BLOCK:, lanes(d + 1)]
                    imag_part = imag_part - sign * pairs[:BLOCK, lanes(d + 1)]
                mixed[:BLOCK, lanes(d)] = real_part
                mixed[BLOCK:, lanes(d)] = imag_part
            taps_grad = dot_parts(maps[2][...], maps[3][...], mixed[...])
            for d in range(parts):
                taps_grad_ref[d] = taps_grad[:, d * BLOCK : (d + 1) * BLOCK]

    outs, token = launch(
        body,
        "convolve_back",
        meta,
        after,
        [series] + list(spectra) + [taps] + list(tables),
        [part_spec(parts, 1)]
        + [
            pl.BlockSpec(
                (1, 2 * BLOCK, wide),
                lambda i, m, k=k: (jnp.clip(i - k * each, 0, each - 1), 0, 0),
            )
            for k in range(pieces)
        ]
        + [whole((parts, 2 * BLOCK, BLOCK))]
        + [whole((2 * BLOCK, BLOCK))] * 2
        + [whole((BLOCK, 2 * BLOCK))] * 2,
        [shape_of((parts, count, BLOCK, BLOCK)), shape_of((parts, BLOCK, BLOCK))],
        [part_spec(parts, 1), whole((parts, BLOCK, BLOCK))],
        (count,),
        [pltpu.VMEM((2 * BLOCK, wide), F32)] * 3
        + [pltpu.VMEM((1, 2 * BLOCK, wide), F32)],
        micros=16,
    )
    return outs[0], outs[1], token


def moments_body(
    meta_ref, rate_ref, turn_ref, grad_ref, out_ref, low_real, low_imag, high_real, high_imag
):
    modes = rate_ref.shape[0]
    count = high_real.shape[0]
    low_table(rate_ref, turn_ref, low_real, low_imag)
    ones = jnp.ones(rate_ref.shape, F32)
    high_table(rate_ref, turn_ref, ones, jnp.zeros_like(ones), high_real, high_imag)
    places = lax.broadcasted_iota(jnp.int32, (STEP_LOW, 1), 0).astype(F32)
    tile = 8

    def per_mode(mode, _):
        row = pl.ds(mode, 1)
        zeros = jnp.zeros((STEP_LOW, BLOCK), F32)

        def per_tile(index, sums):
            plain_real, plain_imag, by_real, by_imag = sums
            for k in range(tile):
                place = index * tile + k
                rows = pl.ds(pl.multiple_of(place * STEP_LOW, STEP_LOW), STEP_LOW)
                grad = grad_ref[rows, :]
                term_real = high_real[place, row, :] * grad
                term_imag = high_imag[place, row, :] * grad
                plain_real += term_real
                plain_imag += term_imag
                weight = (place * STEP_LOW).astype(F32)
                by_real += term_real * weight
                by_imag += term_imag * weight
            return plain_real, plain_imag, by_real, by_imag

        plain_real, plain_imag, by_real, by_imag = lax.fori_loop(
            0, count // tile, per_tile, (zeros,) * 4
        )
        base_real = low_real[mode]
        base_imag = low_imag[mode]

        def total(rows_in):
            return jnp.sum(rows_in, axis=0, keepdims=True)

        first_real = by_real + places * plain_real
        first_imag = by_imag + places * plain_imag
        out_ref[0, row, :] = total(base_real * plain_real - base_imag * plain_imag)
        out_ref[1, row, :] = total(base_real * plain_imag + base_imag * plain_real)
        out_ref[2, row, :] = total(base_real * first_real - base_imag * first_imag)
        out_ref[3, row, :] = total(base_real * first_imag + base_imag * first_real)
        return 0

    lax.fori_loop(0, modes, per_mode, 0)


def make_moments(meta, after, rate, turn, taps_grad):
    modes = rate.shape[0]
    length = taps_grad.shape[0]
    outs, token = launch(
        moments_body,
        "moments",
        meta,
        after,
        [rate, turn, taps_grad],
        [whole((modes, BLOCK)), whole((modes, BLOCK)), whole((length, BLOCK))],
        [shape_of((4, modes, BLOCK))],
        [whole((4, modes, BLOCK))],
        (1,),
        mode_scratch(modes, length // STEP_LOW),
        micros=16,
    )
    return outs[0], token


GELU_SCALE = 0.7978845608
GELU_CUBE = 0.044715


def gelu(value):
    inner = GELU_SCALE * value * (1.0 + GELU_CUBE * (value * value))
    return value * (0.5 + 0.5 * jnp.tanh(inner))


def gelu_slope(value):
    square = value * value
    bend = jnp.tanh(GELU_SCALE * value * (1.0 + GELU_CUBE * square))
    rise = GELU_SCALE + (3.0 * GELU_SCALE * GELU_CUBE) * square
    return 0.5 + 0.5 * (bend + value * (1.0 - bend * bend) * rise)


def sigmoid(value):
    return 0.5 * (1.0 + jnp.tanh(0.5 * value))


def dot(left, right):
    return jnp.dot(left, right, preferred_element_type=F32)


def dot_nt(left, right):
    return lax.dot_general(left, right, (((1,), (1,)), ((), ())), preferred_element_type=F32)


def dot_tn(left, right):
    return lax.dot_general(left, right, (((0,), (0,)), ((), ())), preferred_element_type=F32)


def gather_parts(meta_ref, contexts, chips, blocks, rows_ref):
    count = blocks[0].shape[0]
    for move, ref in zip(moves_of(chips), blocks):
        where = lane_block(partner(meta_ref, contexts, chips, move, False))
        for c in range(count):
            rows_ref[c * BLOCK : (c + 1) * BLOCK, where] = ref[c]


def rows_spec(rows, columns, start=0):
    return pl.BlockSpec((rows, columns), lambda i, m: (start + i, 0))


class Copies:
    def __init__(self, semaphores):
        self.semaphores = semaphores
        self.running = []

    def start(self, source, target):
        copy = pltpu.make_async_copy(source, target, self.semaphores.at[len(self.running)])
        copy.start()
        self.running.append(copy)
        return copy


def in_hbm():
    return pl.BlockSpec(memory_space=pl.ANY)


def make_forward(
    meta,
    after,
    block_input,
    conv,
    signal,
    skip,
    glu,
    glu_bias,
    gain,
    shift,
    up,
    up_bias,
    base,
    step,
):
    contexts, block_len, channels = block_input.shape
    parts = len(conv)
    chips = parts // 2
    hidden_units = up.shape[1]
    wide = hidden_units // parts
    rows = step * BLOCK
    first = base // step
    gate_tile = 256

    half, half_wide = channels // 2, hidden_units // 2
    outs = [
        (half, BF16),
        (half, F32),
        (channels, F32),
        (channels, F32),
        (channels, F32),
        (channels, F32),
        (half, BF16),
        (half, F32),
        (half_wide, BF16),
        (half_wide, F32),
        (hidden_units, F32),
    ]
    copies_in_all = 2 + 8 + 3 * parts

    def body(meta_ref, x_ref, *refs):
        blocks = refs[:parts]
        refs = refs[parts:]
        signal_ref, skip_ref, glu_hbm, glu_bias_ref, gain_ref, shift_ref, up_hbm, up_bias_ref = (
            refs[:8]
        )
        targets = refs[8 : 8 + len(outs)]
        held = refs[8 + len(outs) : 8 + 2 * len(outs)]
        glu_ref, up_ref, rows_scr, semaphores = refs[8 + 2 * len(outs) :]
        (
            act_own,
            act_send,
            mixed_ref,
            gate_a_ref,
            gate_sig_ref,
            hidden_ref,
            second_own,
            second_send,
            wide_own,
            wide_send,
            inner_ref,
        ) = held
        copies = Copies(semaphores)
        glu_copy = copies.start(glu_hbm, glu_ref)
        up_copy = copies.start(up_hbm, up_ref)
        leaving = []

        def leave(*which):
            for k in which:
                leaving.append(copies.start(held[k], targets[k]))

        def share(own_ref, send_ref):
            for h in range(chips):
                here = lane_block(partner(meta_ref, contexts, chips, (h, 0), True))
                there = lane_block(partner(meta_ref, contexts, chips, (h, 1), True))
                own_ref[:, lanes(h)] = rows_scr[:, here].astype(BF16)
                send_ref[:, lanes(h)] = rows_scr[:, there].astype(BF16).astype(F32)

        gather_parts(meta_ref, contexts, chips, blocks, rows_scr)
        mixed = rows_scr[...] + skip_ref[...] * signal_ref[...]
        mixed_ref[...] = mixed
        activated = gelu(mixed)
        rows_scr[...] = activated
        share(act_own, act_send)
        leave(0, 1, 2)
        activated = activated.astype(BF16)
        x = x_ref[...].reshape(rows, channels)
        glu_copy.wait()
        for k in range(channels // gate_tile):
            cols = slice(k * gate_tile, (k + 1) * gate_tile)
            late = slice(channels + k * gate_tile, channels + (k + 1) * gate_tile)
            gate_a = dot(activated, glu_ref[:, cols]) + glu_bias_ref[:, cols]
            gate_sig = sigmoid(dot(activated, glu_ref[:, late]) + glu_bias_ref[:, late])
            gate_a_ref[:, cols] = gate_a
            gate_sig_ref[:, cols] = gate_sig
            hidden_ref[:, cols] = x[:, cols].astype(F32) + gate_a * gate_sig
        leave(3, 4, 5)
        unit, _ = norm_rows(hidden_ref[...])
        second = unit * gain_ref[...] + shift_ref[...]
        rows_scr[...] = second
        share(second_own, second_send)
        leave(6, 7)
        second = second.astype(BF16)
        up_copy.wait()
        for d in (1, 0):
            for h in range(chips):
                slot = slice(h * wide, (h + 1) * wide)
                cols = lane_block(partner(meta_ref, contexts, chips, (h, d), True), wide)
                inner = dot(second, up_ref[:, cols]) + up_bias_ref[:, cols]
                inner_ref[:, cols] = inner
                widened = gelu(inner).astype(BF16)
                leaving.append(copies.start(inner_ref.at[:, cols], targets[10].at[:, cols]))
                if d == 0:
                    wide_own[:, slot] = widened
                    leaving.append(copies.start(wide_own.at[:, slot], targets[8].at[:, slot]))
                else:
                    wide_send[:, slot] = widened.astype(F32)
                    leaving.append(copies.start(wide_send.at[:, slot], targets[9].at[:, slot]))
        for copy in leaving:
            copy.wait()

    results, token = launch(
        body,
        "forward_rows",
        meta,
        after,
        [block_input]
        + list(conv)
        + [signal, skip, glu, glu_bias, gain, shift, up, up_bias],
        [pl.BlockSpec((step, block_len, channels), lambda i, m: (first + i, 0, 0))]
        + block_specs(parts, step)
        + [
            rows_spec(rows, channels, first),
            whole_once((1, channels)),
            in_hbm(),
            whole_once((1, 2 * channels)),
            whole_once((1, channels)),
            whole_once((1, channels)),
            in_hbm(),
            whole_once((1, hidden_units)),
        ],
        [shape_of((rows, columns), kind) for columns, kind in outs],
        [in_hbm()] * len(outs),
        (1,),
        [pltpu.VMEM((rows, columns), kind) for columns, kind in outs]
        + [
            pltpu.VMEM((channels, 2 * channels), BF16),
            pltpu.VMEM((channels, hidden_units), BF16),
            pltpu.VMEM((rows, channels), F32),
            pltpu.SemaphoreType.DMA((copies_in_all,)),
        ],
        micros=16,
    )
    return results, token


def make_output(meta, after, contexts, hidden, wide_own, wide_send, down, bias, base, step):
    all_rows, channels = hidden.shape
    hidden_units = down.shape[0]
    rows = step * BLOCK
    parts = channels // BLOCK
    chips = parts // 2
    wide = hidden_units // parts

    def body(meta_ref, hidden_ref, own_ref, send_ref, down_ref, bias_ref, out_ref):
        total = hidden_ref[...] + bias_ref[...]
        for h in range(chips):
            slot = slice(h * wide, (h + 1) * wide)
            here = lane_block(partner(meta_ref, contexts, chips, (h, 0), True), wide)
            there = lane_block(partner(meta_ref, contexts, chips, (h, 1), True), wide)
            total += dot(own_ref[:, slot], down_ref[here, :])
            total += dot(send_ref[:, slot].astype(BF16), down_ref[there, :])
        first = base + pl.program_id(0) * step
        for c in range(step):
            mask = mask_column(meta_ref, first + c, contexts)
            out_ref[c] = (total[c * BLOCK : (c + 1) * BLOCK] * mask).astype(BF16)

    outs, token = launch(
        body,
        "output_rows",
        meta,
        after,
        [hidden, wide_own, wide_send, down, bias],
        [
            rows_spec(rows, channels),
            rows_spec(rows, hidden_units // 2),
            rows_spec(rows, hidden_units // 2),
            whole_once((hidden_units, channels)),
            whole_once((1, channels)),
        ],
        [shape_of((all_rows // BLOCK, BLOCK, channels), BF16)],
        [pl.BlockSpec((step, BLOCK, channels), lambda i, m: (i, 0, 0))],
        (all_rows // rows,),
        micros=8,
    )
    return outs[0], token


def mask_rows(meta, after, out_grad):
    contexts, block_len, channels = out_grad.shape

    def body(meta_ref, grad_ref, out_ref, sum_ref):
        context = pl.program_id(0)
        rows = grad_ref[0].astype(F32) * mask_column(meta_ref, context, contexts)
        out_ref[...] = rows

        @pl.when(context == 0)
        def _():
            sum_ref[...] = jnp.zeros_like(sum_ref)

        sum_ref[...] += jnp.sum(rows, axis=0, keepdims=True)

    outs, token = launch(
        body,
        "mask_rows",
        meta,
        after,
        [out_grad],
        [pl.BlockSpec((1, block_len, channels), lambda i, m: (i, 0, 0))],
        [shape_of((contexts * block_len, channels)), shape_of((1, channels))],
        [rows_spec(block_len, channels), whole((1, channels))],
        (contexts,),
        micros=4,
    )
    return outs[0], outs[1], token


def make_backward(
    meta,
    after,
    contexts,
    grad_out,
    ahead,
    gain,
    down,
    up,
    glu,
    step,
):
    pieces = len(ahead)
    all_rows, channels = grad_out.shape
    each = all_rows // (pieces * step * BLOCK)
    hidden_units = up.shape[1]
    rows = step * BLOCK
    parts = channels // BLOCK
    chips = parts // 2
    tile = 512

    def body(
        meta_ref,
        grad_ref,
        *refs,
    ):
        gain_ref, down_ref, up_ref, glu_ref = refs[5 * pieces : 5 * pieces + 4]
        inner_out, gates_out, hidden_grad_ref, mixed_rows = refs[5 * pieces + 4 : 5 * pieces + 8]
        more = refs[5 * pieces + 8 :]
        for k in range(pieces):

            @pl.when(pl.program_id(0) // each == k)
            def _(k=k):
                one_piece(
                    grad_ref,
                    *refs[5 * k : 5 * k + 5],
                    gain_ref,
                    down_ref,
                    up_ref,
                    glu_ref,
                    inner_out,
                    gates_out,
                    hidden_grad_ref,
                    mixed_rows,
                    *more,
                    meta_ref=meta_ref,
                )

    def one_piece(
        grad_ref,
        wide_inner,
        hidden_ref,
        gate_a_ref,
        gate_sig_ref,
        mixed_in,
        gain_ref,
        down_ref,
        up_ref,
        glu_ref,
        inner_out,
        gates_out,
        hidden_grad_ref,
        mixed_rows,
        *more,
        meta_ref,
    ):
        mixed_out, inner_sum, gates_sum, gain_sum, shift_sum = more

        @pl.when(pl.program_id(0) == 0)
        def _():
            inner_sum[...] = jnp.zeros_like(inner_sum)
            gates_sum[...] = jnp.zeros_like(gates_sum)
            gain_sum[...] = jnp.zeros_like(gain_sum)
            shift_sum[...] = jnp.zeros_like(shift_sum)

        def add_rows(ref, cols, values):
            ref[:, cols] += jnp.sum(values, axis=0, keepdims=True)

        grad_out = grad_ref[...]
        grad_low = grad_out.astype(BF16)
        grad_second = jnp.zeros(grad_out.shape, F32)
        for k in range(hidden_units // tile):
            cols = slice(k * tile, (k + 1) * tile)
            grad_wide = dot_nt(grad_low, down_ref[cols, :])
            inner = (grad_wide * gelu_slope(wide_inner[:, cols])).astype(BF16)
            inner_full = inner.astype(F32)
            inner_out[:, cols] = inner_full
            add_rows(inner_sum, cols, inner_full)
            grad_second += dot_nt(inner, up_ref[:, cols])
        unit, scale = norm_rows(hidden_ref[...])
        every = slice(0, channels)
        add_rows(gain_sum, every, grad_second * unit)
        add_rows(shift_sum, every, grad_second)
        scaled = grad_second * gain_ref[...]
        grad_hidden = grad_out + scale * (
            scaled
            - jnp.mean(scaled, axis=-1, keepdims=True)
            - unit * jnp.mean(scaled * unit, axis=-1, keepdims=True)
        )
        hidden_grad_ref[...] = grad_hidden
        gate_sig = gate_sig_ref[...]
        gate_grad = grad_hidden * gate_sig
        early = gate_grad.astype(BF16)
        later = (gate_grad * gate_a_ref[...] * (1.0 - gate_sig)).astype(BF16)
        grad_act = dot_nt(early, glu_ref[:, :channels]) + dot_nt(later, glu_ref[:, channels:])
        second_half = slice(channels, 2 * channels)
        for values, cols in ((early.astype(F32), every), (later.astype(F32), second_half)):
            gates_out[:, cols] = values
            add_rows(gates_sum, cols, values)
        mixed_rows[...] = grad_act * gelu_slope(mixed_in[...])
        for p in range(parts):
            for c in range(step):
                mixed_out[p, c] = mixed_rows[c * BLOCK : (c + 1) * BLOCK, lanes(p)]

    sums = [hidden_units, 2 * channels, channels, channels]
    results, token = launch(
        body,
        "backward_rows",
        meta,
        after,
        [grad_out] + [array for piece in ahead for array in piece] + [gain, down, up, glu],
        [rows_spec(rows, channels)]
        + [
            pl.BlockSpec(
                (rows, array.shape[1]),
                lambda i, m, k=k: (jnp.clip(i - k * each, 0, each - 1), 0),
                pipeline_mode=pl.Buffered(1) if each == 1 else None,
            )
            for k, piece in enumerate(ahead)
            for array in piece
        ]
        + [
            whole_once((1, channels)),
            whole_once((hidden_units, channels)),
            whole_once((channels, hidden_units)),
            whole_once((channels, 2 * channels)),
        ],
        [
            shape_of((all_rows, hidden_units)),
            shape_of((all_rows, 2 * channels)),
            shape_of((all_rows, channels)),
            shape_of((all_rows, channels)),
        ]
        + [shape_of((parts, all_rows // BLOCK, BLOCK, BLOCK))]
        + [shape_of((1, columns)) for columns in sums],
        [
            rows_spec(rows, hidden_units),
            rows_spec(rows, 2 * channels),
            rows_spec(rows, channels),
            rows_spec(rows, channels),
        ]
        + [part_spec(parts, step)]
        + [whole((1, columns)) for columns in sums],
        (all_rows // rows,),
        micros=30,
    )
    return {
        "inner": results[0],
        "gates": results[1],
        "hidden": results[2],
        "mixed": results[3],
        "blocks": results[4],
        "sums": results[5:],
    }, token


def weight_grad(meta, after, name, pairs, groups, chips, row_tiles, col_tiles, micros):
    rows = pairs[0][0].shape[1]
    cols = pairs[0][1].shape[1]
    row_block = rows // row_tiles
    col_block = cols // col_tiles
    chip_block = chips // row_tiles
    each = rows // (chips * groups)

    def body(meta_ref, *refs):
        out_ref = refs[-1]
        total = None
        for k in range(len(pairs)):
            left, right = refs[2 * k], refs[2 * k + 1]
            term = dot_tn(left[...].astype(BF16), right[...].astype(BF16))
            total = term if total is None else total + term
        for h in range(chip_block):
            for q in range(groups):
                start = (h * groups + q) * each
                out_ref[q, h * each : (h + 1) * each, :] = total[start : start + each]

    in_specs = []
    operands = []
    nbytes = rows * cols * 4
    tokens_all = 0
    for left, right, start, tokens in pairs:
        in_specs.append(pl.BlockSpec((tokens, row_block), lambda i, j, m: (0, i)))
        in_specs.append(pl.BlockSpec((tokens, col_block), lambda i, j, m, s=start: (s, j)))
        operands += [left, right]
        tokens_all += tokens
        nbytes += tokens * (rows + cols) * 4
    outs, token = launch(
        body,
        name,
        meta,
        after,
        operands,
        in_specs,
        [shape_of((groups, chips * each, cols))],
        [pl.BlockSpec((groups, chip_block * each, col_block), lambda i, j, m: (0, i, j))],
        (row_tiles, col_tiles),
        micros=micros,
    )
    return outs[0], token


def make_input_grad(
    meta,
    after,
    block_input,
    conv_grad,
    mixed_grad,
    signal,
    hidden_grad,
    skip,
    gain,
    base,
):
    contexts, block_len, channels = block_input.shape
    parts, count = conv_grad.shape[:2]

    def body(meta_ref, x_ref, *refs):
        (
            conv_ref,
            mixed_ref,
            signal_ref,
            hidden_grad_ref,
            skip_ref,
            gain_ref,
            out_ref,
            skip_sum,
            gain_sum,
            shift_sum,
        ) = refs

        @pl.when(pl.program_id(0) == 0)
        def _():
            skip_sum[...] = jnp.zeros_like(skip_sum)
            gain_sum[...] = jnp.zeros_like(gain_sum)
            shift_sum[...] = jnp.zeros_like(shift_sum)

        mask = mask_column(meta_ref, pl.program_id(0) + base, contexts)
        conv_rows = jnp.concatenate([conv_ref[p, 0] for p in range(parts)], axis=1)
        mixed = mixed_ref[...]
        skip_sum[...] += jnp.sum(mixed * signal_ref[...], axis=0, keepdims=True)
        grad_normed = (conv_rows + skip_ref[...] * mixed) * mask
        unit, scale = norm_rows(x_ref[0].astype(F32))
        gain_sum[...] += jnp.sum(grad_normed * unit, axis=0, keepdims=True)
        shift_sum[...] += jnp.sum(grad_normed, axis=0, keepdims=True)
        scaled = grad_normed * gain_ref[...]
        grad = hidden_grad_ref[...] + scale * (
            scaled
            - jnp.mean(scaled, axis=-1, keepdims=True)
            - unit * jnp.mean(scaled * unit, axis=-1, keepdims=True)
        )
        out_ref[0] = grad.astype(BF16)

    outs, token = launch(
        body,
        "input_grad",
        meta,
        after,
        [block_input, conv_grad, mixed_grad, signal, hidden_grad, skip, gain],
        [pl.BlockSpec((1, block_len, channels), lambda i, m: (base + i, 0, 0))]
        + [part_spec(parts, 1)]
        + [rows_spec(block_len, channels)] * 3
        + [whole((1, channels))] * 2,
        [shape_of((count, block_len, channels), BF16)] + [shape_of((1, channels))] * 3,
        [pl.BlockSpec((1, block_len, channels), lambda i, m: (i, 0, 0))]
        + [whole((1, channels))] * 3,
        (count,),
        micros=7,
    )
    return outs, token


def scatter_groups(part, chips):
    flat = part.reshape(-1, part.shape[-1])
    mine = lax.psum_scatter(flat, "ctx", scatter_dimension=0, tiled=True)
    return mine.reshape(chips, -1, mine.shape[-1])


def scatter_chips(meta, after, part):
    chips, rows, cols = part.shape
    others = [to_partner(part[hops], (hops, 0)) for hops in range(1, chips)]

    def body(meta_ref, mine_ref, *refs):
        total = mine_ref[0]
        for ref in refs[:-1]:
            total = total + ref[...]
        refs[-1][...] = total

    outs, token = launch(
        body,
        "add_chips",
        meta,
        after,
        [part] + others,
        [pl.BlockSpec((1, rows, cols), lambda i, m: (0, 0, 0))] + [whole((rows, cols))] * (chips - 1),
        [shape_of((rows, cols))],
        [whole((rows, cols))],
        (1,),
        micros=3,
    )
    return outs[0], token


def gather_groups(meta, after, mine):
    rows, cols = mine.shape
    from_x, from_y = to_x(mine), to_y(mine)
    from_both = send_along(mine, lambda c, s: (c ^ 3, s))
    group_place = meta.shape[0] - 1

    def body(meta_ref, *refs):
        out_ref = refs[-1]
        for k in range(4):

            @pl.when(pl.program_id(0) == k)
            def _(k=k):
                out_ref[...] = refs[k][...]

    outs, token = launch(
        body,
        "gather_groups",
        meta,
        after,
        [mine, from_x, from_y, from_both],
        [whole((rows, cols))] * 4,
        [shape_of((4 * rows, cols))],
        [pl.BlockSpec((rows, cols), lambda i, m: (m[group_place] ^ i, 0))],
        (4,),
        micros=4,
    )
    return outs[0], token


def sum_everywhere(value):
    value = value + to_sibling(value)
    value = value + to_x(value)
    value = value + to_y(value)
    value = value + send_along(value, lambda c, s: (c, s ^ 2))
    return value + send_along(value, lambda c, s: (c, s ^ 4))


PIECE = 2


def local_fast(
    block_input,
    valid_len,
    out_grad,
    first_gain,
    first_shift,
    log_step,
    decay_log,
    turn_rate,
    read_real,
    read_imag,
    skip_gain,
    glu_weight,
    glu_bias,
    second_gain,
    second_shift,
    up_weight,
    up_bias,
    down_weight,
    down_bias,
):
    parts = lax.axis_size("seq")
    groups = lax.axis_size("ctx")
    chips = parts // 2
    seq_index = lax.axis_index("seq")
    ctx_index = lax.axis_index("ctx")
    contexts, block_len, channels = block_input.shape
    places = jnp.stack([seq_index, ctx_index]).astype(jnp.int32)
    meta = jnp.concatenate([valid_len, places])

    def row(vector):
        return vector.reshape(1, -1)

    tables = odd_tables()
    bases = list(range(0, contexts, PIECE))
    token = first_gain.reshape(8, BLOCK)

    signal, blocks, token = make_signal(
        meta, token, block_input, row(first_gain), row(first_shift), 0, contexts
    )
    received = swap_blocks(blocks)
    first_channel = seq_index * BLOCK
    own_params = (lax.dynamic_slice_in_dim(log_step, first_channel, BLOCK, 0),) + tuple(
        lax.dynamic_slice_in_dim(tensor.T, first_channel, BLOCK, 1)
        for tensor in (decay_log, turn_rate, read_real, read_imag)
    )
    coefs, coefs_back = jax.vjp(mode_coefs, *own_params)
    taps, token = make_spectrum(meta, token, coefs, tables, parts)
    grad_out, down_bias_part, token = mask_rows(meta, token, out_grad)
    grad_out_got = to_sibling(grad_out)
    convs = []
    spectra = []
    for base in bases:
        blocks, spectrum, token = convolve(
            meta, token, contexts, received, taps, tables, base, PIECE
        )
        convs.append(swap_blocks(blocks))
        spectra.append(spectrum)
    ahead = []
    for base, conv in zip(bases, convs):
        piece, token = make_forward(
            meta,
            token,
            block_input,
            conv,
            signal,
            row(skip_gain),
            glu_weight,
            row(glu_bias),
            row(second_gain),
            row(second_shift),
            up_weight,
            row(up_bias),
            base,
            PIECE,
        )
        ahead.append(piece)
    rows_each = PIECE * BLOCK

    pairs = []
    for k, piece in enumerate(ahead):
        pairs.append((piece[8], grad_out, k, rows_each))
        pairs.append((to_sibling(piece[9]), grad_out_got, k, rows_each))
    act_got = [to_sibling(piece[1]) for piece in ahead]
    second_got = [to_sibling(piece[7]) for piece in ahead]
    token = [token] + act_got + second_got
    down_part, token = weight_grad(meta, token, "down_grad", pairs, groups, chips, chips, 1, 11)
    down_mine = scatter_groups(down_part, chips)

    back, token = make_backward(
        meta,
        token,
        contexts,
        grad_out,
        [(piece[10], piece[5], piece[3], piece[4], piece[2]) for piece in ahead],
        row(second_gain),
        down_weight,
        up_weight,
        glu_weight,
        PIECE,
    )
    moved = swap_parts(back["blocks"])
    inner_got = to_sibling(back["inner"])
    gates_got = to_sibling(back["gates"])
    outputs = []

    def output_of(k, token):
        piece = ahead[k]
        output, token = make_output(
            meta,
            token,
            contexts,
            piece[5],
            piece[8],
            piece[9],
            down_weight,
            row(down_bias),
            bases[k],
            PIECE,
        )
        outputs.append(output)
        return token

    token = output_of(0, token)
    pairs = []
    for k, piece in enumerate(ahead):
        pairs.append((piece[6], back["inner"], k, rows_each))
        pairs.append((second_got[k], inner_got, k, rows_each))
    up_part, token = weight_grad(meta, token, "up_grad", pairs, groups, chips, 1, 4, 12)
    up_mine = scatter_groups(up_part, chips)
    pairs = []
    for k, piece in enumerate(ahead):
        pairs.append((piece[0], back["gates"], k, rows_each))
        pairs.append((act_got[k], gates_got, k, rows_each))
    glu_part, token = weight_grad(meta, token, "glu_grad", pairs, groups, chips, 1, 2, 8)
    glu_mine = scatter_groups(glu_part, chips)
    blocks, taps_grad, token = convolve_back(
        meta, token, contexts, moved, spectra, taps, tables
    )
    conv_grad = swap_parts(blocks)
    down_sum_mine, token = scatter_chips(meta, token, down_mine)
    moments, token = make_moments(
        meta, token, coefs[0], coefs[1], taps_grad.reshape(parts * BLOCK, BLOCK)
    )
    for k in range(1, len(bases)):
        token = output_of(k, token)
    down_total, token = gather_groups(meta, token, down_sum_mine)
    zero_real, zero_imag, one_real, one_imag = (moments[k] for k in range(4))
    coef_real, coef_imag = coefs[2], coefs[3]
    own_grads = coefs_back(
        (
            2.0 * (coef_real * one_real - coef_imag * one_imag),
            -2.0 * (coef_real * one_imag + coef_imag * one_real),
            2.0 * zero_real,
            -2.0 * zero_imag,
        )
    )
    own_rows = jnp.concatenate([own_grads[0][None, :]] + list(own_grads[1:]), axis=0)
    pad = -own_rows.shape[0] % 8
    own_rows = jnp.pad(own_rows, ((0, pad), (0, 0)))
    own_rows = own_rows + to_x(own_rows)
    own_rows = own_rows + to_y(own_rows)
    every_row = lax.all_gather(own_rows, "seq", axis=1, tiled=True)
    modes = decay_log.shape[1]
    mode_grads = [every_row[1 + k * modes : 1 + (k + 1) * modes].T for k in range(4)]

    last, token = make_input_grad(
        meta,
        token,
        block_input,
        conv_grad,
        back["mixed"],
        signal,
        back["hidden"],
        row(skip_gain),
        row(first_gain),
        0,
    )
    up_sum_mine, token = scatter_chips(meta, token, up_mine)
    up_total, token = gather_groups(meta, token, up_sum_mine)
    glu_sum_mine, token = scatter_chips(meta, token, glu_mine)
    glu_total, token = gather_groups(meta, token, glu_sum_mine)

    vectors = [last[2], last[3], last[1]] + [back["sums"][k] for k in (1, 2, 3, 0)]
    vectors.append(down_bias_part)
    flat = jnp.concatenate([vector.reshape(-1, BLOCK) for vector in vectors], axis=0)
    flat = sum_everywhere(flat)
    sums = []
    start = 0
    for vector in vectors:
        size = vector.size // BLOCK
        sums.append(flat[start : start + size].reshape(-1))
        start += size
    gain_sum, shift_sum, skip_sum, glu_bias_sum, gain2_sum, shift2_sum, up_sum, down_sum = sums
    return (
        jnp.concatenate(outputs, axis=0),
        last[0],
        gain_sum,
        shift_sum,
        every_row[0],
        mode_grads[0],
        mode_grads[1],
        mode_grads[2],
        mode_grads[3],
        skip_sum,
        glu_total,
        glu_bias_sum,
        gain2_sum,
        shift2_sum,
        up_total,
        up_sum,
        down_total,
        down_sum,
    )


def local_any(
    block_input,
    valid_len,
    out_grad,
    first_gain,
    first_shift,
    log_step,
    decay_log,
    turn_rate,
    read_real,
    read_imag,
    skip_gain,
    glu_weight,
    glu_bias,
    second_gain,
    second_shift,
    up_weight,
    up_bias,
    down_weight,
    down_bias,
):
    seq_parts = lax.axis_size("seq")
    seq_index = lax.axis_index("seq")
    contexts, block_len, channels = block_input.shape
    total_len = seq_parts * block_len
    row_count = contexts * block_len
    positions = seq_index * block_len + jnp.arange(block_len)
    valid_mask = (positions[None, :] < valid_len[:, None]).astype(jnp.float32)[:, :, None]
    flat_mask = valid_mask.reshape(row_count, 1)
    ssm_params = (log_step, decay_log, turn_rate, read_real, read_imag)
    inputs = block_input.astype(jnp.float32)
    normed_first, unit_first, scale_first = layer_norm(inputs, first_gain, first_shift)
    signal = normed_first * valid_mask
    chan_count = channels // seq_parts
    chan_params = jax.tree.map(
        lambda tensor: lax.dynamic_slice_in_dim(tensor, seq_index * chan_count, chan_count, 0),
        ssm_params,
    )
    all_float = jnp.arange(total_len).astype(jnp.float32)
    kernel_part = kernel_block(chan_params, all_float)
    sig_real, sig_imag = channel_spectrum(signal)
    ker_real, ker_imag = local_spectrum(kernel_part.reshape(1, seq_parts, block_len, chan_count))
    prod_real, prod_imag = times_kernel(sig_real, sig_imag, ker_real, ker_imag)
    conv_out = token_blocks(local_time(prod_real, prod_imag))
    mixed_seq = conv_out + skip_gain * signal
    activated_full, act_back = jax.vjp(gelu_tanh, mixed_seq)
    activated = activated_full.astype(jnp.bfloat16).reshape(row_count, channels)
    gate_rows = jnp.dot(activated, glu_weight, preferred_element_type=jnp.float32) + glu_bias
    gate_a = gate_rows[:, :channels]
    gate_sig = jax.nn.sigmoid(gate_rows[:, channels:])
    hidden = inputs.reshape(row_count, channels) + gate_a * gate_sig
    normed_second, unit_second, scale_second = layer_norm(hidden, second_gain, second_shift)
    second = normed_second.astype(jnp.bfloat16)
    inner_rows = jnp.dot(second, up_weight, preferred_element_type=jnp.float32) + up_bias
    widened_full, wide_back = jax.vjp(gelu_tanh, inner_rows)
    widened = widened_full.astype(jnp.bfloat16)
    result = hidden + jnp.dot(widened, down_weight, preferred_element_type=jnp.float32) + down_bias
    block_output = (result * flat_mask).astype(jnp.bfloat16).reshape(contexts, block_len, channels)
    grad_out = out_grad.reshape(row_count, channels) * flat_mask.astype(jnp.bfloat16)
    grad_out_f = grad_out.astype(jnp.float32)
    down_bias_grad = jnp.sum(grad_out_f, axis=0)
    down_grad = jnp.einsum("rf,rd->fd", widened, grad_out, preferred_element_type=jnp.float32)
    grad_wide = jnp.einsum("rd,fd->rf", grad_out, down_weight, preferred_element_type=jnp.float32)
    grad_inner = wide_back(grad_wide)[0].astype(jnp.bfloat16)
    up_bias_grad = jnp.sum(grad_inner.astype(jnp.float32), axis=0)
    up_grad = jnp.einsum("rd,rf->df", second, grad_inner, preferred_element_type=jnp.float32)
    grad_second = jnp.einsum("rf,df->rd", grad_inner, up_weight, preferred_element_type=jnp.float32)
    second_gain_grad = jnp.sum(grad_second * unit_second, axis=0)
    second_shift_grad = jnp.sum(grad_second, axis=0)
    grad_hidden = grad_out_f + norm_back(grad_second, unit_second, scale_second, second_gain)
    grad_first_half = grad_hidden * gate_sig
    grad_second_half = grad_hidden * gate_a * gate_sig * (1.0 - gate_sig)
    grad_gates = jnp.concatenate([grad_first_half, grad_second_half], axis=1).astype(jnp.bfloat16)
    glu_bias_grad = jnp.sum(grad_gates.astype(jnp.float32), axis=0)
    glu_grad = jnp.einsum("rd,re->de", activated, grad_gates, preferred_element_type=jnp.float32)
    grad_act = jnp.einsum("re,de->rd", grad_gates, glu_weight, preferred_element_type=jnp.float32)
    grad_mixed = act_back(grad_act.reshape(contexts, block_len, channels))[0]
    skip_gain_grad = jnp.sum(grad_mixed * signal, axis=(0, 1))
    grad_real, grad_imag = channel_spectrum(grad_mixed)
    back_real, back_imag = conj_products(
        sig_real, sig_imag, ker_real, ker_imag, grad_real, grad_imag
    )
    returned = local_time(back_real, back_imag)
    grad_conv = token_blocks(returned[:contexts])
    local_grads = kernel_grads(
        chan_params, all_float, returned[contexts].reshape(total_len, chan_count)
    )
    ssm_grads = jax.tree.map(
        lambda whole_grad, piece_grad: lax.dynamic_update_slice_in_dim(
            jnp.zeros_like(whole_grad), piece_grad, seq_index * chan_count, 0
        ),
        ssm_params,
        local_grads,
    )
    grad_signal = grad_conv + skip_gain * grad_mixed
    grad_normed = grad_signal * valid_mask
    first_gain_grad = jnp.sum(grad_normed * unit_first, axis=(0, 1))
    first_shift_grad = jnp.sum(grad_normed, axis=(0, 1))
    input_grad = (
        grad_hidden.reshape(contexts, block_len, channels)
        + norm_back(grad_normed, unit_first, scale_first, first_gain)
    ).astype(jnp.bfloat16)
    step_grad, decay_grad, turn_grad, real_grad, imag_grad = ssm_grads
    (
        first_gain_sum,
        first_shift_sum,
        step_sum,
        decay_sum,
        turn_sum,
        real_sum,
        imag_sum,
        skip_sum,
        glu_bias_sum,
        second_gain_sum,
        second_shift_sum,
        up_bias_sum,
        down_bias_sum,
    ) = lax.psum(
        (
            first_gain_grad,
            first_shift_grad,
            step_grad,
            decay_grad,
            turn_grad,
            real_grad,
            imag_grad,
            skip_gain_grad,
            glu_bias_grad,
            second_gain_grad,
            second_shift_grad,
            up_bias_grad,
            down_bias_grad,
        ),
        ("ctx", "seq"),
    )
    rows_glu, rows_up, rows_down = (
        lax.psum_scatter(glu_grad, "seq", scatter_dimension=0, tiled=True),
        lax.psum_scatter(up_grad, "seq", scatter_dimension=0, tiled=True),
        lax.psum_scatter(down_grad, "seq", scatter_dimension=0, tiled=True),
    )
    glu_total, up_total, down_total = lax.psum((rows_glu, rows_up, rows_down), "ctx")
    return (
        block_output,
        input_grad,
        first_gain_sum,
        first_shift_sum,
        step_sum,
        decay_sum,
        turn_sum,
        real_sum,
        imag_sum,
        skip_sum,
        glu_total,
        glu_bias_sum,
        second_gain_sum,
        second_shift_sum,
        up_total,
        up_bias_sum,
        down_total,
        down_bias_sum,
    )


def solution(mesh):
    in_specs = (
        P("ctx", "seq", None),
        P("ctx"),
        P("ctx", "seq", None),
        P(),
        P(),
        P(),
        P(),
        P(),
        P(),
        P(),
        P(),
        P(),
        P(),
        P(),
        P(),
        P(),
        P(),
        P(),
        P(),
    )
    out_specs = (
        P("ctx", "seq", None),
        P("ctx", "seq", None),
        P(),
        P(),
        P(),
        P(),
        P(),
        P(),
        P(),
        P(),
        P("seq", None),
        P(),
        P(),
        P(),
        P("seq", None),
        P(),
        P("seq", None),
        P(),
    )
    grid_size = (mesh.shape["ctx"], mesh.shape["seq"])
    step = local_fast if grid_size == (4, 8) else local_any
    return jax.shard_map(step, mesh=mesh, in_specs=in_specs, out_specs=out_specs, check_vma=False)
```

```python
import functools
import math

import jax
import jax.numpy as jnp
import numpy as np
from jax import lax
from jax.experimental import pallas as pl
from jax.experimental.pallas import tpu as pltpu
from jax.sharding import PartitionSpec as P

EPSILON = 1e-05
PRECISE = lax.Precision.HIGHEST


def gelu_tanh(values_in):
    return jax.nn.gelu(values_in, approximate=True)


def layer_norm(values_in, gain_vec, shift_vec):
    centre = values_in - jnp.mean(values_in, axis=-1, keepdims=True)
    scale_rows = lax.rsqrt(jnp.mean(centre * centre, axis=-1, keepdims=True) + EPSILON)
    unit_rows = centre * scale_rows
    return (unit_rows * gain_vec + shift_vec, unit_rows, scale_rows)


def norm_back(grad_rows, unit_rows, scale_rows, gain_vec):
    scaled = grad_rows * gain_vec
    return scale_rows * (
        scaled
        - jnp.mean(scaled, axis=-1, keepdims=True)
        - unit_rows * jnp.mean(scaled * unit_rows, axis=-1, keepdims=True)
    )


def kernel_piece(ssm_params, place_block):
    log_step, decay_log, turn_rate, read_real, read_imag = ssm_params
    step_size = jnp.exp(log_step)[:, None]
    decay_rate = jnp.exp(decay_log)
    rate_step = -decay_rate * step_size
    turn_step = turn_rate * step_size
    growth = jnp.exp(rate_step)
    edge_real = growth * jnp.cos(turn_step) - 1.0
    edge_imag = growth * jnp.sin(turn_step)
    modulus = decay_rate * decay_rate + turn_rate * turn_rate
    ratio_real = (-edge_real * decay_rate + edge_imag * turn_rate) / modulus
    ratio_imag = (-edge_imag * decay_rate - edge_real * turn_rate) / modulus
    coef_real = read_real * ratio_real - read_imag * ratio_imag
    coef_imag = read_real * ratio_imag + read_imag * ratio_real
    magnitude = jnp.exp(rate_step[:, :, None] * place_block[None, None, :])
    angles = turn_step[:, :, None] * place_block[None, None, :]
    terms = magnitude * (
        coef_real[:, :, None] * jnp.cos(angles) - coef_imag[:, :, None] * jnp.sin(angles)
    )
    return 2.0 * jnp.sum(terms, axis=1).T


def kernel_layout(ssm_params, positions):
    channels = ssm_params[0].shape[0]
    group_size = min(channels, 128)
    span_size = min(positions.shape[0], 128)
    group_count = channels // group_size
    grouped = jax.tree.map(
        lambda tensor: tensor.reshape((group_count, group_size) + tensor.shape[1:]), ssm_params
    )
    span_rows = positions.reshape(-1, span_size)
    return (channels, group_size, span_size, group_count, grouped, span_rows)


def kernel_block(ssm_params, positions):
    channels, group_size, span_size, group_count, grouped, span_rows = kernel_layout(
        ssm_params, positions
    )

    def per_group(piece_params):
        return lax.map(lambda place_block: kernel_piece(piece_params, place_block), span_rows)

    blocks = lax.map(per_group, grouped)
    return blocks.transpose(1, 2, 0, 3).reshape(positions.shape[0], channels)


def kernel_grads(ssm_params, positions, upstream):
    channels, group_size, span_size, group_count, grouped, span_rows = kernel_layout(
        ssm_params, positions
    )
    upstream_groups = upstream.reshape(
        span_rows.shape[0], span_size, group_count, group_size
    ).transpose(2, 0, 1, 3)

    def per_group(pairing):
        piece_params, piece_grad = pairing

        def accumulate(running, inputs_block):
            place_block, grad_block = inputs_block
            _, pullback = jax.vjp(
                lambda inner_params: kernel_piece(inner_params, place_block), piece_params
            )
            return (jax.tree.map(jnp.add, running, pullback(grad_block)[0]), None)

        initial = jax.tree.map(jnp.zeros_like, piece_params)
        totals, _ = lax.scan(accumulate, initial, (span_rows, piece_grad))
        return totals

    summed = lax.map(per_group, (grouped, upstream_groups))
    return jax.tree.map(lambda tensor: tensor.reshape((channels,) + tensor.shape[2:]), summed)


def phase_table(first_index, second_index, modulus):
    products_mod = first_index[:, None] * second_index[None, :] % modulus
    angles = products_mod.astype(jnp.float32) * (2.0 * math.pi / modulus)
    return (jnp.cos(angles), jnp.sin(angles))


def first_section(series, row_index, freq_index, modulus):
    cosine, sine_part = phase_table(row_index, freq_index, modulus)
    real_part = jnp.einsum("bnjh,nk->bkjh", series, cosine, precision=PRECISE)
    imag_part = -jnp.einsum("bnjh,nk->bkjh", series, sine_part, precision=PRECISE)
    return (real_part, imag_part)


def rotate(real_part, imag_part, row_index, col_index, modulus, direction):
    cosine, sine_part = phase_table(row_index, col_index, modulus)
    cosine = cosine[None, :, :, None]
    sine_part = direction * sine_part[None, :, :, None]
    return (real_part * cosine - imag_part * sine_part, real_part * sine_part + imag_part * cosine)


def mix_columns(real_part, imag_part, col_index, out_index, modulus, direction):
    cosine, sine_part = phase_table(col_index, out_index, modulus)
    sine_part = direction * sine_part

    def contract(operand, matrix):
        return jnp.einsum("bkjh,jm->bkmh", operand, matrix, precision=PRECISE)

    return (
        contract(real_part, cosine) - contract(imag_part, sine_part),
        contract(real_part, sine_part) + contract(imag_part, cosine),
    )


def last_section(real_part, imag_part, freq_index, row_index, modulus, length_all):
    cosine, sine_part = phase_table(freq_index, row_index, modulus)
    summed = jnp.einsum("bkjh,kn->bnjh", real_part, cosine, precision=PRECISE) - jnp.einsum(
        "bkjh,kn->bnjh", imag_part, sine_part, precision=PRECISE
    )
    return summed / length_all


def local_spectrum(series):
    seq_parts = series.shape[1]
    block_len = series.shape[2]
    freq_count = 2 * seq_parts
    modulus = freq_count * block_len
    freq_index = jnp.arange(freq_count)
    col_index = jnp.arange(block_len)
    real_part, imag_part = first_section(series, jnp.arange(seq_parts), freq_index, freq_count)
    real_part, imag_part = rotate(real_part, imag_part, freq_index, col_index, modulus, -1.0)
    return mix_columns(real_part, imag_part, col_index, col_index, block_len, -1.0)


def local_time(real_part, imag_part):
    freq_count = real_part.shape[1]
    block_len = real_part.shape[2]
    seq_parts = freq_count // 2
    modulus = freq_count * block_len
    freq_index = jnp.arange(freq_count)
    col_index = jnp.arange(block_len)
    real_part, imag_part = mix_columns(real_part, imag_part, col_index, col_index, block_len, 1.0)
    real_part, imag_part = rotate(real_part, imag_part, freq_index, col_index, modulus, 1.0)
    return last_section(
        real_part, imag_part, freq_index, jnp.arange(seq_parts), freq_count, modulus
    )


def channel_spectrum(series):
    seq_parts = lax.axis_size("seq")
    spread = lax.all_to_all(series, "seq", split_axis=2, concat_axis=1, tiled=True)
    batch_size, total_len, chan_count = spread.shape
    return local_spectrum(spread.reshape(batch_size, seq_parts, total_len // seq_parts, chan_count))


def token_blocks(series):
    batch_size, seq_parts, block_len, chan_count = series.shape
    flat_series = series.reshape(batch_size, seq_parts * block_len, chan_count)
    return lax.all_to_all(flat_series, "seq", split_axis=1, concat_axis=2, tiled=True)


def times_kernel(sig_real, sig_imag, ker_real, ker_imag):
    return (sig_real * ker_real - sig_imag * ker_imag, sig_real * ker_imag + sig_imag * ker_real)


def conj_products(sig_real, sig_imag, ker_real, ker_imag, grad_real, grad_imag):
    back_real = ker_real * grad_real + ker_imag * grad_imag
    back_imag = ker_real * grad_imag - ker_imag * grad_real
    kern_real = jnp.sum(sig_real * grad_real + sig_imag * grad_imag, axis=0, keepdims=True)
    kern_imag = jnp.sum(sig_real * grad_imag - sig_imag * grad_real, axis=0, keepdims=True)
    return (
        jnp.concatenate([back_real, kern_real], axis=0),
        jnp.concatenate([back_imag, kern_imag], axis=0),
    )


F32 = jnp.float32
BF16 = jnp.bfloat16
BLOCK = 128
STEP_LOW = 32
AXES = ("ctx", "seq")
VMEM_BYTES = 60 * 1024 * 1024
ONCE = pl.Buffered(1)
COST_SCALE = 20.0


def shape_of(shape, kind=F32):
    return jax.ShapeDtypeStruct(shape, kind)


def whole(shape):
    return pl.BlockSpec(shape, lambda *_: (0,) * len(shape))


def whole_once(shape):
    return pl.BlockSpec(shape, lambda *_: (0,) * len(shape), pipeline_mode=ONCE)


def launch(body, name, meta, after, ins, in_specs, outs, out_specs, grid, scratch=(), micros=1):
    n_in, n_out = len(ins), len(outs)
    after = list(after) if isinstance(after, (list, tuple)) else [after]
    anywhere = pl.BlockSpec(memory_space=pl.ANY)

    def kernel(meta_ref, *refs):
        first = n_in + len(after)
        last = first + n_out
        body(meta_ref, *refs[:n_in], *refs[first:last], *refs[last + 1 :])

    results = pl.pallas_call(
        kernel,
        grid_spec=pltpu.PrefetchScalarGridSpec(
            num_scalar_prefetch=1,
            grid=grid,
            in_specs=list(in_specs) + [anywhere] * len(after),
            out_specs=list(out_specs) + [anywhere],
            scratch_shapes=list(scratch),
        ),
        out_shape=list(outs) + [shape_of((8, BLOCK))],
        compiler_params=pltpu.CompilerParams(
            dimension_semantics=("arbitrary",) * len(grid), vmem_limit_bytes=VMEM_BYTES
        ),
        cost_estimate=pl.CostEstimate(
            flops=int(COST_SCALE * micros * 1.15e9), bytes_accessed=0, transcendentals=0
        ),
        name=name,
    )(meta, *ins, *after)
    return list(results[:-1]), results[-1]


def odd_tables():
    points = np.arange(BLOCK)
    turns = np.pi * np.outer(2 * points + 1, points) / (2 * BLOCK)
    ahead = np.concatenate([np.cos(turns), -np.sin(turns)], axis=0)
    back = ahead.T / BLOCK

    def halves(table):
        table = table.astype(np.float32)
        high = table.astype(BF16)
        return high, (table - high.astype(np.float32)).astype(BF16)

    return halves(ahead) + halves(back)


def dot_parts(high, low, operand):
    op_high = operand.astype(BF16)
    op_low = (operand - op_high.astype(F32)).astype(BF16)

    def one(left, right):
        return jnp.dot(left, right, preferred_element_type=F32)

    return one(high, op_high) + (one(high, op_low) + one(low, op_high))


def moves_of(chips):
    return [(h, d) for h in range(chips) for d in (0, 1)]


def partner(meta_ref, contexts, chips, move, ahead):
    place = meta_ref[contexts]
    chip, core = place // 2, place % 2
    hops = move[0] if ahead else chips - move[0]
    other = core if move[1] == 0 else 1 - core
    return ((chip + hops) % chips) * 2 + other


def lane_block(index, size=BLOCK):
    return pl.ds(pl.multiple_of(index * size, size), size)


def send_along(value, move):
    groups = lax.axis_size("ctx")
    places = lax.axis_size("seq")
    pairs = []
    for c in range(groups):
        for s in range(places):
            to_c, to_s = move(c, s)
            pairs.append((c * places + s, to_c * places + to_s))
    return lax.ppermute(value, AXES, pairs)


def to_sibling(value):
    return send_along(value, lambda c, s: (c, s ^ 1))


def to_x(value):
    return send_along(value, lambda c, s: (c ^ 1, s))


def to_y(value):
    return send_along(value, lambda c, s: (c ^ 2, s))


def to_partner(value, move):
    chips = lax.axis_size("seq") // 2
    return send_along(value, lambda c, s: (c, ((s // 2 + move[0]) % chips) * 2 + (s % 2 ^ move[1])))


def swap_blocks(blocks):
    moves = moves_of(len(blocks) // 2)
    chips = len(blocks) // 2
    order = sorted(range(len(moves)), key=lambda k: -min(moves[k][0], chips - moves[k][0]))
    got = {k: blocks[k] if k == 0 else to_partner(blocks[k], moves[k]) for k in order}
    return [got[k] for k in range(len(moves))]


def swap_parts(parts_array):
    return lax.all_to_all(parts_array, "seq", split_axis=0, concat_axis=0, tiled=True)


def part_spec(parts, step):
    return pl.BlockSpec((parts, step, BLOCK, BLOCK), lambda i, m: (0, i, 0, 0))


def block_specs(parts, step, first=0):
    return [pl.BlockSpec((step, BLOCK, BLOCK), lambda i, m: (first + i, 0, 0))] * parts


def block_shapes(parts, count):
    return [shape_of((count, BLOCK, BLOCK))] * parts


def hand_out(meta_ref, contexts, chips, rows_ref, outs):
    for move, out in zip(moves_of(chips), outs):
        where = lane_block(partner(meta_ref, contexts, chips, move, True))
        for c in range(out.shape[0]):
            out[c] = rows_ref[c * BLOCK : (c + 1) * BLOCK, where]


def norm_rows(rows):
    centre = rows - jnp.mean(rows, axis=-1, keepdims=True)
    scale = lax.rsqrt(jnp.mean(centre * centre, axis=-1, keepdims=True) + EPSILON)
    return centre * scale, scale


def mask_column(meta_ref, context, contexts):
    places = lax.broadcasted_iota(jnp.int32, (BLOCK, 1), 0) + meta_ref[contexts] * BLOCK
    return (places < meta_ref[context]).astype(F32)


def make_signal(meta, after, block_input, gain, shift, base, count):
    contexts, block_len, channels = block_input.shape
    parts = channels // BLOCK
    chips = parts // 2

    def body(meta_ref, x_ref, gain_ref, shift_ref, rows_ref, *outs):
        unit, _ = norm_rows(x_ref[0].astype(F32))
        mask = mask_column(meta_ref, pl.program_id(0) + base, contexts)
        rows_ref[...] = (unit * gain_ref[...] + shift_ref[...]) * mask
        hand_out(meta_ref, contexts, chips, rows_ref, outs)

    outs, token = launch(
        body,
        "signal",
        meta,
        after,
        [block_input, gain, shift],
        [
            pl.BlockSpec((1, block_len, channels), lambda i, m: (base + i, 0, 0)),
            whole((1, channels)),
            whole((1, channels)),
        ],
        [shape_of((count * block_len, channels))] + block_shapes(parts, count),
        [rows_spec(block_len, channels)] + block_specs(parts, 1),
        (count,),
        micros=5,
    )
    return outs[0], outs[1:], token


def mode_coefs(log_step, decay_log, turn_rate, read_real, read_imag):
    step_size = jnp.exp(log_step)[None, :]
    decay_rate = jnp.exp(decay_log)
    rate_step = -decay_rate * step_size
    turn_step = turn_rate * step_size
    growth = jnp.exp(rate_step)
    edge_real = growth * jnp.cos(turn_step) - 1.0
    edge_imag = growth * jnp.sin(turn_step)
    modulus = decay_rate * decay_rate + turn_rate * turn_rate
    ratio_real = (-edge_real * decay_rate + edge_imag * turn_rate) / modulus
    ratio_imag = (-edge_imag * decay_rate - edge_real * turn_rate) / modulus
    coef_real = read_real * ratio_real - read_imag * ratio_imag
    coef_imag = read_real * ratio_imag + read_imag * ratio_real
    return rate_step, turn_step, coef_real, coef_imag


def times(a, b):
    return a[0] * b[0] - a[1] * b[1], a[0] * b[1] + a[1] * b[0]


def low_table(rate_ref, turn_ref, low_real, low_imag):
    place = lax.broadcasted_iota(jnp.int32, (8, BLOCK), 0)
    size = jnp.exp(rate_ref[...])
    low_real[:, 0, :] = size * jnp.cos(turn_ref[...])
    low_imag[:, 0, :] = size * jnp.sin(turn_ref[...])

    def fill(mode, _):
        power = (low_real[mode, 0:1, :], low_imag[mode, 0:1, :])
        piece = (jnp.ones((8, BLOCK), F32), jnp.zeros((8, BLOCK), F32))
        for bit in range(3):
            chosen = ((place >> bit) & 1) == 1
            moved = times(piece, power)
            piece = (jnp.where(chosen, moved[0], piece[0]), jnp.where(chosen, moved[1], piece[1]))
            power = times(power, power)
        for block in range(STEP_LOW // 8):
            low_real[mode, block * 8 : (block + 1) * 8, :] = piece[0]
            low_imag[mode, block * 8 : (block + 1) * 8, :] = piece[1]
            piece = times(piece, power)
        return 0

    lax.fori_loop(0, rate_ref.shape[0], fill, 0)


def high_table(rate_ref, turn_ref, start_real, start_imag, high_real, high_imag):
    size = jnp.exp(rate_ref[...] * STEP_LOW)
    angle = turn_ref[...] * STEP_LOW
    move_real = size * jnp.cos(angle)
    move_imag = size * jnp.sin(angle)

    def fill(place, carry):
        now_real, now_imag = carry
        high_real[place] = now_real
        high_imag[place] = now_imag
        return (
            now_real * move_real - now_imag * move_imag,
            now_real * move_imag + now_imag * move_real,
        )

    lax.fori_loop(0, high_real.shape[0], fill, (start_real, start_imag))


def alternate_sign(rows):
    place = lax.broadcasted_iota(jnp.int32, (rows, 1), 0)
    return (1 - 2 * (place & 1)).astype(F32)


def spectrum_body(
    meta_ref,
    rate_ref,
    turn_ref,
    coef_real_ref,
    coef_imag_ref,
    ahead_high,
    ahead_low,
    out_ref,
    low_real,
    low_imag,
    high_real,
    high_imag,
    taps,
):
    modes = rate_ref.shape[0]
    parts = out_ref.shape[0]
    low_table(rate_ref, turn_ref, low_real, low_imag)
    high_table(rate_ref, turn_ref, coef_real_ref[...], coef_imag_ref[...], high_real, high_imag)
    tile = 8

    def per_tile(index, _):
        first = index * tile

        def per_mode(mode, sums):
            base_real = low_real[mode]
            base_imag = low_imag[mode]
            row = pl.ds(mode, 1)
            return tuple(
                sums[k]
                + (
                    high_real[first + k, row, :] * base_real
                    - high_imag[first + k, row, :] * base_imag
                )
                for k in range(tile)
            )

        zeros = jnp.zeros((STEP_LOW, BLOCK), F32)
        sums = lax.fori_loop(0, modes, per_mode, (zeros,) * tile)
        for k in range(tile):
            taps[pl.ds(pl.multiple_of((first + k) * STEP_LOW, STEP_LOW), STEP_LOW), :] = (
                2.0 * sums[k]
            )
        return 0

    lax.fori_loop(0, high_real.shape[0] // tile, per_tile, 0)
    wide = jnp.concatenate([taps[d * BLOCK : (d + 1) * BLOCK, :] for d in range(parts)], axis=1)
    plain = dot_parts(ahead_high[...], ahead_low[...], wide)
    sign = alternate_sign(BLOCK)
    for d in range(parts):
        here = plain[:, d * BLOCK : (d + 1) * BLOCK]
        real_part, imag_part = here[:BLOCK], here[BLOCK:]
        if d > 0:
            before = plain[:, (d - 1) * BLOCK : d * BLOCK]
            real_part = real_part - sign * before[BLOCK:]
            imag_part = imag_part + sign * before[:BLOCK]
        out_ref[d, :BLOCK, :] = real_part
        out_ref[d, BLOCK:, :] = imag_part


def mode_scratch(modes, high_count):
    return [
        pltpu.VMEM((modes, STEP_LOW, BLOCK), F32),
        pltpu.VMEM((modes, STEP_LOW, BLOCK), F32),
        pltpu.VMEM((high_count, modes, BLOCK), F32),
        pltpu.VMEM((high_count, modes, BLOCK), F32),
    ]


def make_spectrum(meta, after, coefs, tables, parts):
    modes = coefs[0].shape[0]
    high_count = parts * BLOCK // STEP_LOW
    outs, token = launch(
        spectrum_body,
        "taps_spectrum",
        meta,
        after,
        list(coefs) + [tables[0], tables[1]],
        [whole((modes, BLOCK))] * 4 + [whole((2 * BLOCK, BLOCK))] * 2,
        [shape_of((parts, 2 * BLOCK, BLOCK))],
        [whole((parts, 2 * BLOCK, BLOCK))],
        (1,),
        mode_scratch(modes, high_count) + [pltpu.VMEM((parts * BLOCK, BLOCK), F32)],
        micros=12,
    )
    return outs[0], token


def spectra_of(meta_ref, contexts, chips, tables, series, write):
    wide = jnp.concatenate([ref[0] for ref in series], axis=1)
    result = dot_parts(tables[0][...], tables[1][...], wide)
    for k, move in enumerate(moves_of(chips)):
        here = partner(meta_ref, contexts, chips, move, False)
        write(lane_block(here), result[:, k * BLOCK : (k + 1) * BLOCK])


def lanes(t):
    return pl.ds(t * BLOCK, BLOCK)


def convolve(meta, after, contexts, series, taps, tables, base, count):
    parts = len(series)
    chips = parts // 2
    wide = parts * BLOCK

    def body(meta_ref, *refs):
        blocks = refs[:parts]
        taps_ref = refs[parts]
        maps = refs[parts + 1 : parts + 5]
        outs = refs[parts + 5 : 2 * parts + 5]
        spec_ref, mixed, rows = refs[2 * parts + 5 :]

        def write(where, values):
            spec_ref[0, :, where] = values

        spectra_of(meta_ref, contexts, chips, maps[:2], blocks, write)

        def per_tile(index, _):
            real_rows = pl.ds(pl.multiple_of(index * 8, 8), 8)
            imag_rows = pl.ds(pl.multiple_of(BLOCK + index * 8, 8), 8)
            k_real = [taps_ref[d, real_rows, :] for d in range(parts)]
            k_imag = [taps_ref[d, imag_rows, :] for d in range(parts)]
            u_real = [spec_ref[0, real_rows, lanes(t)] for t in range(parts)]
            u_imag = [spec_ref[0, imag_rows, lanes(t)] for t in range(parts)]
            for s in range(parts):
                sum_real = jnp.zeros((8, BLOCK), F32)
                sum_imag = jnp.zeros((8, BLOCK), F32)
                for t in range(s + 1):
                    d = s - t
                    sum_real += k_real[d] * u_real[t] - k_imag[d] * u_imag[t]
                    sum_imag += k_real[d] * u_imag[t] + k_imag[d] * u_real[t]
                mixed[real_rows, lanes(s)] = sum_real
                mixed[imag_rows, lanes(s)] = sum_imag
            return 0

        lax.fori_loop(0, BLOCK // 8, per_tile, 0)
        rows[...] = dot_parts(maps[2][...], maps[3][...], mixed[...])
        hand_out(meta_ref, contexts, chips, rows, outs)

    outs, token = launch(
        body,
        "convolve",
        meta,
        after,
        list(series) + [taps] + list(tables),
        block_specs(parts, 1, base)
        + [whole((parts, 2 * BLOCK, BLOCK))]
        + [whole((2 * BLOCK, BLOCK))] * 2
        + [whole((BLOCK, 2 * BLOCK))] * 2,
        block_shapes(parts, count) + [shape_of((count, 2 * BLOCK, wide))],
        block_specs(parts, 1) + [pl.BlockSpec((1, 2 * BLOCK, wide), lambda i, m: (i, 0, 0))],
        (count,),
        [pltpu.VMEM((2 * BLOCK, wide), F32), pltpu.VMEM((BLOCK, wide), F32)],
        micros=7,
    )
    return outs[:parts], outs[parts], token


def convolve_back(meta, after, contexts, series, spectra, taps, tables):
    parts, count = series.shape[:2]
    wide = parts * BLOCK
    pieces = len(spectra)
    each = count // pieces

    def body(meta_ref, *refs):
        series_ref = refs[0]
        refs = refs[1:]
        spec_refs = refs[:pieces]
        refs = refs[pieces:]
        taps_ref = refs[0]
        maps = refs[1:5]
        out_ref, taps_grad_ref, grad_spec, mixed, pairs, spec_ref = refs[5:]
        step = pl.program_id(0)
        for k in range(pieces):

            @pl.when(step // each == k)
            def _(k=k):
                spec_ref[...] = spec_refs[k][...]

        @pl.when(step == 0)
        def _():
            pairs[...] = jnp.zeros_like(pairs)

        series_wide = jnp.concatenate([series_ref[t, 0] for t in range(parts)], axis=1)
        grad_spec[...] = dot_parts(maps[0][...], maps[1][...], series_wide)

        def per_tile(index, _):
            real_rows = pl.ds(pl.multiple_of(index * 8, 8), 8)
            imag_rows = pl.ds(pl.multiple_of(BLOCK + index * 8, 8), 8)
            k_real = [taps_ref[d, real_rows, :] for d in range(parts)]
            k_imag = [taps_ref[d, imag_rows, :] for d in range(parts)]
            g_real = [grad_spec[real_rows, lanes(t)] for t in range(parts)]
            g_imag = [grad_spec[imag_rows, lanes(t)] for t in range(parts)]
            for t in range(parts):
                sum_real = jnp.zeros((8, BLOCK), F32)
                sum_imag = jnp.zeros((8, BLOCK), F32)
                for s in range(t, parts):
                    d = s - t
                    sum_real += k_real[d] * g_real[s] + k_imag[d] * g_imag[s]
                    sum_imag += k_real[d] * g_imag[s] - k_imag[d] * g_real[s]
                mixed[real_rows, lanes(t)] = sum_real
                mixed[imag_rows, lanes(t)] = sum_imag
            u_real = [spec_ref[0, real_rows, lanes(t)] for t in range(parts)]
            u_imag = [spec_ref[0, imag_rows, lanes(t)] for t in range(parts)]
            for d in range(parts):
                sum_real = pairs[real_rows, lanes(d)]
                sum_imag = pairs[imag_rows, lanes(d)]
                for t in range(parts - d):
                    s = t + d
                    sum_real += u_real[t] * g_real[s] + u_imag[t] * g_imag[s]
                    sum_imag += u_real[t] * g_imag[s] - u_imag[t] * g_real[s]
                pairs[real_rows, lanes(d)] = sum_real
                pairs[imag_rows, lanes(d)] = sum_imag
            return 0

        lax.fori_loop(0, BLOCK // 8, per_tile, 0)
        rows = dot_parts(maps[2][...], maps[3][...], mixed[...])
        for t in range(parts):
            out_ref[t, 0] = rows[:, t * BLOCK : (t + 1) * BLOCK]

        @pl.when(step == count - 1)
        def _():
            sign = alternate_sign(BLOCK)
            for d in range(parts):
                real_part = pairs[:BLOCK, lanes(d)]
                imag_part = pairs[BLOCK:, lanes(d)]
                if d + 1 < parts:
                    real_part = real_part + sign * pairs[BLOCK:, lanes(d + 1)]
                    imag_part = imag_part - sign * pairs[:BLOCK, lanes(d + 1)]
                mixed[:BLOCK, lanes(d)] = real_part
                mixed[BLOCK:, lanes(d)] = imag_part
            taps_grad = dot_parts(maps[2][...], maps[3][...], mixed[...])
            for d in range(parts):
                taps_grad_ref[d] = taps_grad[:, d * BLOCK : (d + 1) * BLOCK]

    outs, token = launch(
        body,
        "convolve_back",
        meta,
        after,
        [series] + list(spectra) + [taps] + list(tables),
        [part_spec(parts, 1)]
        + [
            pl.BlockSpec(
                (1, 2 * BLOCK, wide),
                lambda i, m, k=k: (jnp.clip(i - k * each, 0, each - 1), 0, 0),
            )
            for k in range(pieces)
        ]
        + [whole((parts, 2 * BLOCK, BLOCK))]
        + [whole((2 * BLOCK, BLOCK))] * 2
        + [whole((BLOCK, 2 * BLOCK))] * 2,
        [shape_of((parts, count, BLOCK, BLOCK)), shape_of((parts, BLOCK, BLOCK))],
        [part_spec(parts, 1), whole((parts, BLOCK, BLOCK))],
        (count,),
        [pltpu.VMEM((2 * BLOCK, wide), F32)] * 3
        + [pltpu.VMEM((1, 2 * BLOCK, wide), F32)],
        micros=16,
    )
    return outs[0], outs[1], token


def moments_body(
    meta_ref, rate_ref, turn_ref, grad_ref, out_ref, low_real, low_imag, high_real, high_imag
):
    modes = rate_ref.shape[0]
    count = high_real.shape[0]
    low_table(rate_ref, turn_ref, low_real, low_imag)
    ones = jnp.ones(rate_ref.shape, F32)
    high_table(rate_ref, turn_ref, ones, jnp.zeros_like(ones), high_real, high_imag)
    places = lax.broadcasted_iota(jnp.int32, (STEP_LOW, 1), 0).astype(F32)
    tile = 8

    def per_mode(mode, _):
        row = pl.ds(mode, 1)
        zeros = jnp.zeros((STEP_LOW, BLOCK), F32)

        def per_tile(index, sums):
            plain_real, plain_imag, by_real, by_imag = sums
            for k in range(tile):
                place = index * tile + k
                rows = pl.ds(pl.multiple_of(place * STEP_LOW, STEP_LOW), STEP_LOW)
                grad = grad_ref[rows, :]
                term_real = high_real[place, row, :] * grad
                term_imag = high_imag[place, row, :] * grad
                plain_real += term_real
                plain_imag += term_imag
                weight = (place * STEP_LOW).astype(F32)
                by_real += term_real * weight
                by_imag += term_imag * weight
            return plain_real, plain_imag, by_real, by_imag

        plain_real, plain_imag, by_real, by_imag = lax.fori_loop(
            0, count // tile, per_tile, (zeros,) * 4
        )
        base_real = low_real[mode]
        base_imag = low_imag[mode]

        def total(rows_in):
            return jnp.sum(rows_in, axis=0, keepdims=True)

        first_real = by_real + places * plain_real
        first_imag = by_imag + places * plain_imag
        out_ref[0, row, :] = total(base_real * plain_real - base_imag * plain_imag)
        out_ref[1, row, :] = total(base_real * plain_imag + base_imag * plain_real)
        out_ref[2, row, :] = total(base_real * first_real - base_imag * first_imag)
        out_ref[3, row, :] = total(base_real * first_imag + base_imag * first_real)
        return 0

    lax.fori_loop(0, modes, per_mode, 0)


def make_moments(meta, after, rate, turn, taps_grad):
    modes = rate.shape[0]
    length = taps_grad.shape[0]
    outs, token = launch(
        moments_body,
        "moments",
        meta,
        after,
        [rate, turn, taps_grad],
        [whole((modes, BLOCK)), whole((modes, BLOCK)), whole((length, BLOCK))],
        [shape_of((4, modes, BLOCK))],
        [whole((4, modes, BLOCK))],
        (1,),
        mode_scratch(modes, length // STEP_LOW),
        micros=16,
    )
    return outs[0], token


GELU_SCALE = 0.7978845608
GELU_CUBE = 0.044715


def gelu(value):
    inner = GELU_SCALE * value * (1.0 + GELU_CUBE * (value * value))
    return value * (0.5 + 0.5 * jnp.tanh(inner))


def gelu_slope(value):
    square = value * value
    bend = jnp.tanh(GELU_SCALE * value * (1.0 + GELU_CUBE * square))
    rise = GELU_SCALE + (3.0 * GELU_SCALE * GELU_CUBE) * square
    return 0.5 + 0.5 * (bend + value * (1.0 - bend * bend) * rise)


def sigmoid(value):
    return 0.5 * (1.0 + jnp.tanh(0.5 * value))


def dot(left, right):
    return jnp.dot(left, right, preferred_element_type=F32)


def dot_nt(left, right):
    return lax.dot_general(left, right, (((1,), (1,)), ((), ())), preferred_element_type=F32)


def dot_tn(left, right):
    return lax.dot_general(left, right, (((0,), (0,)), ((), ())), preferred_element_type=F32)


def gather_parts(meta_ref, contexts, chips, blocks, rows_ref):
    count = blocks[0].shape[0]
    for move, ref in zip(moves_of(chips), blocks):
        where = lane_block(partner(meta_ref, contexts, chips, move, False))
        for c in range(count):
            rows_ref[c * BLOCK : (c + 1) * BLOCK, where] = ref[c]


def rows_spec(rows, columns, start=0):
    return pl.BlockSpec((rows, columns), lambda i, m: (start + i, 0))


class Copies:
    def __init__(self, semaphores):
        self.semaphores = semaphores
        self.running = []

    def start(self, source, target):
        copy = pltpu.make_async_copy(source, target, self.semaphores.at[len(self.running)])
        copy.start()
        self.running.append(copy)
        return copy


def in_hbm():
    return pl.BlockSpec(memory_space=pl.ANY)


def make_forward(
    meta,
    after,
    block_input,
    conv,
    signal,
    skip,
    glu,
    glu_bias,
    gain,
    shift,
    up,
    up_bias,
    base,
    step,
):
    contexts, block_len, channels = block_input.shape
    parts = len(conv)
    chips = parts // 2
    hidden_units = up.shape[1]
    wide = hidden_units // parts
    rows = step * BLOCK
    first = base // step
    gate_tile = 256

    half, half_wide = channels // 2, hidden_units // 2
    outs = [
        (half, BF16),
        (half, F32),
        (channels, F32),
        (channels, F32),
        (channels, F32),
        (channels, F32),
        (half, BF16),
        (half, F32),
        (half_wide, BF16),
        (half_wide, F32),
        (hidden_units, F32),
    ]
    copies_in_all = 2 + 8 + 3 * parts

    def body(meta_ref, x_ref, *refs):
        blocks = refs[:parts]
        refs = refs[parts:]
        signal_ref, skip_ref, glu_hbm, glu_bias_ref, gain_ref, shift_ref, up_hbm, up_bias_ref = (
            refs[:8]
        )
        targets = refs[8 : 8 + len(outs)]
        held = refs[8 + len(outs) : 8 + 2 * len(outs)]
        glu_ref, up_ref, rows_scr, semaphores = refs[8 + 2 * len(outs) :]
        (
            act_own,
            act_send,
            mixed_ref,
            gate_a_ref,
            gate_sig_ref,
            hidden_ref,
            second_own,
            second_send,
            wide_own,
            wide_send,
            inner_ref,
        ) = held
        copies = Copies(semaphores)
        glu_copy = copies.start(glu_hbm, glu_ref)
        up_copy = copies.start(up_hbm, up_ref)
        leaving = []

        def leave(*which):
            for k in which:
                leaving.append(copies.start(held[k], targets[k]))

        def share(own_ref, send_ref):
            for h in range(chips):
                here = lane_block(partner(meta_ref, contexts, chips, (h, 0), True))
                there = lane_block(partner(meta_ref, contexts, chips, (h, 1), True))
                own_ref[:, lanes(h)] = rows_scr[:, here].astype(BF16)
                send_ref[:, lanes(h)] = rows_scr[:, there].astype(BF16).astype(F32)

        gather_parts(meta_ref, contexts, chips, blocks, rows_scr)
        mixed = rows_scr[...] + skip_ref[...] * signal_ref[...]
        mixed_ref[...] = mixed
        activated = gelu(mixed)
        rows_scr[...] = activated
        share(act_own, act_send)
        leave(0, 1, 2)
        activated = activated.astype(BF16)
        x = x_ref[...].reshape(rows, channels)
        glu_copy.wait()
        for k in range(channels // gate_tile):
            cols = slice(k * gate_tile, (k + 1) * gate_tile)
            late = slice(channels + k * gate_tile, channels + (k + 1) * gate_tile)
            gate_a = dot(activated, glu_ref[:, cols]) + glu_bias_ref[:, cols]
            gate_sig = sigmoid(dot(activated, glu_ref[:, late]) + glu_bias_ref[:, late])
            gate_a_ref[:, cols] = gate_a
            gate_sig_ref[:, cols] = gate_sig
            hidden_ref[:, cols] = x[:, cols].astype(F32) + gate_a * gate_sig
        leave(3, 4, 5)
        unit, _ = norm_rows(hidden_ref[...])
        second = unit * gain_ref[...] + shift_ref[...]
        rows_scr[...] = second
        share(second_own, second_send)
        leave(6, 7)
        second = second.astype(BF16)
        up_copy.wait()
        for d in (1, 0):
            for h in range(chips):
                slot = slice(h * wide, (h + 1) * wide)
                cols = lane_block(partner(meta_ref, contexts, chips, (h, d), True), wide)
                inner = dot(second, up_ref[:, cols]) + up_bias_ref[:, cols]
                inner_ref[:, cols] = inner
                widened = gelu(inner).astype(BF16)
                leaving.append(copies.start(inner_ref.at[:, cols], targets[10].at[:, cols]))
                if d == 0:
                    wide_own[:, slot] = widened
                    leaving.append(copies.start(wide_own.at[:, slot], targets[8].at[:, slot]))
                else:
                    wide_send[:, slot] = widened.astype(F32)
                    leaving.append(copies.start(wide_send.at[:, slot], targets[9].at[:, slot]))
        for copy in leaving:
            copy.wait()

    results, token = launch(
        body,
        "forward_rows",
        meta,
        after,
        [block_input]
        + list(conv)
        + [signal, skip, glu, glu_bias, gain, shift, up, up_bias],
        [pl.BlockSpec((step, block_len, channels), lambda i, m: (first + i, 0, 0))]
        + block_specs(parts, step)
        + [
            rows_spec(rows, channels, first),
            whole_once((1, channels)),
            in_hbm(),
            whole_once((1, 2 * channels)),
            whole_once((1, channels)),
            whole_once((1, channels)),
            in_hbm(),
            whole_once((1, hidden_units)),
        ],
        [shape_of((rows, columns), kind) for columns, kind in outs],
        [in_hbm()] * len(outs),
        (1,),
        [pltpu.VMEM((rows, columns), kind) for columns, kind in outs]
        + [
            pltpu.VMEM((channels, 2 * channels), BF16),
            pltpu.VMEM((channels, hidden_units), BF16),
            pltpu.VMEM((rows, channels), F32),
            pltpu.SemaphoreType.DMA((copies_in_all,)),
        ],
        micros=16,
    )
    return results, token


def make_output(meta, after, contexts, hidden, wide_own, wide_send, down, bias, base, step):
    all_rows, channels = hidden.shape
    hidden_units = down.shape[0]
    rows = step * BLOCK
    parts = channels // BLOCK
    chips = parts // 2
    wide = hidden_units // parts

    def body(meta_ref, hidden_ref, own_ref, send_ref, down_ref, bias_ref, out_ref):
        total = hidden_ref[...] + bias_ref[...]
        for h in range(chips):
            slot = slice(h * wide, (h + 1) * wide)
            here = lane_block(partner(meta_ref, contexts, chips, (h, 0), True), wide)
            there = lane_block(partner(meta_ref, contexts, chips, (h, 1), True), wide)
            total += dot(own_ref[:, slot], down_ref[here, :])
            total += dot(send_ref[:, slot].astype(BF16), down_ref[there, :])
        first = base + pl.program_id(0) * step
        for c in range(step):
            mask = mask_column(meta_ref, first + c, contexts)
            out_ref[c] = (total[c * BLOCK : (c + 1) * BLOCK] * mask).astype(BF16)

    outs, token = launch(
        body,
        "output_rows",
        meta,
        after,
        [hidden, wide_own, wide_send, down, bias],
        [
            rows_spec(rows, channels),
            rows_spec(rows, hidden_units // 2),
            rows_spec(rows, hidden_units // 2),
            whole_once((hidden_units, channels)),
            whole_once((1, channels)),
        ],
        [shape_of((all_rows // BLOCK, BLOCK, channels), BF16)],
        [pl.BlockSpec((step, BLOCK, channels), lambda i, m: (i, 0, 0))],
        (all_rows // rows,),
        micros=8,
    )
    return outs[0], token


def mask_rows(meta, after, out_grad):
    contexts, block_len, channels = out_grad.shape

    def body(meta_ref, grad_ref, out_ref, sum_ref):
        context = pl.program_id(0)
        rows = grad_ref[0].astype(F32) * mask_column(meta_ref, context, contexts)
        out_ref[...] = rows

        @pl.when(context == 0)
        def _():
            sum_ref[...] = jnp.zeros_like(sum_ref)

        sum_ref[...] += jnp.sum(rows, axis=0, keepdims=True)

    outs, token = launch(
        body,
        "mask_rows",
        meta,
        after,
        [out_grad],
        [pl.BlockSpec((1, block_len, channels), lambda i, m: (i, 0, 0))],
        [shape_of((contexts * block_len, channels)), shape_of((1, channels))],
        [rows_spec(block_len, channels), whole((1, channels))],
        (contexts,),
        micros=4,
    )
    return outs[0], outs[1], token


def make_backward(
    meta,
    after,
    contexts,
    grad_out,
    signal,
    ahead,
    gain,
    down,
    up,
    glu,
    step,
):
    pieces = len(ahead)
    all_rows, channels = grad_out.shape
    each = all_rows // (pieces * step * BLOCK)
    hidden_units = up.shape[1]
    rows = step * BLOCK
    parts = channels // BLOCK
    chips = parts // 2
    tile = 512

    def body(
        meta_ref,
        grad_ref,
        signal_ref,
        *refs,
    ):
        gain_ref, down_ref, up_ref, glu_ref = refs[5 * pieces : 5 * pieces + 4]
        inner_out, gates_out, hidden_grad_ref, mixed_rows = refs[5 * pieces + 4 : 5 * pieces + 8]
        more = refs[5 * pieces + 8 :]
        for k in range(pieces):

            @pl.when(pl.program_id(0) // each == k)
            def _(k=k):
                one_piece(
                    grad_ref,
                    signal_ref,
                    *refs[5 * k : 5 * k + 5],
                    gain_ref,
                    down_ref,
                    up_ref,
                    glu_ref,
                    inner_out,
                    gates_out,
                    hidden_grad_ref,
                    mixed_rows,
                    *more,
                    meta_ref=meta_ref,
                )

    def one_piece(
        grad_ref,
        signal_ref,
        wide_inner,
        hidden_ref,
        gate_a_ref,
        gate_sig_ref,
        mixed_in,
        gain_ref,
        down_ref,
        up_ref,
        glu_ref,
        inner_out,
        gates_out,
        hidden_grad_ref,
        mixed_rows,
        *more,
        meta_ref,
    ):
        mixed_out, inner_sum, gates_sum, gain_sum, shift_sum, skip_sum = more

        @pl.when(pl.program_id(0) == 0)
        def _():
            inner_sum[...] = jnp.zeros_like(inner_sum)
            gates_sum[...] = jnp.zeros_like(gates_sum)
            gain_sum[...] = jnp.zeros_like(gain_sum)
            shift_sum[...] = jnp.zeros_like(shift_sum)
            skip_sum[...] = jnp.zeros_like(skip_sum)

        def add_rows(ref, cols, values):
            ref[:, cols] += jnp.sum(values, axis=0, keepdims=True)

        grad_out = grad_ref[...]
        grad_low = grad_out.astype(BF16)
        grad_second = jnp.zeros(grad_out.shape, F32)
        for k in range(hidden_units // tile):
            cols = slice(k * tile, (k + 1) * tile)
            grad_wide = dot_nt(grad_low, down_ref[cols, :])
            inner = (grad_wide * gelu_slope(wide_inner[:, cols])).astype(BF16)
            inner_full = inner.astype(F32)
            inner_out[:, cols] = inner_full
            add_rows(inner_sum, cols, inner_full)
            grad_second += dot_nt(inner, up_ref[:, cols])
        unit, scale = norm_rows(hidden_ref[...])
        every = slice(0, channels)
        add_rows(gain_sum, every, grad_second * unit)
        add_rows(shift_sum, every, grad_second)
        scaled = grad_second * gain_ref[...]
        grad_hidden = grad_out + scale * (
            scaled
            - jnp.mean(scaled, axis=-1, keepdims=True)
            - unit * jnp.mean(scaled * unit, axis=-1, keepdims=True)
        )
        hidden_grad_ref[...] = grad_hidden
        gate_sig = gate_sig_ref[...]
        gate_grad = grad_hidden * gate_sig
        early = gate_grad.astype(BF16)
        later = (gate_grad * gate_a_ref[...] * (1.0 - gate_sig)).astype(BF16)
        grad_act = dot_nt(early, glu_ref[:, :channels]) + dot_nt(later, glu_ref[:, channels:])
        second_half = slice(channels, 2 * channels)
        for values, cols in ((early.astype(F32), every), (later.astype(F32), second_half)):
            gates_out[:, cols] = values
            add_rows(gates_sum, cols, values)
        mixed_rows[...] = grad_act * gelu_slope(mixed_in[...])
        add_rows(skip_sum, every, mixed_rows[...] * signal_ref[...])
        for p in range(parts):
            for c in range(step):
                mixed_out[p, c] = mixed_rows[c * BLOCK : (c + 1) * BLOCK, lanes(p)]

    sums = [hidden_units, 2 * channels, channels, channels, channels]
    results, token = launch(
        body,
        "backward_rows",
        meta,
        after,
        [grad_out, signal] + [array for piece in ahead for array in piece] + [gain, down, up, glu],
        [pl.BlockSpec((rows, channels), lambda i, m: (i, 0), pipeline_mode=ONCE)] * 2
        + [
            pl.BlockSpec(
                (rows, array.shape[1]),
                lambda i, m, k=k: (jnp.clip(i - k * each, 0, each - 1), 0),
                pipeline_mode=pl.Buffered(1) if each == 1 else None,
            )
            for k, piece in enumerate(ahead)
            for array in piece
        ]
        + [
            whole_once((1, channels)),
            whole_once((hidden_units, channels)),
            whole_once((channels, hidden_units)),
            whole_once((channels, 2 * channels)),
        ],
        [
            shape_of((all_rows, hidden_units)),
            shape_of((all_rows, 2 * channels)),
            shape_of((all_rows, channels)),
            shape_of((all_rows, channels)),
        ]
        + [shape_of((parts, all_rows // BLOCK, BLOCK, BLOCK))]
        + [shape_of((1, columns)) for columns in sums],
        [
            rows_spec(rows, hidden_units),
            rows_spec(rows, 2 * channels),
            rows_spec(rows, channels),
            rows_spec(rows, channels),
        ]
        + [part_spec(parts, step)]
        + [whole((1, columns)) for columns in sums],
        (all_rows // rows,),
        micros=30,
    )
    return {
        "inner": results[0],
        "gates": results[1],
        "hidden": results[2],
        "mixed": results[3],
        "blocks": results[4],
        "sums": results[5:],
    }, token


def weight_grad(meta, after, name, pairs, groups, chips, row_tiles, col_tiles, micros, extra=None):
    rows = pairs[0][0].shape[1]
    cols = pairs[0][1].shape[1]
    row_block = rows // row_tiles
    col_block = cols // col_tiles
    chip_block = chips // row_tiles
    each = rows // (chips * groups)

    def body(meta_ref, *refs):
        out_ref = refs[-1]
        if extra is not None:
            out_ref[:, chips * each :, :] = refs[-2][...]
        total = None
        for k in range(len(pairs)):
            left, right = refs[2 * k], refs[2 * k + 1]
            term = dot_tn(left[...].astype(BF16), right[...].astype(BF16))
            total = term if total is None else total + term
        for h in range(chip_block):
            for q in range(groups):
                start = (h * groups + q) * each
                out_ref[q, h * each : (h + 1) * each, :] = total[start : start + each]

    in_specs = []
    operands = []
    nbytes = rows * cols * 4
    tokens_all = 0
    for left, right, start, tokens in pairs:
        in_specs.append(pl.BlockSpec((tokens, row_block), lambda i, j, m: (0, i)))
        in_specs.append(pl.BlockSpec((tokens, col_block), lambda i, j, m, s=start: (s, j)))
        operands += [left, right]
        tokens_all += tokens
        nbytes += tokens * (rows + cols) * 4
    more = 0
    if extra is not None:
        more = extra.shape[1]
        operands.append(extra)
        in_specs.append(pl.BlockSpec((groups, more, col_block), lambda i, j, m: (0, 0, j)))
    out_rows = chips * each + more
    block_rows = chip_block * each + more
    outs, token = launch(
        body,
        name,
        meta,
        after,
        operands,
        in_specs,
        [shape_of((groups, out_rows, cols))],
        [pl.BlockSpec((groups, block_rows, col_block), lambda i, j, m: (0, i, j))],
        (row_tiles, col_tiles),
        micros=micros,
    )
    return outs[0], token


def make_input_grad(
    meta,
    after,
    block_input,
    conv_grad,
    mixed_grad,
    hidden_grad,
    skip,
    gain,
    base,
):
    contexts, block_len, channels = block_input.shape
    parts, count = conv_grad.shape[:2]

    def body(meta_ref, x_ref, *refs):
        (
            conv_ref,
            mixed_ref,
            hidden_grad_ref,
            skip_ref,
            gain_ref,
            out_ref,
            gain_sum,
            shift_sum,
        ) = refs

        @pl.when(pl.program_id(0) == 0)
        def _():
            gain_sum[...] = jnp.zeros_like(gain_sum)
            shift_sum[...] = jnp.zeros_like(shift_sum)

        mask = mask_column(meta_ref, pl.program_id(0) + base, contexts)
        conv_rows = jnp.concatenate([conv_ref[p, 0] for p in range(parts)], axis=1)
        mixed = mixed_ref[...]
        grad_normed = (conv_rows + skip_ref[...] * mixed) * mask
        unit, scale = norm_rows(x_ref[0].astype(F32))
        gain_sum[...] += jnp.sum(grad_normed * unit, axis=0, keepdims=True)
        shift_sum[...] += jnp.sum(grad_normed, axis=0, keepdims=True)
        scaled = grad_normed * gain_ref[...]
        grad = hidden_grad_ref[...] + scale * (
            scaled
            - jnp.mean(scaled, axis=-1, keepdims=True)
            - unit * jnp.mean(scaled * unit, axis=-1, keepdims=True)
        )
        out_ref[0] = grad.astype(BF16)

    outs, token = launch(
        body,
        "input_grad",
        meta,
        after,
        [block_input, conv_grad, mixed_grad, hidden_grad, skip, gain],
        [pl.BlockSpec((1, block_len, channels), lambda i, m: (base + i, 0, 0))]
        + [part_spec(parts, 1)]
        + [rows_spec(block_len, channels)] * 2
        + [whole((1, channels))] * 2,
        [shape_of((count, block_len, channels), BF16)] + [shape_of((1, channels))] * 2,
        [pl.BlockSpec((1, block_len, channels), lambda i, m: (i, 0, 0))]
        + [whole((1, channels))] * 2,
        (count,),
        micros=7,
    )
    return outs, token


def scatter_groups(part):
    flat = part.reshape(-1, part.shape[-1])
    return lax.psum_scatter(flat, "ctx", scatter_dimension=0, tiled=True)


def to_near_chip(value):
    return send_along(value, lambda c, s: (c, s ^ 2))


def to_far_chip(value):
    return send_along(value, lambda c, s: (c, s ^ 4))


def pick_chips(meta, after, mine, chips, rows):
    cols = mine.shape[1]
    pairs = chips // 2
    place = meta.shape[0] - 2

    def source(i, m):
        chip = m[place] // 2
        side = chip % 2
        target = 2 * (i % pairs) + jnp.where(i < pairs, 1 - side, side)
        return ((target + chips - chip) % chips, 0)

    def body(meta_ref, mine_ref, send_ref, keep_ref):
        for k in range(chips):

            @pl.when(pl.program_id(0) == k)
            def _(k=k):
                (send_ref, keep_ref)[k // pairs][k % pairs] = mine_ref[...]

    outs, token = launch(
        body,
        "pick_chips",
        meta,
        after,
        [mine],
        [pl.BlockSpec((rows, cols), source)],
        [shape_of((pairs, rows, cols))] * 2,
        [whole((pairs, rows, cols))] * 2,
        (chips,),
        micros=2,
    )
    return (outs[1], to_near_chip(outs[0])), token


def add_pairs(meta, after, part):
    keep, got = part
    pairs, rows, cols = keep.shape
    place = meta.shape[0] - 2

    def body(meta_ref, keep_far, got_far, keep_near, got_near, send_ref, keep_ref):
        send_ref[...] = keep_far[0] + got_far[0]
        keep_ref[...] = keep_near[0] + got_near[0]

    def spec(far):
        def index(i, m):
            pair = m[place] // 4
            return ((pairs - 1 - pair) if far else pair, 0, 0)

        return pl.BlockSpec((1, rows, cols), index)

    outs, token = launch(
        body,
        "add_pairs",
        meta,
        after,
        [keep, got, keep, got],
        [spec(True), spec(True), spec(False), spec(False)],
        [shape_of((rows, cols))] * 2,
        [whole((rows, cols))] * 2,
        (1,),
        micros=3,
    )
    return (outs[1], to_far_chip(outs[0])), token


def add_chips(meta, after, mine, others):
    rows, cols = others[0].shape

    def body(meta_ref, *refs):
        total = refs[0][...]
        for ref in refs[1:-1]:
            total = total + ref[...]
        refs[-1][...] = total

    outs, token = launch(
        body,
        "add_chips",
        meta,
        after,
        [mine] + others,
        [whole((rows, cols))] * (1 + len(others)),
        [shape_of((rows, cols))],
        [whole((rows, cols))],
        (1,),
        micros=3,
    )
    return outs[0], token


def sum_places(meta, after, every, first):
    places, rows, cols = every.shape

    def body(meta_ref, in_ref, out_ref):
        total = in_ref[0, first:, :]
        for k in range(1, places):
            total = total + in_ref[k, first:, :]
        out_ref[...] = total

    outs, token = launch(
        body,
        "sum_places",
        meta,
        after,
        [every],
        [whole(every.shape)],
        [shape_of((rows - first, cols))],
        [whole((rows - first, cols))],
        (1,),
        micros=2,
    )
    return outs[0], token


def send_groups(mine):
    return [mine, to_x(mine), to_y(mine), send_along(mine, lambda c, s: (c ^ 3, s))]


def gather_groups(meta, after, sent):
    rows, cols = sent[0].shape
    group_place = meta.shape[0] - 1

    def body(meta_ref, *refs):
        out_ref = refs[-1]
        for k in range(4):

            @pl.when(pl.program_id(0) == k)
            def _(k=k):
                out_ref[...] = refs[k][...]

    outs, token = launch(
        body,
        "gather_groups",
        meta,
        after,
        sent,
        [whole((rows, cols))] * 4,
        [shape_of((4 * rows, cols))],
        [pl.BlockSpec((rows, cols), lambda i, m: (m[group_place] ^ i, 0))],
        (4,),
        micros=4,
    )
    return outs[0], token


PIECE = 2


def local_fast(
    block_input,
    valid_len,
    out_grad,
    first_gain,
    first_shift,
    log_step,
    decay_log,
    turn_rate,
    read_real,
    read_imag,
    skip_gain,
    glu_weight,
    glu_bias,
    second_gain,
    second_shift,
    up_weight,
    up_bias,
    down_weight,
    down_bias,
):
    parts = lax.axis_size("seq")
    groups = lax.axis_size("ctx")
    chips = parts // 2
    seq_index = lax.axis_index("seq")
    ctx_index = lax.axis_index("ctx")
    contexts, block_len, channels = block_input.shape
    places = jnp.stack([seq_index, ctx_index]).astype(jnp.int32)
    meta = jnp.concatenate([valid_len, places])

    def row(vector):
        return vector.reshape(1, -1)

    tables = odd_tables()
    bases = list(range(0, contexts, PIECE))
    token = first_gain.reshape(8, BLOCK)

    signal, blocks, token = make_signal(
        meta, token, block_input, row(first_gain), row(first_shift), 0, contexts
    )
    received = swap_blocks(blocks)
    first_channel = seq_index * BLOCK
    own_params = (lax.dynamic_slice_in_dim(log_step, first_channel, BLOCK, 0),) + tuple(
        lax.dynamic_slice_in_dim(tensor.T, first_channel, BLOCK, 1)
        for tensor in (decay_log, turn_rate, read_real, read_imag)
    )
    coefs, coefs_back = jax.vjp(mode_coefs, *own_params)
    taps, token = make_spectrum(meta, token, coefs, tables, parts)
    grad_out, down_bias_part, token = mask_rows(meta, token, out_grad)
    grad_out_got = to_sibling(grad_out)
    convs = []
    spectra = []
    for base in bases:
        blocks, spectrum, token = convolve(
            meta, token, contexts, received, taps, tables, base, PIECE
        )
        convs.append(swap_blocks(blocks))
        spectra.append(spectrum)
    ahead = []
    for base, conv in zip(bases, convs):
        piece, token = make_forward(
            meta,
            token,
            block_input,
            conv,
            signal,
            row(skip_gain),
            glu_weight,
            row(glu_bias),
            row(second_gain),
            row(second_shift),
            up_weight,
            row(up_bias),
            base,
            PIECE,
        )
        ahead.append(piece)
    rows_each = PIECE * BLOCK

    pairs = []
    for k, piece in enumerate(ahead):
        pairs.append((piece[8], grad_out, k, rows_each))
        pairs.append((to_sibling(piece[9]), grad_out_got, k, rows_each))
    act_got = [to_sibling(piece[1]) for piece in ahead]
    second_got = [to_sibling(piece[7]) for piece in ahead]
    token = [token] + act_got + second_got
    down_part, token = weight_grad(meta, token, "down_grad", pairs, groups, chips, chips, 1, 11)
    down_mine = scatter_groups(down_part)

    back, token = make_backward(
        meta,
        token,
        contexts,
        grad_out,
        signal,
        [(piece[10], piece[5], piece[3], piece[4], piece[2]) for piece in ahead],
        row(second_gain),
        down_weight,
        up_weight,
        glu_weight,
        PIECE,
    )
    moved = swap_parts(back["blocks"])
    inner_got = to_sibling(back["inner"])
    gates_got = to_sibling(back["gates"])
    outputs = []

    def output_of(k, token):
        piece = ahead[k]
        output, token = make_output(
            meta,
            token,
            contexts,
            piece[5],
            piece[8],
            piece[9],
            down_weight,
            row(down_bias),
            bases[k],
            PIECE,
        )
        outputs.append(output)
        return token

    token = output_of(0, token)
    pairs = []
    for k, piece in enumerate(ahead):
        pairs.append((piece[6], back["inner"], k, rows_each))
        pairs.append((second_got[k], inner_got, k, rows_each))
    up_part, token = weight_grad(meta, token, "up_grad", pairs, groups, chips, 1, 4, 12)
    up_mine = scatter_groups(up_part)
    pairs = []
    for k, piece in enumerate(ahead):
        pairs.append((piece[0], back["gates"], k, rows_each))
        pairs.append((act_got[k], gates_got, k, rows_each))
    glu_part, token = weight_grad(meta, token, "glu_grad", pairs, groups, chips, 1, 2, 8)
    glu_mine = scatter_groups(glu_part)
    down_rows = down_mine.shape[0] // chips
    narrow_rows = up_mine.shape[0] // chips
    down_part, token = pick_chips(meta, token, down_mine, chips, down_rows)
    blocks, taps_grad, token = convolve_back(meta, token, contexts, moved, spectra, taps, tables)
    conv_grad = swap_parts(blocks)
    down_part, token = add_pairs(meta, token, down_part)
    moments, token = make_moments(
        meta, token, coefs[0], coefs[1], taps_grad.reshape(parts * BLOCK, BLOCK)
    )
    for k in range(1, len(bases)):
        token = output_of(k, token)
    last, token = make_input_grad(
        meta,
        token,
        block_input,
        conv_grad,
        back["mixed"],
        back["hidden"],
        row(skip_gain),
        row(first_gain),
        0,
    )
    up_part, token = pick_chips(meta, token, up_mine, chips, narrow_rows)
    zero_real, zero_imag, one_real, one_imag = (moments[k] for k in range(4))
    coef_real, coef_imag = coefs[2], coefs[3]
    own_grads = coefs_back(
        (
            2.0 * (coef_real * one_real - coef_imag * one_imag),
            -2.0 * (coef_real * one_imag + coef_imag * one_real),
            2.0 * zero_real,
            -2.0 * zero_imag,
        )
    )
    vectors = [last[1], last[2]] + [back["sums"][k] for k in (4, 1, 2, 3, 0)]
    vectors.append(down_bias_part)
    own_rows = [own_grads[0][None, :]] + list(own_grads[1:])
    mode_rows = sum(rows.shape[0] for rows in own_rows)
    gap = -mode_rows % 8
    own_rows.append(jnp.zeros((gap, BLOCK), F32))
    mode_rows += gap
    small = jnp.concatenate(own_rows + [v.reshape(-1, BLOCK) for v in vectors], axis=0)
    small, token = add_chips(meta, token, small, [to_x(small)])
    up_part, token = add_pairs(meta, token, up_part)
    small, token = add_chips(meta, token, small, [to_y(small)])
    every = swap_parts(jnp.broadcast_to(small[None], (parts,) + small.shape))
    glu_part, token = pick_chips(meta, token, glu_mine, chips, narrow_rows)
    down_sum, token = add_chips(meta, token, down_part[0], [down_part[1]])
    down_sent = send_groups(down_sum)
    up_sum, token = add_chips(meta, token, up_part[0], [up_part[1]])
    up_sent = send_groups(up_sum)
    glu_part, token = add_pairs(meta, token, glu_part)
    flat, token = sum_places(meta, token, every, mode_rows)
    down_total, token = gather_groups(meta, token, down_sent)
    glu_sum, token = add_chips(meta, token, glu_part[0], [glu_part[1]])
    glu_sent = send_groups(glu_sum)
    up_total, token = gather_groups(meta, token, up_sent)
    glu_total, token = gather_groups(meta, token, glu_sent)

    modes = decay_log.shape[1]
    step_grad = every[:, 0].reshape(-1)
    mode_grads = [
        every[:, 1 + k * modes : 1 + (k + 1) * modes].transpose(0, 2, 1).reshape(-1, modes)
        for k in range(4)
    ]
    sums = []
    start = 0
    for vector in vectors:
        size = vector.size // BLOCK
        sums.append(flat[start : start + size].reshape(-1))
        start += size
    gain_sum, shift_sum, skip_sum, glu_bias_sum, gain2_sum, shift2_sum = sums[:6]
    up_bias_sum, down_bias_sum = sums[6:]
    return (
        jnp.concatenate(outputs, axis=0),
        last[0],
        gain_sum,
        shift_sum,
        step_grad,
        mode_grads[0],
        mode_grads[1],
        mode_grads[2],
        mode_grads[3],
        skip_sum,
        glu_total,
        glu_bias_sum,
        gain2_sum,
        shift2_sum,
        up_total,
        up_bias_sum,
        down_total,
        down_bias_sum,
    )


def local_any(
    block_input,
    valid_len,
    out_grad,
    first_gain,
    first_shift,
    log_step,
    decay_log,
    turn_rate,
    read_real,
    read_imag,
    skip_gain,
    glu_weight,
    glu_bias,
    second_gain,
    second_shift,
    up_weight,
    up_bias,
    down_weight,
    down_bias,
):
    seq_parts = lax.axis_size("seq")
    seq_index = lax.axis_index("seq")
    contexts, block_len, channels = block_input.shape
    total_len = seq_parts * block_len
    row_count = contexts * block_len
    positions = seq_index * block_len + jnp.arange(block_len)
    valid_mask = (positions[None, :] < valid_len[:, None]).astype(jnp.float32)[:, :, None]
    flat_mask = valid_mask.reshape(row_count, 1)
    ssm_params = (log_step, decay_log, turn_rate, read_real, read_imag)
    inputs = block_input.astype(jnp.float32)
    normed_first, unit_first, scale_first = layer_norm(inputs, first_gain, first_shift)
    signal = normed_first * valid_mask
    chan_count = channels // seq_parts
    chan_params = jax.tree.map(
        lambda tensor: lax.dynamic_slice_in_dim(tensor, seq_index * chan_count, chan_count, 0),
        ssm_params,
    )
    all_float = jnp.arange(total_len).astype(jnp.float32)
    kernel_part = kernel_block(chan_params, all_float)
    sig_real, sig_imag = channel_spectrum(signal)
    ker_real, ker_imag = local_spectrum(kernel_part.reshape(1, seq_parts, block_len, chan_count))
    prod_real, prod_imag = times_kernel(sig_real, sig_imag, ker_real, ker_imag)
    conv_out = token_blocks(local_time(prod_real, prod_imag))
    mixed_seq = conv_out + skip_gain * signal
    activated_full, act_back = jax.vjp(gelu_tanh, mixed_seq)
    activated = activated_full.astype(jnp.bfloat16).reshape(row_count, channels)
    gate_rows = jnp.dot(activated, glu_weight, preferred_element_type=jnp.float32) + glu_bias
    gate_a = gate_rows[:, :channels]
    gate_sig = jax.nn.sigmoid(gate_rows[:, channels:])
    hidden = inputs.reshape(row_count, channels) + gate_a * gate_sig
    normed_second, unit_second, scale_second = layer_norm(hidden, second_gain, second_shift)
    second = normed_second.astype(jnp.bfloat16)
    inner_rows = jnp.dot(second, up_weight, preferred_element_type=jnp.float32) + up_bias
    widened_full, wide_back = jax.vjp(gelu_tanh, inner_rows)
    widened = widened_full.astype(jnp.bfloat16)
    result = hidden + jnp.dot(widened, down_weight, preferred_element_type=jnp.float32) + down_bias
    block_output = (result * flat_mask).astype(jnp.bfloat16).reshape(contexts, block_len, channels)
    grad_out = out_grad.reshape(row_count, channels) * flat_mask.astype(jnp.bfloat16)
    grad_out_f = grad_out.astype(jnp.float32)
    down_bias_grad = jnp.sum(grad_out_f, axis=0)
    down_grad = jnp.einsum("rf,rd->fd", widened, grad_out, preferred_element_type=jnp.float32)
    grad_wide = jnp.einsum("rd,fd->rf", grad_out, down_weight, preferred_element_type=jnp.float32)
    grad_inner = wide_back(grad_wide)[0].astype(jnp.bfloat16)
    up_bias_grad = jnp.sum(grad_inner.astype(jnp.float32), axis=0)
    up_grad = jnp.einsum("rd,rf->df", second, grad_inner, preferred_element_type=jnp.float32)
    grad_second = jnp.einsum("rf,df->rd", grad_inner, up_weight, preferred_element_type=jnp.float32)
    second_gain_grad = jnp.sum(grad_second * unit_second, axis=0)
    second_shift_grad = jnp.sum(grad_second, axis=0)
    grad_hidden = grad_out_f + norm_back(grad_second, unit_second, scale_second, second_gain)
    grad_first_half = grad_hidden * gate_sig
    grad_second_half = grad_hidden * gate_a * gate_sig * (1.0 - gate_sig)
    grad_gates = jnp.concatenate([grad_first_half, grad_second_half], axis=1).astype(jnp.bfloat16)
    glu_bias_grad = jnp.sum(grad_gates.astype(jnp.float32), axis=0)
    glu_grad = jnp.einsum("rd,re->de", activated, grad_gates, preferred_element_type=jnp.float32)
    grad_act = jnp.einsum("re,de->rd", grad_gates, glu_weight, preferred_element_type=jnp.float32)
    grad_mixed = act_back(grad_act.reshape(contexts, block_len, channels))[0]
    skip_gain_grad = jnp.sum(grad_mixed * signal, axis=(0, 1))
    grad_real, grad_imag = channel_spectrum(grad_mixed)
    back_real, back_imag = conj_products(
        sig_real, sig_imag, ker_real, ker_imag, grad_real, grad_imag
    )
    returned = local_time(back_real, back_imag)
    grad_conv = token_blocks(returned[:contexts])
    local_grads = kernel_grads(
        chan_params, all_float, returned[contexts].reshape(total_len, chan_count)
    )
    ssm_grads = jax.tree.map(
        lambda whole_grad, piece_grad: lax.dynamic_update_slice_in_dim(
            jnp.zeros_like(whole_grad), piece_grad, seq_index * chan_count, 0
        ),
        ssm_params,
        local_grads,
    )
    grad_signal = grad_conv + skip_gain * grad_mixed
    grad_normed = grad_signal * valid_mask
    first_gain_grad = jnp.sum(grad_normed * unit_first, axis=(0, 1))
    first_shift_grad = jnp.sum(grad_normed, axis=(0, 1))
    input_grad = (
        grad_hidden.reshape(contexts, block_len, channels)
        + norm_back(grad_normed, unit_first, scale_first, first_gain)
    ).astype(jnp.bfloat16)
    step_grad, decay_grad, turn_grad, real_grad, imag_grad = ssm_grads
    (
        first_gain_sum,
        first_shift_sum,
        step_sum,
        decay_sum,
        turn_sum,
        real_sum,
        imag_sum,
        skip_sum,
        glu_bias_sum,
        second_gain_sum,
        second_shift_sum,
        up_bias_sum,
        down_bias_sum,
    ) = lax.psum(
        (
            first_gain_grad,
            first_shift_grad,
            step_grad,
            decay_grad,
            turn_grad,
            real_grad,
            imag_grad,
            skip_gain_grad,
            glu_bias_grad,
            second_gain_grad,
            second_shift_grad,
            up_bias_grad,
            down_bias_grad,
        ),
        ("ctx", "seq"),
    )
    rows_glu, rows_up, rows_down = (
        lax.psum_scatter(glu_grad, "seq", scatter_dimension=0, tiled=True),
        lax.psum_scatter(up_grad, "seq", scatter_dimension=0, tiled=True),
        lax.psum_scatter(down_grad, "seq", scatter_dimension=0, tiled=True),
    )
    glu_total, up_total, down_total = lax.psum((rows_glu, rows_up, rows_down), "ctx")
    return (
        block_output,
        input_grad,
        first_gain_sum,
        first_shift_sum,
        step_sum,
        decay_sum,
        turn_sum,
        real_sum,
        imag_sum,
        skip_sum,
        glu_total,
        glu_bias_sum,
        second_gain_sum,
        second_shift_sum,
        up_total,
        up_bias_sum,
        down_total,
        down_bias_sum,
    )


def solution(mesh):
    in_specs = (
        P("ctx", "seq", None),
        P("ctx"),
        P("ctx", "seq", None),
        P(),
        P(),
        P(),
        P(),
        P(),
        P(),
        P(),
        P(),
        P(),
        P(),
        P(),
        P(),
        P(),
        P(),
        P(),
        P(),
    )
    out_specs = (
        P("ctx", "seq", None),
        P("ctx", "seq", None),
        P(),
        P(),
        P(),
        P(),
        P(),
        P(),
        P(),
        P(),
        P("seq", None),
        P(),
        P(),
        P(),
        P("seq", None),
        P(),
        P("seq", None),
        P(),
    )
    grid_size = (mesh.shape["ctx"], mesh.shape["seq"])
    step = local_fast if grid_size == (4, 8) else local_any
    return jax.shard_map(step, mesh=mesh, in_specs=in_specs, out_specs=out_specs, check_vma=False)
```
